256 devices in a mesh: dp: 32 (over x, y, core), tensor: 8 (over z).
Axes of the slice: x: 4, y: 4, z: 8, core: 2. Of those that a mesh axis runs over, the one named last changes fastest.
Arguments:
- inputs: bfloat16 [1024, 6144], P('dp'), may hold values from -6 to 6
- norm_gain: float32 [6144], replicated, may hold values from 0.1 to 1.9
- out_grad: bfloat16 [1024, 21504], P('dp', 'tensor'), may hold values from -0.59765625 to 0.59765625
- weight: bfloat16 [6144, 21504], P('dp', 'tensor'), may hold values from -0.078125 to 0.078125
- moment: float32 [6144, 21504], P('dp', 'tensor'), may hold values from -3 to 3
- right_basis: float32 [21504, 512], P(('tensor', 'dp')), may hold values from -0.0390625 to 0.0390625
Outputs:
- input_grad: bfloat16 [1024, 6144], P('dp', 'tensor')
- gain_grad: float32 [6144], P('tensor')
- moment_new: float32 [6144, 21504], P('dp', 'tensor')
- basis_new: float32 [21504, 512], P(('tensor', 'dp'))
- update: float32 [6144, 21504], P('dp', 'tensor')
The draws below stay inside these ranges and needn't reach their ends.
All inputs are finite; a program needn't handle non-finite values.
Results may differ from the reference program's by a relative error of at most 0.0031.
Values may be sent and summed in bfloat16 or wider, within the bound.
A program may use at most 128 MiB of HBM per device.

```python
import math
import jax
import jax.numpy as jnp
from jax import lax

D = 6144
HEADS = 24
HEAD_DIM = 128
FF = 12288
RANK = 512
TOKENS = 1024
F = 21504
N_TENSOR = 8


def steps_of(rng, shape, pieces, smallest, high):
    def one(axis_at, parts):
        draws = jax.random.uniform(jax.random.fold_in(jax.random.fold_in(rng, 6), axis_at), (parts,), jnp.float32, smallest / len(pieces), high / len(pieces))
        return jnp.repeat(jnp.exp(draws), shape[axis_at] // parts).reshape((-1,) + (1,) * (len(shape) - axis_at - 1))

    loudness = one(*pieces[0])
    for cut in pieces[1:]:
        loudness = loudness * one(*cut)
    return loudness


def normal_values(own_key, extent, width, reach, pieces=(), kind=jnp.bfloat16):
    array = jax.random.normal(own_key, extent, jnp.float32) * width
    if len(pieces) > 0:
        array = steps_of(own_key, extent, pieces, -0.22, 0.18) * array
    return jnp.clip(array, min=-reach, max=reach).astype(kind)


def setup_inputs(seed: int = 0) -> dict:
    seeds = jax.random.split(jax.random.key(seed), 7)
    inputs = normal_values(seeds[0], (TOKENS, D), 1.0, 6.0, ((0, 32),))
    norm_gain = jnp.clip(1.0 + 0.18 * jax.random.normal(seeds[1], (D,), jnp.float32), 0.1, 1.9)
    out_grad = normal_values(seeds[2], (TOKENS, F), 0.1, 0.59765625, ((0, 32), (1, 8)))
    weight = normal_values(seeds[3], (D, F), D ** -0.5, 0.078125, ((0, 32), (1, 8)))
    moment = normal_values(seeds[4], (D, F), 0.5, 3.0, ((0, 32), (1, 8)), jnp.float32)
    right_basis = normal_values(seeds[5], (F, RANK), F ** -0.5, 0.0390625, ((0, 256),), jnp.float32)
    return {"inputs": inputs, "norm_gain": norm_gain, "out_grad": out_grad, "weight": weight, "moment": moment, "right_basis": right_basis}


PRECISE = lax.Precision.HIGHEST
MOMENTUM = 0.8
NORM_EPSILON = 1e-06

def column_scale():
    qkv_cols = 3 * HEADS * HEAD_DIM
    group_cols = (qkv_cols + FF) // N_TENSOR
    position = jnp.arange(N_TENSOR * group_cols, dtype=jnp.int32) % group_cols
    qkv_scale = 0.2 * math.sqrt(D * qkv_cols / RANK)
    mlp_scale = 0.2 * math.sqrt(D * FF / RANK)
    return jnp.where(position < qkv_cols // N_TENSOR, qkv_scale, mlp_scale).astype(jnp.float32)

def reference(inputs, norm_gain, out_grad, weight, moment, right_basis):
    widened = inputs.astype(jnp.float32)
    row_mean = lax.optimization_barrier(jnp.mean(widened, axis=1, keepdims=True))
    centered = widened - row_mean
    row_var = lax.optimization_barrier(jnp.mean(centered * centered, axis=1, keepdims=True))
    inv_std = lax.rsqrt(row_var + NORM_EPSILON)
    standard = centered * inv_std
    normed = (standard * norm_gain).astype(jnp.bfloat16)
    weight_grad = jnp.dot(normed.T.astype(jnp.float32), out_grad.astype(jnp.float32), preferred_element_type=jnp.float32)
    normed_grad = jnp.dot(out_grad.astype(jnp.float32), weight.T.astype(jnp.float32), preferred_element_type=jnp.float32)
    scaled_grad = normed_grad * norm_gain
    mean_grad = lax.optimization_barrier(jnp.mean(scaled_grad, axis=1, keepdims=True))
    mean_proj = lax.optimization_barrier(jnp.mean(scaled_grad * standard, axis=1, keepdims=True))
    input_grad = (inv_std * (scaled_grad - mean_grad - standard * mean_proj)).astype(jnp.bfloat16)
    gain_grad = lax.optimization_barrier(jnp.sum(normed_grad * standard, axis=0))
    buffer = moment + weight_grad
    projected = jnp.dot(buffer, right_basis, precision=PRECISE)
    gram = jnp.dot(projected.T, projected, precision=PRECISE)
    factor = jnp.linalg.cholesky(gram)
    orthonormal = lax.linalg.triangular_solve(factor, projected, left_side=False, lower=True, transpose_a=True)
    coeffs = jnp.dot(buffer.T, orthonormal, precision=PRECISE)
    moment_new = buffer - (1.0 - MOMENTUM) * jnp.dot(orthonormal, coeffs.T, precision=PRECISE)
    col_norms = jnp.sqrt(lax.optimization_barrier(jnp.sum(coeffs * coeffs, axis=0)))
    basis_new = coeffs / (col_norms + 1e-08)
    update = jnp.dot(orthonormal, basis_new.T, precision=PRECISE) * column_scale()[None, :]
    return (input_grad, gain_grad, moment_new, basis_new, update)
```

```python
import math

import jax
import jax.numpy as jnp
from jax import lax
from jax.experimental import pallas as pl
from jax.experimental.pallas import tpu as pltpu
from jax.sharding import PartitionSpec as P

D = 6144
HEADS = 24
HEAD_DIM = 128
FF = 12288
RANK = 512
MOMENTUM = 0.8
NORM_EPSILON = 1e-06

HI = lax.Precision.HIGHEST
MESH = pl.DeviceIdType.MESH
VMEM_LIMIT = 56 * 1024 * 1024
F32 = jnp.float32
BF16 = jnp.bfloat16


def dp_of(x, y, core):
    return (x * 4 + y) * 2 + core


def place():
    dp = lax.axis_index("dp")
    return dp // 8, (dp // 2) % 4, dp % 2, lax.axis_index("tensor")


def send(src, dst, send_sem, recv_sem, **peer):
    copy = pltpu.make_async_remote_copy(
        src_ref=src, dst_ref=dst, send_sem=send_sem, recv_sem=recv_sem,
        device_id=peer, device_id_type=MESH,
    )
    copy.start()
    return copy


def wait_recv(dst, recv_sem, **peer):
    pltpu.make_async_remote_copy(
        src_ref=dst, dst_ref=dst, send_sem=recv_sem, recv_sem=recv_sem,
        device_id=peer, device_id_type=MESH,
    ).wait_recv()


def greet(peers):
    barrier = pltpu.get_barrier_semaphore()
    for peer in peers:
        pl.semaphore_signal(barrier, inc=1, device_id=peer, device_id_type=MESH)
    pl.semaphore_wait(barrier, len(peers))


def plane_neighbours(x, y, core):
    return [
        {"dp": dp_of((x + 1) % 4, y, core)},
        {"dp": dp_of((x + 3) % 4, y, core)},
        {"dp": dp_of(x, (y + 1) % 4, core)},
        {"dp": dp_of(x, (y + 3) % 4, core)},
        {"dp": dp_of(x, y, 1 - core)},
    ]


def round_robin(generators):
    live = list(generators)
    while live:
        still = []
        for g in live:
            try:
                next(g)
                still.append(g)
            except StopIteration:
                pass
        live = still


def gather_stream(loc, first, ssem, rsem, base, sent):
    x0, y0, core, _ = place()
    a0, b0 = (x0, y0) if first == "x" else (y0, x0)
    sib = dp_of(x0, y0, 1 - core)

    def xy(a, b):
        return (a % 4, b % 4) if first == "x" else (b % 4, a % 4)

    def at(a, b, part, who=None):
        return loc(core if who is None else who, *xy(a, b), part)

    def to(a, b, block, part, slot):
        ref = at(*block, part)
        sent.append(send(ref, ref, ssem.at[base + slot], rsem.at[base + slot], dp=dp_of(*xy(a, b), core)))

    def got(block, part, slot):
        wait_recv(at(*block, part), rsem.at[base + slot], dp=sib)

    def share(block, slot):
        ref = at(*block, 2)
        sent.append(send(ref, ref, ssem.at[base + slot], rsem.at[base + slot], dp=sib))

    def spread(k, block):
        to(a0, b0 + 1, block, 2, 4 + 4 * k)
        to(a0, b0 - 1, block, 2, 5 + 4 * k)

    offs = (0, -1, 1, 2)
    to(a0 + 1, b0, (a0, b0), 2, 0)
    to(a0 - 1, b0, (a0, b0), 2, 1)
    yield
    spread(0, (a0, b0))
    share((a0, b0), 20)
    yield
    got((a0 - 1, b0), 2, 0)
    to(a0 + 1, b0, (a0 - 1, b0), 0, 2)
    spread(1, (a0 - 1, b0))
    yield
    got((a0 + 1, b0), 2, 1)
    to(a0 - 1, b0, (a0 + 1, b0), 1, 3)
    spread(2, (a0 + 1, b0))
    yield
    share((a0 - 1, b0), 21)
    share((a0 + 1, b0), 22)
    got((a0 + 2, b0), 0, 2)
    got((a0 + 2, b0), 1, 3)
    spread(3, (a0 + 2, b0))
    share((a0 + 2, b0), 23)
    yield
    for k in range(4):
        a = a0 + offs[k]
        got((a, b0 - 1), 2, 4 + 4 * k)
        to(a0, b0 + 1, (a, b0 - 1), 0, 6 + 4 * k)
        got((a, b0 + 1), 2, 5 + 4 * k)
        to(a0, b0 - 1, (a, b0 + 1), 1, 7 + 4 * k)
        share((a, b0 - 1), 24 + 3 * k)
        share((a, b0 + 1), 25 + 3 * k)
        yield
    for k in range(4):
        a = a0 + offs[k]
        got((a, b0 + 2), 0, 6 + 4 * k)
        got((a, b0 + 2), 1, 7 + 4 * k)
        share((a, b0 + 2), 26 + 3 * k)
        yield
    for k in range(4):
        a = a0 + offs[k]
        wait_recv(at(a, b0, 2, 1 - core), rsem.at[base + 20 + k], dp=sib)
        for j, b in enumerate((b0 - 1, b0 + 1, b0 + 2)):
            wait_recv(at(a, b, 2, 1 - core), rsem.at[base + 24 + 3 * k + j], dp=sib)
        yield


GATHER_SLOTS = 36


def gather_kernel(r_ref, g_ref, rall_ref, gall_ref, got_ref, ssem, rsem, hsem):
    x, y, core, _ = place()
    chip = x * 4 + y
    greet(plane_neighbours(x, y, core))
    rows = r_ref.shape[0]
    tokens = g_ref.shape[0]
    cols = g_ref.shape[1]
    cut = 1408
    other = pl.multiple_of(256 * (1 - core), 128)
    swap = send(r_ref.at[:, pl.ds(other, 256)], got_ref, hsem.at[0], hsem.at[1], dp=dp_of(x, y, 1 - core))
    own_g = pltpu.make_async_copy(
        g_ref, gall_ref.at[pl.ds(pl.multiple_of(tokens * (2 * chip + core), 32), tokens)], hsem.at[2]
    )
    own_g.start()

    def loc_r(s):
        def loc(who, bx, by, part):
            lo, n = ((0, 88), (88, 80), (0, 168))[part]
            row = pl.multiple_of((bx * 4 + by) * 168 + lo, 8)
            col = pl.multiple_of(256 * who + 128 * s, 128)
            return rall_ref.at[pl.ds(row, n), pl.ds(col, 128)]
        return loc

    def loc_g(s):
        def loc(who, bx, by, part):
            lo, n = ((0, cut), (cut, cols - cut), (0, cols))[part]
            row = pl.multiple_of(tokens * (2 * (bx * 4 + by) + who) + 16 * s, 16)
            return gall_ref.at[pl.ds(row, 16), pl.ds(lo, n)]
        return loc

    sent = []
    own_g.wait()
    g_streams = [
        gather_stream(loc_g(0), "x", ssem, rsem, 2 * GATHER_SLOTS, sent),
        gather_stream(loc_g(1), "y", ssem, rsem, 3 * GATHER_SLOTS, sent),
    ]
    swap.wait()
    mine = r_ref[:, pl.ds(pl.multiple_of(256 * core, 128), 256)]
    theirs = got_ref[...]
    first = jnp.where(core == 0, mine, theirs)
    second = jnp.where(core == 0, theirs, mine)
    row = pl.multiple_of(chip * 168, 8)
    col = pl.multiple_of(256 * core, 128)
    rall_ref[pl.ds(row, 168), pl.ds(col, 256)] = jnp.concatenate([first, second], axis=0)
    r_streams = [
        gather_stream(loc_r(0), "x", ssem, rsem, 0, sent),
        gather_stream(loc_r(1), "y", ssem, rsem, GATHER_SLOTS, sent),
    ]
    round_robin(r_streams + g_streams)
    for copy in sent:
        copy.wait_send()


def gather_both(right_basis, out_grad):
    vm = pl.BlockSpec(memory_space=pltpu.VMEM)
    return pl.pallas_call(
        gather_kernel,
        out_shape=(
            jax.ShapeDtypeStruct((32 * right_basis.shape[0], RANK), F32),
            jax.ShapeDtypeStruct((32 * out_grad.shape[0], out_grad.shape[1]), BF16),
        ),
        in_specs=[vm, vm],
        out_specs=(vm, vm),
        scratch_shapes=[
            pltpu.VMEM((right_basis.shape[0], 256), F32),
            pltpu.SemaphoreType.DMA((4 * GATHER_SLOTS,)),
            pltpu.SemaphoreType.DMA((4 * GATHER_SLOTS,)),
            pltpu.SemaphoreType.DMA((3,)),
        ],
        compiler_params=pltpu.CompilerParams(
            collective_id=1, has_side_effects=True, vmem_limit_bytes=VMEM_LIMIT
        ),
    )(right_basis, out_grad)


def gram_kernel(part_ref, p_ref, g_ref, zbuf, gbuf, cbuf, xbuf, ybuf, ssem, rsem):
    x, y, core, z = place()
    xs = [(x + d) % 4 for d in (1, 2, 3)]
    ys = [(y + d) % 4 for d in (1, 2, 3)]
    zs = [(z + d) % 8 for d in range(1, 8)]
    dp = lax.axis_index("dp")
    sib = dp_of(x, y, 1 - core)
    greet(
        [{"tensor": q} for q in zs]
        + [{"dp": dp_of(q, y, core)} for q in xs]
        + [{"dp": dp_of(x, q, core)} for q in ys]
        + [{"dp": sib}]
    )
    sent = []
    order = (3, 4, 2, 5, 1, 6, 0)

    def rows24(q):
        return pl.ds(pl.multiple_of(24 * q, 8), 24)

    for i in order:
        sent.append(send(part_ref.at[rows24(zs[i])], zbuf.at[i], ssem.at[i], rsem.at[i], tensor=zs[i]))
    total = part_ref[rows24(z), :]
    for i in reversed(order):
        wait_recv(zbuf.at[i], rsem.at[i], tensor=zs[i])
        total = total + zbuf[i]
    p_ref[rows24(z), :] = total
    mine = p_ref.at[rows24(z)]
    for i in order:
        sent.append(send(mine, mine, ssem.at[7 + i], rsem.at[7 + i], tensor=zs[i]))
    for i in reversed(order):
        src = (z + 7 - i) % 8
        wait_recv(p_ref.at[rows24(src)], rsem.at[7 + i], tensor=zs[i])

    gbuf[...] = lax.dot_general(
        p_ref[:, pl.ds(pl.multiple_of(128 * (z // 2), 128), 128)], p_ref[...],
        (((0,), (0,)), ((), ())), precision=HI, preferred_element_type=F32,
    )
    half = 64 * (z % 2)
    sent.append(send(gbuf.at[pl.ds(pl.multiple_of(half + 32 * (1 - core), 32), 32)], cbuf, ssem.at[14], rsem.at[14], dp=sib))
    wait_recv(cbuf, rsem.at[14], dp=sib)
    cbuf[...] += gbuf[pl.ds(pl.multiple_of(half + 32 * core, 32), 32), :]
    for i in range(3):
        sent.append(send(
            cbuf.at[pl.ds(pl.multiple_of(8 * xs[i], 8), 8)], xbuf.at[i], ssem.at[15 + i], rsem.at[15 + i],
            dp=dp_of(xs[i], y, core),
        ))
    total = cbuf[pl.ds(pl.multiple_of(8 * x, 8), 8), :]
    for i in range(3):
        wait_recv(xbuf.at[i], rsem.at[15 + i], dp=sib)
        total = total + xbuf[i]
    ybuf[y] = total
    for i in range(3):
        sent.append(send(ybuf.at[y], ybuf.at[y], ssem.at[18 + i], rsem.at[18 + i], dp=dp_of(x, ys[i], core)))
    for i in range(3):
        wait_recv(ybuf.at[(y + 3 - i) % 4], rsem.at[18 + i], dp=sib)
    g_ref[z, core, x] = (ybuf[0] + ybuf[1]) + (ybuf[2] + ybuf[3])
    mine = g_ref.at[z, core, x]
    for i in order:
        sent.append(send(mine, mine, ssem.at[21 + i], rsem.at[21 + i], tensor=zs[i]))
    for i in reversed(order):
        wait_recv(g_ref.at[(z + 7 - i) % 8, core, x], rsem.at[21 + i], tensor=zs[i])
    mine = g_ref.at[:, core, x]
    for i in range(3):
        sent.append(send(mine, mine, ssem.at[28 + i], rsem.at[28 + i], dp=dp_of(xs[i], y, core)))
    sent.append(send(mine, mine, ssem.at[31], rsem.at[31], dp=sib))
    for i in range(3):
        src = (x + 3 - i) % 4
        wait_recv(g_ref.at[:, core, src], rsem.at[28 + i], dp=sib)
        got = g_ref.at[:, core, src]
        sent.append(send(got, got, ssem.at[32 + i], rsem.at[32 + i], dp=sib))
    wait_recv(g_ref.at[:, 1 - core, x], rsem.at[31], dp=sib)
    for i in range(3):
        wait_recv(g_ref.at[:, 1 - core, (x + 3 - i) % 4], rsem.at[32 + i], dp=sib)
    for copy in sent:
        copy.wait_send()


def projected_gram(part):
    vm = pl.BlockSpec(memory_space=pltpu.VMEM)
    p, g = pl.pallas_call(
        gram_kernel,
        out_shape=(
            jax.ShapeDtypeStruct(part.shape, F32),
            jax.ShapeDtypeStruct((8, 2, 4, 8, RANK), F32),
        ),
        in_specs=[vm],
        out_specs=(vm, vm),
        scratch_shapes=[
            pltpu.VMEM((7, 24, RANK), F32),
            pltpu.VMEM((128, RANK), F32),
            pltpu.VMEM((32, RANK), F32),
            pltpu.VMEM((3, 8, RANK), F32),
            pltpu.VMEM((4, 8, RANK), F32),
            pltpu.SemaphoreType.DMA((35,)),
            pltpu.SemaphoreType.DMA((35,)),
        ],
        compiler_params=pltpu.CompilerParams(
            collective_id=2, has_side_effects=True, vmem_limit_bytes=VMEM_LIMIT
        ),
    )(part)
    return p, g.reshape(RANK, RANK)


def chol_kernel(g_ref, p_ref, ot_ref, s_ref, w_ref):
    n_p = p_ref.shape[1]
    s_ref[:, 0:512] = g_ref[...]
    s_ref[:, 512:512 + n_p] = p_ref[...]
    s_ref[:, 512 + n_p:] = jnp.zeros((512, s_ref.shape[1] - 512 - n_p), F32)
    lane = lax.broadcasted_iota(jnp.int32, (8, 128), 1)
    sub = lax.broadcasted_iota(jnp.int32, (8, 128), 0)

    def lane_splat(v, j):
        return jnp.broadcast_to(v[:, j:j + 1], (8, 128))

    def row_splat(v, i):
        return jnp.broadcast_to(v[i:i + 1, :], (8, 128))

    def block(kb, carry):
        base = pl.multiple_of(kb * 128, 128)
        tiles = [s_ref[pl.ds(pl.multiple_of(base + 8 * i, 8), 8), pl.ds(base, 128)] for i in range(16)]
        for k in range(16):
            x = tiles[k]
            inside = (lane >= 8 * k) & (lane < 8 * k + 8)
            c = [lane_splat(x, 8 * k + q) for q in range(8)]
            x = jnp.where(inside, (lane - 8 * k == sub).astype(F32), x)
            inv, up, rows = [], [], []
            scale = jnp.ones((8, 128), F32)
            for p in range(8):
                pd = row_splat(c[p], p)
                ip = 1.0 / pd
                scale = jnp.where(sub == p, lax.rsqrt(pd), scale)
                m = jnp.where(sub > p, c[p] * ip, 0.0)
                u = {}
                for q in range(p + 1, 8):
                    u[q] = row_splat(c[q], p)
                    c[q] = c[q] - m * u[q]
                r = row_splat(x, p)
                x = x - m * r
                inv.append(ip)
                up.append(u)
                rows.append(r)
            w_ref[8 * k:8 * k + 8, :] = jnp.where(lane <= sub + 8 * k, x * scale, 0.0)
            for g in range(k + 1, 16):
                v = tiles[g]
                e = [lane_splat(v, 8 * k + q) for q in range(8)]
                v = jnp.where(inside, 0.0, v)
                for p in range(8):
                    m = e[p] * inv[p]
                    for q in range(p + 1, 8):
                        e[q] = e[q] - m * up[p][q]
                    v = v - m * rows[p]
                tiles[g] = v
        rows_k = pl.ds(base, 128)
        s_ref[rows_k, :] = jnp.dot(w_ref[...], s_ref[rows_k, :], precision=HI, preferred_element_type=F32)
        for rb in range(1, 4):
            @pl.when(rb > kb)
            def _():
                ub = s_ref[rows_k, 128 * rb:128 * rb + 128]
                s_ref[128 * rb:128 * rb + 128, 128 * rb:] -= lax.dot_general(
                    ub, s_ref[rows_k, 128 * rb:], (((0,), (0,)), ((), ())), precision=HI,
                    preferred_element_type=F32,
                )
        return carry

    lax.fori_loop(0, 4, block, 0)
    ot_ref[...] = s_ref[:, 512:512 + n_p]


def chol_solve(gram, projected_t):
    n_p = projected_t.shape[1]
    vm = pl.BlockSpec(memory_space=pltpu.VMEM)
    return pl.pallas_call(
        chol_kernel,
        out_shape=jax.ShapeDtypeStruct((RANK, n_p), F32),
        in_specs=[vm, vm],
        out_specs=vm,
        scratch_shapes=[pltpu.VMEM((RANK, 768), F32), pltpu.VMEM((128, 128), F32)],
        compiler_params=pltpu.CompilerParams(vmem_limit_bytes=VMEM_LIMIT),
    )(gram, projected_t)


SPLIT = ((0, 96), (96, 80), (0, 176))


def coeff_kernel(c_ref, call_ref, cown_ref, csq_ref, pair, sbuf, rbuf, acc, s2, r2, fin, fsib, agb,
                 xsq, ysq, zsq, sqs, ssem, rsem, gs, gr):
    x, y, core, z = place()
    sib = dp_of(x, y, 1 - core)
    xs = [(x + d) % 4 for d in (1, 2, 3)]
    ys = [(y + d) % 4 for d in (1, 2, 3)]
    zs = [(z + d) % 8 for d in range(1, 8)]
    greet(
        [{"tensor": q} for q in zs]
        + [{"dp": dp_of(q, y, core)} for q in xs]
        + [{"dp": dp_of(x, q, core)} for q in ys]
        + [{"dp": sib}]
    )
    sent = []
    first = ("x", "y")

    def chunk(ref, s, a, cols=None):
        a = a % 4
        if cols is None:
            return ref.at[s, a] if s == 0 else ref.at[s, :, a]
        return ref.at[a, :, :, cols] if s == 0 else ref.at[:, a, :, cols]

    def cols_of(who, s):
        return pl.ds(pl.multiple_of(256 * who + 128 * s, 128), 128)

    a0 = (x, y)
    b0 = (y, x)
    n = 0
    pieces = {}
    for off in (2, 1, 3, 0):
        for s in (0, 1):
            sent.append(send(
                chunk(c_ref, s, a0[s] + off, cols_of(1 - core, s)), chunk(pair, s, a0[s] + off),
                ssem.at[n], rsem.at[n], dp=sib,
            ))
            pieces[off, s] = n
            n += 1

    def own(s, off, b):
        a = (a0[s] + off) % 4
        bx, by = (a, b) if s == 0 else (b, a)
        return c_ref[bx, by, :, cols_of(core, s)] + pair[s, bx, by]

    def pair_ready(s, off):
        wait_recv(chunk(pair, s, a0[s] + off), rsem.at[pieces[off, s]], dp=sib)

    def dev(s, a, b):
        a, b = a % 4, b % 4
        return dp_of(a, b, core) if s == 0 else dp_of(b, a, core)

    zero_pad = jnp.zeros((8, 128), F32)

    def padded(v):
        return jnp.concatenate([v, zero_pad], axis=0).astype(BF16)

    def reduce_stream(s):
        base = 8 + 8 * s
        a, b = a0[s], b0[s]
        right, left = dev(s, a + 1, b), dev(s, a - 1, b)
        pair_ready(s, 2)
        for j in range(4):
            sbuf[s, 0, j] = padded(own(s, 2, j))
        sent.append(send(sbuf.at[s, 0, 0:2], rbuf.at[s, 0, 0:2], ssem.at[base], rsem.at[base], dp=right))
        sent.append(send(sbuf.at[s, 0, 2:4], rbuf.at[s, 0, 2:4], ssem.at[base + 1], rsem.at[base + 1], dp=left))
        yield
        pair_ready(s, 1)
        pair_ready(s, 3)
        for j in (2, 3):
            sbuf[s, 1, j] = padded(own(s, 1, j))
        for j in (0, 1):
            sbuf[s, 2, j] = padded(own(s, 3, j))
        yield
        wait_recv(rbuf.at[s, 0, 0:2], rsem.at[base], dp=left)
        for j in (0, 1):
            sbuf[s, 1, j] = padded(own(s, 1, j) + rbuf[s, 0, j, 0:168].astype(F32))
        sent.append(send(sbuf.at[s, 1], rbuf.at[s, 1], ssem.at[base + 2], rsem.at[base + 2], dp=right))
        yield
        wait_recv(rbuf.at[s, 0, 2:4], rsem.at[base + 1], dp=right)
        for j in (2, 3):
            sbuf[s, 2, j] = padded(own(s, 3, j) + rbuf[s, 0, j, 0:168].astype(F32))
        sent.append(send(sbuf.at[s, 2], rbuf.at[s, 2], ssem.at[base + 3], rsem.at[base + 3], dp=left))
        yield
        pair_ready(s, 0)
        for j in range(4):
            acc[s, j] = own(s, 0, j)
        yield
        wait_recv(rbuf.at[s, 1], rsem.at[base + 2], dp=left)
        wait_recv(rbuf.at[s, 2], rsem.at[base + 3], dp=right)

        def summed(off):
            j = (b + off) % 4
            return acc[s, j] + (rbuf[s, 1, j, 0:168].astype(F32) + rbuf[s, 2, j, 0:168].astype(F32))

        right, left = dev(s, a, b + 1), dev(s, a, b - 1)
        s2[s, 0] = padded(summed(2))
        sent.append(send(s2.at[s, 0, 0:96], r2.at[s, 0, 0:96], ssem.at[base + 4], rsem.at[base + 4], dp=right))
        sent.append(send(s2.at[s, 0, 96:176], r2.at[s, 0, 96:176], ssem.at[base + 5], rsem.at[base + 5], dp=left))
        yield
        one, three, zero = summed(1), summed(3), summed(0)
        wait_recv(r2.at[s, 0, 0:96], rsem.at[base + 4], dp=left)
        s2[s, 1, 0:96] = (one[0:96] + r2[s, 0, 0:96].astype(F32)).astype(BF16)
        s2[s, 1, 96:176] = padded(one[96:168])
        sent.append(send(s2.at[s, 1], r2.at[s, 1], ssem.at[base + 6], rsem.at[base + 6], dp=right))
        wait_recv(r2.at[s, 0, 96:176], rsem.at[base + 5], dp=right)
        s2[s, 2, 0:96] = three[0:96].astype(BF16)
        s2[s, 2, 96:176] = padded(three[96:168] + r2[s, 0, 96:168].astype(F32))
        sent.append(send(s2.at[s, 2], r2.at[s, 2], ssem.at[base + 7], rsem.at[base + 7], dp=left))
        yield
        wait_recv(r2.at[s, 1], rsem.at[base + 6], dp=left)
        wait_recv(r2.at[s, 2], rsem.at[base + 7], dp=right)
        total = zero + (r2[s, 1, 0:168].astype(F32) + r2[s, 2, 0:168].astype(F32))
        fin[:, 128 * s:128 * s + 128] = total
        agb[x * 4 + y, :, cols_of(core, s)] = padded(total)
        yield

    round_robin([reduce_stream(0), reduce_stream(1)])

    def norms():
        sent.append(send(fin, fsib, ssem.at[24], rsem.at[24], dp=sib))
        v = fin[...]
        xsq[x] = jnp.broadcast_to(jnp.sum(v * v, axis=0, keepdims=True), (8, 256))
        for i in range(3):
            sent.append(send(xsq.at[x], xsq.at[x], ssem.at[25 + i], rsem.at[25 + i], dp=dp_of(xs[i], y, core)))
        yield
        for i in range(3):
            wait_recv(xsq.at[(x + 3 - i) % 4], rsem.at[25 + i], dp=sib)
        ysq[y] = (xsq[0] + xsq[1]) + (xsq[2] + xsq[3])
        for i in range(3):
            sent.append(send(ysq.at[y], ysq.at[y], ssem.at[28 + i], rsem.at[28 + i], dp=dp_of(x, ys[i], core)))
        yield
        for i in range(3):
            wait_recv(ysq.at[(y + 3 - i) % 4], rsem.at[28 + i], dp=sib)
        zsq[z] = (ysq[0] + ysq[1]) + (ysq[2] + ysq[3])
        for i in range(7):
            sent.append(send(zsq.at[z], zsq.at[z], ssem.at[31 + i], rsem.at[31 + i], tensor=zs[i]))
        yield
        for i in range(7):
            wait_recv(zsq.at[(z + 7 - i) % 8], rsem.at[31 + i], tensor=zs[i])
        total = zsq[0]
        for i in range(1, 8):
            total = total + zsq[i]
        sqs[core] = total
        sent.append(send(sqs.at[core], sqs.at[core], ssem.at[38], rsem.at[38], dp=sib))
        yield
        wait_recv(fsib, rsem.at[24], dp=sib)
        left = jnp.where(core == 0, fin[0:84], fsib[84:168])
        right = jnp.where(core == 0, fsib[0:84], fin[84:168])
        cown_ref[:, 0:256] = left
        cown_ref[:, 256:512] = right
        yield
        wait_recv(sqs.at[1 - core], rsem.at[38], dp=sib)
        csq_ref[:, 0:256] = sqs[0]
        csq_ref[:, 256:512] = sqs[1]
        yield

    def loc(s):
        def at(who, bx, by, part):
            lo, rows = SPLIT[part]
            return agb.at[bx * 4 + by, pl.ds(lo, rows), cols_of(who, s)]
        return at

    round_robin([
        gather_stream(loc(0), first[0], gs, gr, 0, sent),
        gather_stream(loc(1), first[1], gs, gr, GATHER_SLOTS, sent),
        norms(),
    ])
    for j in range(8):
        two = jnp.concatenate([agb[2 * j, 0:168].astype(F32), agb[2 * j + 1, 0:168].astype(F32)], axis=0)
        call_ref[336 * j:336 * j + 336, :] = two.astype(BF16)
    for copy in sent:
        copy.wait_send()


def coeff_sum(part):
    vm = pl.BlockSpec(memory_space=pltpu.VMEM)
    return pl.pallas_call(
        coeff_kernel,
        out_shape=(
            jax.ShapeDtypeStruct((2688, RANK), BF16),
            jax.ShapeDtypeStruct((84, RANK), F32),
            jax.ShapeDtypeStruct((8, RANK), F32),
        ),
        in_specs=[vm],
        out_specs=(vm, vm, vm),
        scratch_shapes=[
            pltpu.VMEM((2, 4, 4, 168, 128), F32),
            pltpu.VMEM((2, 3, 4, 176, 128), BF16),
            pltpu.VMEM((2, 3, 4, 176, 128), BF16),
            pltpu.VMEM((2, 4, 168, 128), F32),
            pltpu.VMEM((2, 3, 176, 128), BF16),
            pltpu.VMEM((2, 3, 176, 128), BF16),
            pltpu.VMEM((168, 256), F32),
            pltpu.VMEM((168, 256), F32),
            pltpu.VMEM((16, 176, RANK), BF16),
            pltpu.VMEM((4, 8, 256), F32),
            pltpu.VMEM((4, 8, 256), F32),
            pltpu.VMEM((8, 8, 256), F32),
            pltpu.VMEM((2, 8, 256), F32),
            pltpu.SemaphoreType.DMA((39,)),
            pltpu.SemaphoreType.DMA((39,)),
            pltpu.SemaphoreType.DMA((2 * GATHER_SLOTS,)),
            pltpu.SemaphoreType.DMA((2 * GATHER_SLOTS,)),
        ],
        compiler_params=pltpu.CompilerParams(
            collective_id=3, has_side_effects=True, vmem_limit_bytes=VMEM_LIMIT
        ),
    )(part.reshape(4, 4, 168, RANK))


def final_kernel(o_ref, inv_ref, c_ref, buf_ref, scale_ref, mom_ref, upd_ref, lhs):
    rows = o_ref.shape[0]

    @pl.when(pl.program_id(0) == 0)
    def _():
        o = o_ref[...]
        oi = o * inv_ref[...]
        for j, v in enumerate((o, oi)):
            top = v.astype(BF16)
            lhs[2 * j * rows:(2 * j + 1) * rows, :] = top
            lhs[(2 * j + 1) * rows:(2 * j + 2) * rows, :] = (v - top.astype(F32)).astype(BF16)

    out = lax.dot_general(lhs[...], c_ref[...], (((1,), (1,)), ((), ())), preferred_element_type=F32)
    mom_ref[...] = buf_ref[...] - (1.0 - MOMENTUM) * (out[0:rows] + out[rows:2 * rows])
    upd_ref[...] = (out[2 * rows:3 * rows] + out[3 * rows:4 * rows]) * scale_ref[...]


def final_products(o, inv, coeffs, buffer, scale):
    rows, cols = buffer.shape
    tile = 384
    return pl.pallas_call(
        final_kernel,
        grid=(cols // tile,),
        out_shape=(jax.ShapeDtypeStruct(buffer.shape, F32), jax.ShapeDtypeStruct(buffer.shape, F32)),
        in_specs=[
            pl.BlockSpec((rows, RANK), lambda i: (0, 0)),
            pl.BlockSpec((1, RANK), lambda i: (0, 0)),
            pl.BlockSpec((tile, RANK), lambda i: (i, 0)),
            pl.BlockSpec((rows, tile), lambda i: (0, i)),
            pl.BlockSpec((1, tile), lambda i: (0, i)),
        ],
        out_specs=(pl.BlockSpec((rows, tile), lambda i: (0, i)), pl.BlockSpec((rows, tile), lambda i: (0, i))),
        scratch_shapes=[pltpu.VMEM((4 * rows, RANK), BF16)],
        compiler_params=pltpu.CompilerParams(vmem_limit_bytes=VMEM_LIMIT),
    )(o, inv, coeffs, buffer, scale)


def per_device(inputs, norm_gain, out_grad, weight, moment, right_basis):
    tensor_count = lax.axis_size("tensor")
    tensor_index = lax.axis_index("tensor")
    width = inputs.shape[1]
    group_cols = weight.shape[1]
    widened = inputs.astype(F32)
    row_mean = jnp.mean(widened, axis=1, keepdims=True)
    centered = widened - row_mean
    row_var = jnp.mean(centered * centered, axis=1, keepdims=True)
    inv_std = lax.rsqrt(row_var + NORM_EPSILON)
    standard = centered * inv_std
    normed = (standard * norm_gain).astype(BF16)
    feature_block = lax.all_to_all(normed, "dp", split_axis=1, concat_axis=0, tiled=True)
    basis_all, shard_in = gather_both(right_basis, out_grad)
    grad_acc = lax.dot_general(feature_block, shard_in, (((0,), (0,)), ((), ())), preferred_element_type=F32)
    buffer = moment + grad_acc
    part = jnp.dot(buffer, basis_all, precision=HI, preferred_element_type=F32)
    projected, gram = projected_gram(part)
    ortho_t = chol_solve(gram, projected.T)
    coeff_part = lax.dot_general(
        buffer, ortho_t, (((0,), (1,)), ((), ())), precision=lax.Precision.HIGH, preferred_element_type=F32
    )
    coeffs, coeff_own, squares = coeff_sum(coeff_part)
    col_inverse = 1.0 / (jnp.sqrt(squares[0:1]) + 1e-08)
    basis_new = coeff_own * col_inverse
    qkv_group = 3 * HEADS * HEAD_DIM // tensor_count
    qkv_scale = 0.2 * math.sqrt(D * (3 * HEADS * HEAD_DIM) / RANK)
    mlp_scale = 0.2 * math.sqrt(D * FF / RANK)
    position = jnp.arange(group_cols, dtype=jnp.int32)
    col_scale = jnp.where(position < qkv_group, qkv_scale, mlp_scale).astype(F32)
    moment_new, update = final_products(ortho_t.T, col_inverse, coeffs, buffer, col_scale[None, :])

    share_cols = width // tensor_count
    offset = tensor_index * share_cols
    back_rows = lax.dot_general(shard_in, weight, (((1,), (1,)), ((), ())), preferred_element_type=F32)
    back_mine = lax.all_to_all(back_rows, "dp", split_axis=0, concat_axis=1, tiled=True)
    normed_grad = lax.psum_scatter(back_mine, "tensor", scatter_dimension=1, tiled=True)
    standard_here = lax.dynamic_slice_in_dim(standard, offset, share_cols, 1)
    gain_here = lax.dynamic_slice_in_dim(norm_gain, offset, share_cols, 0)
    scaled_grad = normed_grad * gain_here
    sums = jnp.stack([jnp.sum(scaled_grad, axis=1), jnp.sum(scaled_grad * standard_here, axis=1)])
    sums = lax.psum(sums, "tensor") * (1.0 / width)
    full_grad = inv_std * (scaled_grad - sums[0][:, None] - standard_here * sums[1][:, None])
    input_grad = full_grad.astype(BF16)
    gain_grad = lax.psum(jnp.sum(normed_grad * standard_here, axis=0), "dp")
    return (input_grad, gain_grad, moment_new, basis_new, update)


def solution(mesh):
    in_specs = (
        P("dp", None),
        P(),
        P("dp", "tensor"),
        P("dp", "tensor"),
        P("dp", "tensor"),
        P(("tensor", "dp"), None),
    )
    out_specs = (
        P("dp", "tensor"),
        P("tensor"),
        P("dp", "tensor"),
        P(("tensor", "dp"), None),
        P("dp", "tensor"),
    )
    return jax.shard_map(
        per_device, mesh=mesh, in_specs=in_specs, out_specs=out_specs, check_vma=False
    )
```

```python
import math

import jax
import jax.numpy as jnp
from jax import lax
from jax.experimental import pallas as pl
from jax.experimental.pallas import tpu as pltpu
from jax.sharding import PartitionSpec as P

D = 6144
HEADS = 24
HEAD_DIM = 128
FF = 12288
RANK = 512
MOMENTUM = 0.8
NORM_EPSILON = 1e-06

HI = lax.Precision.HIGHEST
MESH = pl.DeviceIdType.MESH
VMEM_LIMIT = 56 * 1024 * 1024
F32 = jnp.float32
BF16 = jnp.bfloat16


def dp_of(x, y, core):
    return (x * 4 + y) * 2 + core


def place():
    dp = lax.axis_index("dp")
    return dp // 8, (dp // 2) % 4, dp % 2, lax.axis_index("tensor")


def send(src, dst, send_sem, recv_sem, **peer):
    copy = pltpu.make_async_remote_copy(
        src_ref=src, dst_ref=dst, send_sem=send_sem, recv_sem=recv_sem,
        device_id=peer, device_id_type=MESH,
    )
    copy.start()
    return copy


def wait_recv(dst, recv_sem, **peer):
    pltpu.make_async_remote_copy(
        src_ref=dst, dst_ref=dst, send_sem=recv_sem, recv_sem=recv_sem,
        device_id=peer, device_id_type=MESH,
    ).wait_recv()


def greet(peers):
    barrier = pltpu.get_barrier_semaphore()
    for peer in peers:
        pl.semaphore_signal(barrier, inc=1, device_id=peer, device_id_type=MESH)
    pl.semaphore_wait(barrier, len(peers))


def plane_peers(x, y, core):
    return (
        [{"dp": dp_of((x + d) % 4, y, core)} for d in (1, 2, 3)]
        + [{"dp": dp_of(x, (y + d) % 4, core)} for d in (1, 2, 3)]
        + [{"dp": dp_of(x, y, 1 - core)}]
    )


def round_robin(generators):
    live = list(generators)
    while live:
        still = []
        for g in live:
            try:
                next(g)
                still.append(g)
            except StopIteration:
                pass
        live = still


def gather_stream(loc, first, ssem, rsem, base, sent):
    x0, y0, core, _ = place()
    a0, b0 = (x0, y0) if first == "x" else (y0, x0)
    sib = dp_of(x0, y0, 1 - core)

    def xy(a, b):
        return (a % 4, b % 4) if first == "x" else (b % 4, a % 4)

    def at(a, b, part, who=None):
        return loc(core if who is None else who, *xy(a, b), part)

    def to(a, b, block, part, slot):
        ref = at(*block, part)
        sent.append(send(ref, ref, ssem.at[base + slot], rsem.at[base + slot], dp=dp_of(*xy(a, b), core)))

    def got(block, part, slot):
        wait_recv(at(*block, part), rsem.at[base + slot], dp=sib)

    def share(block, slot):
        ref = at(*block, 2)
        sent.append(send(ref, ref, ssem.at[base + slot], rsem.at[base + slot], dp=sib))

    def spread(k, block):
        to(a0, b0 + 1, block, 2, 4 + 4 * k)
        to(a0, b0 - 1, block, 2, 5 + 4 * k)

    offs = (0, -1, 1, 2)
    to(a0 + 1, b0, (a0, b0), 2, 0)
    to(a0 - 1, b0, (a0, b0), 2, 1)
    yield
    spread(0, (a0, b0))
    share((a0, b0), 20)
    yield
    got((a0 - 1, b0), 2, 0)
    to(a0 + 1, b0, (a0 - 1, b0), 0, 2)
    spread(1, (a0 - 1, b0))
    yield
    got((a0 + 1, b0), 2, 1)
    to(a0 - 1, b0, (a0 + 1, b0), 1, 3)
    spread(2, (a0 + 1, b0))
    yield
    share((a0 - 1, b0), 21)
    share((a0 + 1, b0), 22)
    got((a0 + 2, b0), 0, 2)
    got((a0 + 2, b0), 1, 3)
    spread(3, (a0 + 2, b0))
    share((a0 + 2, b0), 23)
    yield
    for k in range(4):
        a = a0 + offs[k]
        got((a, b0 - 1), 2, 4 + 4 * k)
        to(a0, b0 + 1, (a, b0 - 1), 0, 6 + 4 * k)
        got((a, b0 + 1), 2, 5 + 4 * k)
        to(a0, b0 - 1, (a, b0 + 1), 1, 7 + 4 * k)
        share((a, b0 - 1), 24 + 3 * k)
        share((a, b0 + 1), 25 + 3 * k)
        yield
    for k in range(4):
        a = a0 + offs[k]
        got((a, b0 + 2), 0, 6 + 4 * k)
        got((a, b0 + 2), 1, 7 + 4 * k)
        share((a, b0 + 2), 26 + 3 * k)
        yield
    for k in range(4):
        a = a0 + offs[k]
        wait_recv(at(a, b0, 2, 1 - core), rsem.at[base + 20 + k], dp=sib)
        for j, b in enumerate((b0 - 1, b0 + 1, b0 + 2)):
            wait_recv(at(a, b, 2, 1 - core), rsem.at[base + 24 + 3 * k + j], dp=sib)
        yield


GATHER_SLOTS = 36
EXCHANGE_SLOTS = 7


def exchange_stream(src, xbuf, ybuf, out, ssem, rsem, base, sent):
    x, y, core, _ = place()
    sib = dp_of(x, y, 1 - core)
    for i in range(3):
        to = (x + 1 + i) % 4
        sent.append(send(src.at[to], xbuf.at[x], ssem.at[base + i], rsem.at[base + i], dp=dp_of(to, y, core)))
    xbuf[x] = src[x]
    yield
    for i in range(3):
        wait_recv(xbuf.at[(x + 3 - i) % 4], rsem.at[base + i], dp=sib)
    for i in range(3):
        to = (y + 1 + i) % 4
        sent.append(send(
            xbuf.at[:, to], ybuf.at[:, y], ssem.at[base + 3 + i], rsem.at[base + 3 + i], dp=dp_of(x, to, core)
        ))
    ybuf[:, y] = xbuf[:, y]
    yield
    for i in range(3):
        wait_recv(ybuf.at[:, (y + 3 - i) % 4], rsem.at[base + 3 + i], dp=sib)
    sent.append(send(ybuf.at[:, :, 1 - core], out.at[:, :, core], ssem.at[base + 6], rsem.at[base + 6], dp=sib))
    out[:, :, core] = ybuf[:, :, core]
    yield
    wait_recv(out.at[:, :, 1 - core], rsem.at[base + 6], dp=sib)
    yield


def gather_kernel(r_ref, g_ref, n_ref, rall_ref, gall_ref, nall_ref, got_ref, xbuf, ybuf, ssem, rsem, hsem):
    x, y, core, _ = place()
    chip = x * 4 + y
    greet(plane_peers(x, y, core))
    rows = r_ref.shape[0]
    tokens = g_ref.shape[0]
    cols = g_ref.shape[1]
    cut = 1408
    other = pl.multiple_of(256 * (1 - core), 128)
    swap = send(r_ref.at[:, pl.ds(other, 256)], got_ref, hsem.at[0], hsem.at[1], dp=dp_of(x, y, 1 - core))
    own_g = pltpu.make_async_copy(
        g_ref, gall_ref.at[pl.ds(pl.multiple_of(tokens * (2 * chip + core), 32), tokens)], hsem.at[2]
    )
    own_g.start()

    def loc_r(s):
        def loc(who, bx, by, part):
            lo, n = ((0, 88), (88, 80), (0, 168))[part]
            row = pl.multiple_of((bx * 4 + by) * 168 + lo, 8)
            col = pl.multiple_of(256 * who + 128 * s, 128)
            return rall_ref.at[pl.ds(row, n), pl.ds(col, 128)]
        return loc

    def loc_g(s):
        def loc(who, bx, by, part):
            lo, n = ((0, cut), (cut, cols - cut), (0, cols))[part]
            row = pl.multiple_of(tokens * (2 * (bx * 4 + by) + who) + 16 * s, 16)
            return gall_ref.at[pl.ds(row, 16), pl.ds(lo, n)]
        return loc

    sent = []
    own_g.wait()
    g_streams = [
        gather_stream(loc_g(0), "x", ssem, rsem, 2 * GATHER_SLOTS, sent),
        gather_stream(loc_g(1), "y", ssem, rsem, 3 * GATHER_SLOTS, sent),
    ]
    swap.wait()
    mine = r_ref[:, pl.ds(pl.multiple_of(256 * core, 128), 256)]
    theirs = got_ref[...]
    first = jnp.where(core == 0, mine, theirs)
    second = jnp.where(core == 0, theirs, mine)
    row = pl.multiple_of(chip * 168, 8)
    col = pl.multiple_of(256 * core, 128)
    rall_ref[pl.ds(row, 168), pl.ds(col, 256)] = jnp.concatenate([first, second], axis=0)
    r_streams = [
        gather_stream(loc_r(0), "x", ssem, rsem, 0, sent),
        gather_stream(loc_r(1), "y", ssem, rsem, GATHER_SLOTS, sent),
    ]
    round_robin(
        r_streams + g_streams + [exchange_stream(n_ref, xbuf, ybuf, nall_ref, ssem, rsem, 4 * GATHER_SLOTS, sent)]
    )
    for copy in sent:
        copy.wait_send()


def gather_both(right_basis, out_grad, normed):
    vm = pl.BlockSpec(memory_space=pltpu.VMEM)
    return pl.pallas_call(
        gather_kernel,
        out_shape=(
            jax.ShapeDtypeStruct((32 * right_basis.shape[0], RANK), F32),
            jax.ShapeDtypeStruct((32 * out_grad.shape[0], out_grad.shape[1]), BF16),
            jax.ShapeDtypeStruct(normed.shape, BF16),
        ),
        in_specs=[vm, vm, vm],
        out_specs=(vm, vm, vm),
        scratch_shapes=[
            pltpu.VMEM((right_basis.shape[0], 256), F32),
            pltpu.VMEM(normed.shape, BF16),
            pltpu.VMEM(normed.shape, BF16),
            pltpu.SemaphoreType.DMA((4 * GATHER_SLOTS + EXCHANGE_SLOTS,)),
            pltpu.SemaphoreType.DMA((4 * GATHER_SLOTS + EXCHANGE_SLOTS,)),
            pltpu.SemaphoreType.DMA((3,)),
        ],
        compiler_params=pltpu.CompilerParams(
            collective_id=1, has_side_effects=True, vmem_limit_bytes=VMEM_LIMIT
        ),
    )(right_basis, out_grad, normed)


def split(v):
    top = v.astype(BF16)
    return top, (v - top.astype(F32)).astype(BF16)


def gram_kernel(b_ref, r_ref, back_ref, p_ref, g_ref, bt_ref, btsib_ref, backall_ref,
                both, part_ref, zbuf, gbuf, cbuf, xbuf, ybuf, ex, ey, ssem, rsem):
    x, y, core, z = place()
    xs = [(x + d) % 4 for d in (1, 2, 3)]
    ys = [(y + d) % 4 for d in (1, 2, 3)]
    zs = [(z + d) % 8 for d in range(1, 8)]
    dp = lax.axis_index("dp")
    sib = dp_of(x, y, 1 - core)
    greet(
        [{"tensor": q} for q in zs]
        + [{"dp": dp_of(q, y, core)} for q in xs]
        + [{"dp": dp_of(x, q, core)} for q in ys]
        + [{"dp": sib}]
    )
    sent = []
    order = (3, 4, 2, 5, 1, 6, 0)
    back = exchange_stream(back_ref, ex, ey, backall_ref, ssem, rsem, 36, sent)
    next(back)
    rows, cols = b_ref.shape
    top, low = split(b_ref[...])
    both[0:rows, :] = top
    both[rows:2 * rows, :] = low
    part_ref[...] = jnp.zeros_like(part_ref)
    for t in range(0, cols, 384):
        r_top, r_low = split(r_ref[t:t + 384, :])
        one = jnp.dot(both[:, t:t + 384], r_top, preferred_element_type=F32)
        two = jnp.dot(both[0:rows, t:t + 384], r_low, preferred_element_type=F32)
        part_ref[...] += one[0:rows] + (one[rows:] + two)

    def rows24(q):
        return pl.ds(pl.multiple_of(24 * q, 8), 24)

    for i in order:
        sent.append(send(part_ref.at[rows24(zs[i])], zbuf.at[i], ssem.at[i], rsem.at[i], tensor=zs[i]))
    for t in range(0, cols, 384):
        bt_ref[t:t + 384, :] = both[:, t:t + 384].astype(F32).T.astype(BF16)
    sent.append(send(bt_ref, btsib_ref, ssem.at[35], rsem.at[35], dp=sib))
    next(back)
    total = part_ref[rows24(z), :]
    for i in reversed(order):
        wait_recv(zbuf.at[i], rsem.at[i], tensor=zs[i])
        total = total + zbuf[i]
    p_ref[rows24(z), :] = total
    mine = p_ref.at[rows24(z)]
    for i in order:
        sent.append(send(mine, mine, ssem.at[7 + i], rsem.at[7 + i], tensor=zs[i]))
    for i in reversed(order):
        src = (z + 7 - i) % 8
        wait_recv(p_ref.at[rows24(src)], rsem.at[7 + i], tensor=zs[i])
    next(back)

    gbuf[...] = lax.dot_general(
        p_ref[:, pl.ds(pl.multiple_of(128 * (z // 2), 128), 128)], p_ref[...],
        (((0,), (0,)), ((), ())), precision=HI, preferred_element_type=F32,
    )
    half = 64 * (z % 2)
    sent.append(send(gbuf.at[pl.ds(pl.multiple_of(half + 32 * (1 - core), 32), 32)], cbuf, ssem.at[14], rsem.at[14], dp=sib))
    wait_recv(cbuf, rsem.at[14], dp=sib)
    cbuf[...] += gbuf[pl.ds(pl.multiple_of(half + 32 * core, 32), 32), :]
    for i in range(3):
        sent.append(send(
            cbuf.at[pl.ds(pl.multiple_of(8 * xs[i], 8), 8)], xbuf.at[i], ssem.at[15 + i], rsem.at[15 + i],
            dp=dp_of(xs[i], y, core),
        ))
    total = cbuf[pl.ds(pl.multiple_of(8 * x, 8), 8), :]
    for i in range(3):
        wait_recv(xbuf.at[i], rsem.at[15 + i], dp=sib)
        total = total + xbuf[i]
    ybuf[y] = total
    for i in range(3):
        sent.append(send(ybuf.at[y], ybuf.at[y], ssem.at[18 + i], rsem.at[18 + i], dp=dp_of(x, ys[i], core)))
    for i in range(3):
        wait_recv(ybuf.at[(y + 3 - i) % 4], rsem.at[18 + i], dp=sib)
    g_ref[z, core, x] = (ybuf[0] + ybuf[1]) + (ybuf[2] + ybuf[3])
    mine = g_ref.at[z, core, x]
    for i in order:
        sent.append(send(mine, mine, ssem.at[21 + i], rsem.at[21 + i], tensor=zs[i]))
    for i in reversed(order):
        wait_recv(g_ref.at[(z + 7 - i) % 8, core, x], rsem.at[21 + i], tensor=zs[i])
    mine = g_ref.at[:, core, x]
    for i in range(3):
        sent.append(send(mine, mine, ssem.at[28 + i], rsem.at[28 + i], dp=dp_of(xs[i], y, core)))
    sent.append(send(mine, mine, ssem.at[31], rsem.at[31], dp=sib))
    for i in range(3):
        src = (x + 3 - i) % 4
        wait_recv(g_ref.at[:, core, src], rsem.at[28 + i], dp=sib)
        got = g_ref.at[:, core, src]
        sent.append(send(got, got, ssem.at[32 + i], rsem.at[32 + i], dp=sib))
    wait_recv(g_ref.at[:, 1 - core, x], rsem.at[31], dp=sib)
    for i in range(3):
        wait_recv(g_ref.at[:, 1 - core, (x + 3 - i) % 4], rsem.at[32 + i], dp=sib)
    next(back)
    wait_recv(btsib_ref, rsem.at[35], dp=sib)
    for copy in sent:
        copy.wait_send()


def projected_gram(buffer, basis, back):
    vm = pl.BlockSpec(memory_space=pltpu.VMEM)
    rows, cols = buffer.shape
    p, g, bt, bt_sib, back_all = pl.pallas_call(
        gram_kernel,
        out_shape=(
            jax.ShapeDtypeStruct((rows, RANK), F32),
            jax.ShapeDtypeStruct((8, 2, 4, 8, RANK), F32),
            jax.ShapeDtypeStruct((cols, 2 * rows), BF16),
            jax.ShapeDtypeStruct((cols, 2 * rows), BF16),
            jax.ShapeDtypeStruct(back.shape, F32),
        ),
        in_specs=[vm, vm, vm],
        out_specs=(vm, vm, vm, vm, vm),
        scratch_shapes=[
            pltpu.VMEM((2 * rows, cols), BF16),
            pltpu.VMEM((rows, RANK), F32),
            pltpu.VMEM((7, 24, RANK), F32),
            pltpu.VMEM((128, RANK), F32),
            pltpu.VMEM((32, RANK), F32),
            pltpu.VMEM((3, 8, RANK), F32),
            pltpu.VMEM((4, 8, RANK), F32),
            pltpu.VMEM(back.shape, F32),
            pltpu.VMEM(back.shape, F32),
            pltpu.SemaphoreType.DMA((36 + EXCHANGE_SLOTS,)),
            pltpu.SemaphoreType.DMA((36 + EXCHANGE_SLOTS,)),
        ],
        compiler_params=pltpu.CompilerParams(
            collective_id=2, has_side_effects=True, vmem_limit_bytes=VMEM_LIMIT
        ),
    )(buffer, basis, back)
    return p, g.reshape(RANK, RANK), bt, bt_sib, back_all


def chol_kernel(g_ref, p_ref, o_ref, s_ref, w_ref):
    n_p = p_ref.shape[0]
    s_ref[:, 0:512] = g_ref[...]
    s_ref[:, 512:512 + n_p] = p_ref[...].T
    s_ref[:, 512 + n_p:] = jnp.zeros((512, s_ref.shape[1] - 512 - n_p), F32)
    lane = lax.broadcasted_iota(jnp.int32, (8, 128), 1)
    sub = lax.broadcasted_iota(jnp.int32, (8, 128), 0)

    def lane_splat(v, j):
        return jnp.broadcast_to(v[:, j:j + 1], (8, 128))

    def row_splat(v, i):
        return jnp.broadcast_to(v[i:i + 1, :], (8, 128))

    def block(kb, carry):
        base = pl.multiple_of(kb * 128, 128)
        tiles = [s_ref[pl.ds(pl.multiple_of(base + 8 * i, 8), 8), pl.ds(base, 128)] for i in range(16)]
        for k in range(16):
            x = tiles[k]
            inside = (lane >= 8 * k) & (lane < 8 * k + 8)
            c = [lane_splat(x, 8 * k + q) for q in range(8)]
            x = jnp.where(inside, (lane - 8 * k == sub).astype(F32), x)
            inv, up, rows = [], [], []
            scale = jnp.ones((8, 128), F32)
            for p in range(8):
                pd = row_splat(c[p], p)
                ip = 1.0 / pd
                scale = jnp.where(sub == p, lax.rsqrt(pd), scale)
                m = jnp.where(sub > p, c[p] * ip, 0.0)
                u = {}
                for q in range(p + 1, 8):
                    u[q] = row_splat(c[q], p)
                    c[q] = c[q] - m * u[q]
                r = row_splat(x, p)
                x = x - m * r
                inv.append(ip)
                up.append(u)
                rows.append(r)
            w_ref[8 * k:8 * k + 8, :] = jnp.where(lane <= sub + 8 * k, x * scale, 0.0)
            for g in range(k + 1, 16):
                v = tiles[g]
                e = [lane_splat(v, 8 * k + q) for q in range(8)]
                v = jnp.where(inside, 0.0, v)
                for p in range(8):
                    m = e[p] * inv[p]
                    for q in range(p + 1, 8):
                        e[q] = e[q] - m * up[p][q]
                    v = v - m * rows[p]
                tiles[g] = v
        rows_k = pl.ds(base, 128)
        s_ref[rows_k, :] = jnp.dot(w_ref[...], s_ref[rows_k, :], precision=HI, preferred_element_type=F32)
        for rb in range(1, 4):
            @pl.when(rb > kb)
            def _():
                ub = s_ref[rows_k, 128 * rb:128 * rb + 128]
                s_ref[128 * rb:128 * rb + 128, 128 * rb:] -= lax.dot_general(
                    ub, s_ref[rows_k, 128 * rb:], (((0,), (0,)), ((), ())), precision=HI,
                    preferred_element_type=F32,
                )
        return carry

    lax.fori_loop(0, 4, block, 0)
    o_ref[...] = s_ref[:, 512:512 + n_p].T


def chol_solve(gram, projected):
    vm = pl.BlockSpec(memory_space=pltpu.VMEM)
    return pl.pallas_call(
        chol_kernel,
        out_shape=jax.ShapeDtypeStruct(projected.shape, F32),
        in_specs=[vm, vm],
        out_specs=vm,
        scratch_shapes=[pltpu.VMEM((RANK, 768), F32), pltpu.VMEM((128, 128), F32)],
        compiler_params=pltpu.CompilerParams(vmem_limit_bytes=VMEM_LIMIT),
    )(gram, projected)


SPLIT = ((0, 96), (96, 80), (0, 176))


def coeff_kernel(bt_ref, btsib_ref, o_ref, back_ref, std_ref, gain_ref, inv_ref,
                 call_ref, cown_ref, csq_ref, ig_ref, gg_ref,
                 osib, rhs, c_ref, sbuf, rbuf, acc, s2, r2, fin, fsib, agb,
                 xsq, ysq, zsq, sqs, ngbuf, stat, gx, gy, gc, ssem, rsem, gs, gr, ns, nr):
    x, y, core, z = place()
    sib = dp_of(x, y, 1 - core)
    xs = [(x + d) % 4 for d in (1, 2, 3)]
    ys = [(y + d) % 4 for d in (1, 2, 3)]
    zs = [(z + d) % 8 for d in range(1, 8)]
    greet(
        [{"tensor": q} for q in zs]
        + [{"dp": dp_of(q, y, core)} for q in xs]
        + [{"dp": dp_of(x, q, core)} for q in ys]
        + [{"dp": sib}]
    )
    sent = []
    first = ("x", "y")

    def half(who):
        return pl.ds(pl.multiple_of(256 * who, 128), 256)

    sent.append(send(o_ref.at[:, half(1 - core)], osib, ssem.at[0], rsem.at[0], dp=sib))
    for i in range(7):
        sent.append(send(back_ref.at[zs[i]], ngbuf.at[i], ns.at[i], nr.at[i], tensor=zs[i]))

    def fill(v):
        top, low = split(v)
        n = v.shape[0]
        rhs[0:n, 0:256] = top
        rhs[n:2 * n, 0:256] = top
        rhs[0:n, 256:512] = low
        rhs[n:2 * n, 256:512] = low

    cols = bt_ref.shape[0]
    fill(o_ref[:, half(core)])
    for t in range(0, cols, 384):
        two = jnp.dot(bt_ref[t:t + 384, :], rhs[...], preferred_element_type=F32)
        c_ref[t:t + 384, :] = two[:, 0:256] + two[:, 256:512]
    wait_recv(osib, rsem.at[0], dp=sib)
    fill(osib[...])
    for t in range(0, cols, 384):
        two = jnp.dot(btsib_ref[t:t + 384, :], rhs[...], preferred_element_type=F32)
        c_ref[t:t + 384, :] += two[:, 0:256] + two[:, 256:512]

    def cols_of(who, s):
        return pl.ds(pl.multiple_of(256 * who + 128 * s, 128), 128)

    a0 = (x, y)
    b0 = (y, x)

    def own(s, off, b):
        a = (a0[s] + off) % 4
        bx, by = (a, b) if s == 0 else (b, a)
        return c_ref[pl.ds(pl.multiple_of(168 * (bx * 4 + by), 8), 168), 128 * s:128 * s + 128]

    def dev(s, a, b):
        a, b = a % 4, b % 4
        return dp_of(a, b, core) if s == 0 else dp_of(b, a, core)

    zero_pad = jnp.zeros((8, 128), F32)

    def padded(v):
        return jnp.concatenate([v, zero_pad], axis=0).astype(BF16)

    def reduce_stream(s):
        base = 8 + 8 * s
        a, b = a0[s], b0[s]
        right, left = dev(s, a + 1, b), dev(s, a - 1, b)
        for j in range(4):
            sbuf[s, 0, j] = padded(own(s, 2, j))
        sent.append(send(sbuf.at[s, 0, 0:2], rbuf.at[s, 0, 0:2], ssem.at[base], rsem.at[base], dp=right))
        sent.append(send(sbuf.at[s, 0, 2:4], rbuf.at[s, 0, 2:4], ssem.at[base + 1], rsem.at[base + 1], dp=left))
        yield
        for j in (2, 3):
            sbuf[s, 1, j] = padded(own(s, 1, j))
        for j in (0, 1):
            sbuf[s, 2, j] = padded(own(s, 3, j))
        yield
        wait_recv(rbuf.at[s, 0, 0:2], rsem.at[base], dp=left)
        for j in (0, 1):
            sbuf[s, 1, j] = padded(own(s, 1, j) + rbuf[s, 0, j, 0:168].astype(F32))
        sent.append(send(sbuf.at[s, 1], rbuf.at[s, 1], ssem.at[base + 2], rsem.at[base + 2], dp=right))
        yield
        wait_recv(rbuf.at[s, 0, 2:4], rsem.at[base + 1], dp=right)
        for j in (2, 3):
            sbuf[s, 2, j] = padded(own(s, 3, j) + rbuf[s, 0, j, 0:168].astype(F32))
        sent.append(send(sbuf.at[s, 2], rbuf.at[s, 2], ssem.at[base + 3], rsem.at[base + 3], dp=left))
        yield
        for j in range(4):
            acc[s, j] = own(s, 0, j)
        yield
        wait_recv(rbuf.at[s, 1], rsem.at[base + 2], dp=left)
        wait_recv(rbuf.at[s, 2], rsem.at[base + 3], dp=right)

        def summed(off):
            j = (b + off) % 4
            return acc[s, j] + (rbuf[s, 1, j, 0:168].astype(F32) + rbuf[s, 2, j, 0:168].astype(F32))

        right, left = dev(s, a, b + 1), dev(s, a, b - 1)
        s2[s, 0] = padded(summed(2))
        sent.append(send(s2.at[s, 0, 0:96], r2.at[s, 0, 0:96], ssem.at[base + 4], rsem.at[base + 4], dp=right))
        sent.append(send(s2.at[s, 0, 96:176], r2.at[s, 0, 96:176], ssem.at[base + 5], rsem.at[base + 5], dp=left))
        yield
        one, three, zero = summed(1), summed(3), summed(0)
        wait_recv(r2.at[s, 0, 0:96], rsem.at[base + 4], dp=left)
        s2[s, 1, 0:96] = (one[0:96] + r2[s, 0, 0:96].astype(F32)).astype(BF16)
        s2[s, 1, 96:176] = padded(one[96:168])
        sent.append(send(s2.at[s, 1], r2.at[s, 1], ssem.at[base + 6], rsem.at[base + 6], dp=right))
        wait_recv(r2.at[s, 0, 96:176], rsem.at[base + 5], dp=right)
        s2[s, 2, 0:96] = three[0:96].astype(BF16)
        s2[s, 2, 96:176] = padded(three[96:168] + r2[s, 0, 96:168].astype(F32))
        sent.append(send(s2.at[s, 2], r2.at[s, 2], ssem.at[base + 7], rsem.at[base + 7], dp=left))
        yield
        wait_recv(r2.at[s, 1], rsem.at[base + 6], dp=left)
        wait_recv(r2.at[s, 2], rsem.at[base + 7], dp=right)
        total = zero + (r2[s, 1, 0:168].astype(F32) + r2[s, 2, 0:168].astype(F32))
        fin[:, 128 * s:128 * s + 128] = total
        agb[x * 4 + y, :, cols_of(core, s)] = padded(total)
        yield

    round_robin([reduce_stream(0), reduce_stream(1)])

    def norms():
        sent.append(send(fin, fsib, ssem.at[24], rsem.at[24], dp=sib))
        v = fin[...]
        xsq[x] = jnp.broadcast_to(jnp.sum(v * v, axis=0, keepdims=True), (8, 256))
        for i in range(3):
            sent.append(send(xsq.at[x], xsq.at[x], ssem.at[25 + i], rsem.at[25 + i], dp=dp_of(xs[i], y, core)))
        yield
        for i in range(3):
            wait_recv(xsq.at[(x + 3 - i) % 4], rsem.at[25 + i], dp=sib)
        ysq[y] = (xsq[0] + xsq[1]) + (xsq[2] + xsq[3])
        for i in range(3):
            sent.append(send(ysq.at[y], ysq.at[y], ssem.at[28 + i], rsem.at[28 + i], dp=dp_of(x, ys[i], core)))
        yield
        for i in range(3):
            wait_recv(ysq.at[(y + 3 - i) % 4], rsem.at[28 + i], dp=sib)
        zsq[z] = (ysq[0] + ysq[1]) + (ysq[2] + ysq[3])
        for i in range(7):
            sent.append(send(zsq.at[z], zsq.at[z], ssem.at[31 + i], rsem.at[31 + i], tensor=zs[i]))
        yield
        for i in range(7):
            wait_recv(zsq.at[(z + 7 - i) % 8], rsem.at[31 + i], tensor=zs[i])
        total = zsq[0]
        for i in range(1, 8):
            total = total + zsq[i]
        sqs[core] = total
        sent.append(send(sqs.at[core], sqs.at[core], ssem.at[38], rsem.at[38], dp=sib))
        yield
        wait_recv(fsib, rsem.at[24], dp=sib)
        left = jnp.where(core == 0, fin[0:84], fsib[84:168])
        right = jnp.where(core == 0, fsib[0:84], fin[84:168])
        cown_ref[:, 0:256] = left
        cown_ref[:, 256:512] = right
        yield
        wait_recv(sqs.at[1 - core], rsem.at[38], dp=sib)
        csq_ref[:, 0:256] = sqs[0]
        csq_ref[:, 256:512] = sqs[1]
        yield

    def input_grad():
        total = back_ref[z]
        for i in range(7):
            wait_recv(ngbuf.at[i], nr.at[i], tensor=zs[i])
            total = total + ngbuf[i]
        std = std_ref[...]
        scaled = total * gain_ref[...]
        lane = lax.broadcasted_iota(jnp.int32, (32, 128), 1)

        def per_token(v):
            return jnp.sum(jnp.sum(v, axis=0), axis=1, keepdims=True)

        stat[z] = jnp.where(lane < 64, per_token(scaled), per_token(scaled * std))
        for i in range(7):
            sent.append(send(stat.at[z], stat.at[z], ns.at[7 + i], nr.at[7 + i], tensor=zs[i]))
        gx[x] = jnp.broadcast_to(jnp.sum(total * std, axis=1, keepdims=True), gx.shape[1:])
        for i in range(3):
            sent.append(send(gx.at[x], gx.at[x], ns.at[14 + i], nr.at[14 + i], dp=dp_of(xs[i], y, core)))
        yield
        for i in range(3):
            wait_recv(gx.at[(x + 3 - i) % 4], nr.at[14 + i], dp=sib)
        gy[y] = (gx[0] + gx[1]) + (gx[2] + gx[3])
        for i in range(3):
            sent.append(send(gy.at[y], gy.at[y], ns.at[17 + i], nr.at[17 + i], dp=dp_of(x, ys[i], core)))
        for i in range(7):
            wait_recv(stat.at[(z + 7 - i) % 8], nr.at[7 + i], tensor=zs[i])
        sums = stat[0]
        for i in range(1, 8):
            sums = sums + stat[i]
        sums = sums * (1.0 / (32 * 192))
        ig_ref[...] = (inv_ref[...] * (scaled - sums[:, 0:1] - std * sums[:, 64:65])).astype(BF16)
        yield
        for i in range(3):
            wait_recv(gy.at[(y + 3 - i) % 4], nr.at[17 + i], dp=sib)
        gc[core] = (gy[0] + gy[1]) + (gy[2] + gy[3])
        sent.append(send(gc.at[core], gc.at[core], ns.at[20], nr.at[20], dp=sib))
        yield
        wait_recv(gc.at[1 - core], nr.at[20], dp=sib)
        gg_ref[...] = gc[0] + gc[1]
        yield

    def loc(s):
        def at(who, bx, by, part):
            lo, rows = SPLIT[part]
            return agb.at[bx * 4 + by, pl.ds(lo, rows), cols_of(who, s)]
        return at

    round_robin([
        gather_stream(loc(0), first[0], gs, gr, 0, sent),
        gather_stream(loc(1), first[1], gs, gr, GATHER_SLOTS, sent),
        norms(),
        input_grad(),
    ])
    for j in range(8):
        two = jnp.concatenate([agb[2 * j, 0:168].astype(F32), agb[2 * j + 1, 0:168].astype(F32)], axis=0)
        call_ref[336 * j:336 * j + 336, :] = two.astype(BF16)
    for copy in sent:
        copy.wait_send()


def coeff_sum(bt, bt_sib, ortho, back, standard, gain, inv_std):
    vm = pl.BlockSpec(memory_space=pltpu.VMEM)
    block = standard.shape
    return pl.pallas_call(
        coeff_kernel,
        out_shape=(
            jax.ShapeDtypeStruct((2688, RANK), BF16),
            jax.ShapeDtypeStruct((84, RANK), F32),
            jax.ShapeDtypeStruct((8, RANK), F32),
            jax.ShapeDtypeStruct(block, BF16),
            jax.ShapeDtypeStruct((4, 8, 192), F32),
        ),
        in_specs=[vm] * 7,
        out_specs=(vm,) * 5,
        scratch_shapes=[
            pltpu.VMEM((192, 256), F32),
            pltpu.VMEM((384, RANK), BF16),
            pltpu.VMEM((2688, 256), F32),
            pltpu.VMEM((2, 3, 4, 176, 128), BF16),
            pltpu.VMEM((2, 3, 4, 176, 128), BF16),
            pltpu.VMEM((2, 4, 168, 128), F32),
            pltpu.VMEM((2, 3, 176, 128), BF16),
            pltpu.VMEM((2, 3, 176, 128), BF16),
            pltpu.VMEM((168, 256), F32),
            pltpu.VMEM((168, 256), F32),
            pltpu.VMEM((16, 176, RANK), BF16),
            pltpu.VMEM((4, 8, 256), F32),
            pltpu.VMEM((4, 8, 256), F32),
            pltpu.VMEM((8, 8, 256), F32),
            pltpu.VMEM((2, 8, 256), F32),
            pltpu.VMEM((7,) + block, F32),
            pltpu.VMEM((8, 32, 128), F32),
            pltpu.VMEM((4, 4, 8, 192), F32),
            pltpu.VMEM((4, 4, 8, 192), F32),
            pltpu.VMEM((2, 4, 8, 192), F32),
            pltpu.SemaphoreType.DMA((39,)),
            pltpu.SemaphoreType.DMA((39,)),
            pltpu.SemaphoreType.DMA((2 * GATHER_SLOTS,)),
            pltpu.SemaphoreType.DMA((2 * GATHER_SLOTS,)),
            pltpu.SemaphoreType.DMA((21,)),
            pltpu.SemaphoreType.DMA((21,)),
        ],
        compiler_params=pltpu.CompilerParams(
            collective_id=3, has_side_effects=True, vmem_limit_bytes=VMEM_LIMIT
        ),
    )(bt, bt_sib, ortho, back, standard, gain, inv_std)


def final_kernel(o_ref, inv_ref, c_ref, buf_ref, scale_ref, mom_ref, upd_ref, lhs):
    rows = o_ref.shape[0]

    @pl.when(pl.program_id(0) == 0)
    def _():
        o = o_ref[...]
        oi = o * inv_ref[...]
        lhs[0:rows, :] = o.astype(BF16)
        top, low = split(oi)
        lhs[rows:2 * rows, :] = top
        lhs[2 * rows:3 * rows, :] = low

    out = lax.dot_general(lhs[...], c_ref[...], (((1,), (1,)), ((), ())), preferred_element_type=F32)
    mom_ref[...] = buf_ref[...] - (1.0 - MOMENTUM) * out[0:rows]
    upd_ref[...] = (out[rows:2 * rows] + out[2 * rows:3 * rows]) * scale_ref[...]


def final_products(o, inv, coeffs, buffer, scale):
    rows, cols = buffer.shape
    tile = 896
    return pl.pallas_call(
        final_kernel,
        grid=(cols // tile,),
        out_shape=(jax.ShapeDtypeStruct(buffer.shape, F32), jax.ShapeDtypeStruct(buffer.shape, F32)),
        in_specs=[
            pl.BlockSpec((rows, RANK), lambda i: (0, 0)),
            pl.BlockSpec((1, RANK), lambda i: (0, 0)),
            pl.BlockSpec((tile, RANK), lambda i: (i, 0)),
            pl.BlockSpec((rows, tile), lambda i: (0, i)),
            pl.BlockSpec((1, tile), lambda i: (0, i)),
        ],
        out_specs=(pl.BlockSpec((rows, tile), lambda i: (0, i)), pl.BlockSpec((rows, tile), lambda i: (0, i))),
        scratch_shapes=[pltpu.VMEM((3 * rows, RANK), BF16)],
        compiler_params=pltpu.CompilerParams(vmem_limit_bytes=VMEM_LIMIT),
    )(o, inv, coeffs, buffer, scale)


def per_device(inputs, norm_gain, out_grad, weight, moment, right_basis):
    tensor_count = lax.axis_size("tensor")
    tensor_index = lax.axis_index("tensor")
    width = inputs.shape[1]
    group_cols = weight.shape[1]
    widened = inputs.astype(F32)
    row_mean = jnp.mean(widened, axis=1, keepdims=True)
    centered = widened - row_mean
    row_var = jnp.mean(centered * centered, axis=1, keepdims=True)
    inv_std = lax.rsqrt(row_var + NORM_EPSILON)
    standard = centered * inv_std
    normed = (standard * norm_gain).astype(BF16)
    tokens, features = inputs.shape[0], weight.shape[0]
    to_owners = normed.reshape(tokens, 4, 4, 2, features).transpose(1, 2, 3, 0, 4)
    basis_all, shard_in, feature_block = gather_both(right_basis, out_grad, to_owners)
    grad_acc = lax.dot_general(
        feature_block.reshape(32 * tokens, features), shard_in, (((0,), (0,)), ((), ())), preferred_element_type=F32
    )
    buffer = moment + grad_acc
    back_rows = lax.dot_general(shard_in, weight, (((1,), (1,)), ((), ())), preferred_element_type=F32)
    projected, gram, bt, bt_sib, back_all = projected_gram(
        buffer, basis_all, back_rows.reshape(4, 4, 2, tokens, features)
    )
    ortho = chol_solve(gram, projected)
    share_cols = width // tensor_count
    share_blocks = share_cols // features

    def here(v):
        own = lax.dynamic_slice_in_dim(v, tensor_index * share_cols, share_cols, 1)
        return own.reshape(v.shape[0], share_blocks, features).transpose(1, 0, 2)

    coeffs, coeff_own, squares, input_grad, gain_grad = coeff_sum(
        bt, bt_sib, ortho, back_all.reshape(tensor_count, share_blocks, tokens, features),
        here(standard), here(norm_gain[None, :]), jnp.broadcast_to(inv_std, (tokens, features)),
    )
    input_grad = input_grad.transpose(1, 0, 2).reshape(tokens, share_cols)
    gain_grad = gain_grad[:, 0].reshape(share_cols)
    col_inverse = 1.0 / (jnp.sqrt(squares[0:1]) + 1e-08)
    basis_new = coeff_own * col_inverse
    qkv_group = 3 * HEADS * HEAD_DIM // tensor_count
    qkv_scale = 0.2 * math.sqrt(D * (3 * HEADS * HEAD_DIM) / RANK)
    mlp_scale = 0.2 * math.sqrt(D * FF / RANK)
    position = jnp.arange(group_cols, dtype=jnp.int32)
    col_scale = jnp.where(position < qkv_group, qkv_scale, mlp_scale).astype(F32)
    moment_new, update = final_products(ortho, col_inverse, coeffs, buffer, col_scale[None, :])
    return (input_grad, gain_grad, moment_new, basis_new, update)


def solution(mesh):
    in_specs = (
        P("dp", None),
        P(),
        P("dp", "tensor"),
        P("dp", "tensor"),
        P("dp", "tensor"),
        P(("tensor", "dp"), None),
    )
    out_specs = (
        P("dp", "tensor"),
        P("tensor"),
        P("dp", "tensor"),
        P(("tensor", "dp"), None),
        P("dp", "tensor"),
    )
    return jax.shard_map(
        per_device, mesh=mesh, in_specs=in_specs, out_specs=out_specs, check_vma=False
    )
```

```python
import math

import jax
import jax.numpy as jnp
from jax import lax
from jax.experimental import pallas as pl
from jax.experimental.pallas import tpu as pltpu
from jax.sharding import PartitionSpec as P

D = 6144
HEADS = 24
HEAD_DIM = 128
FF = 12288
RANK = 512
MOMENTUM = 0.8
NORM_EPSILON = 1e-06

HI = lax.Precision.HIGHEST
MESH = pl.DeviceIdType.MESH
VMEM_LIMIT = 56 * 1024 * 1024
F32 = jnp.float32
BF16 = jnp.bfloat16


def dp_of(x, y, core):
    return (x * 4 + y) * 2 + core


def place():
    dp = lax.axis_index("dp")
    return dp // 8, (dp // 2) % 4, dp % 2, lax.axis_index("tensor")


def send(src, dst, send_sem, recv_sem, **peer):
    copy = pltpu.make_async_remote_copy(
        src_ref=src, dst_ref=dst, send_sem=send_sem, recv_sem=recv_sem,
        device_id=peer, device_id_type=MESH,
    )
    copy.start()
    return copy


def wait_recv(dst, recv_sem, **peer):
    pltpu.make_async_remote_copy(
        src_ref=dst, dst_ref=dst, send_sem=recv_sem, recv_sem=recv_sem,
        device_id=peer, device_id_type=MESH,
    ).wait_recv()


def greet(peers):
    barrier = pltpu.get_barrier_semaphore()
    for peer in peers:
        pl.semaphore_signal(barrier, inc=1, device_id=peer, device_id_type=MESH)
    pl.semaphore_wait(barrier, len(peers))


def plane_peers(x, y, core):
    return (
        [{"dp": dp_of((x + d) % 4, y, core)} for d in (1, 2, 3)]
        + [{"dp": dp_of(x, (y + d) % 4, core)} for d in (1, 2, 3)]
        + [{"dp": dp_of(x, y, 1 - core)}]
    )


def round_robin(generators):
    live = list(generators)
    while live:
        still = []
        for g in live:
            try:
                next(g)
                still.append(g)
            except StopIteration:
                pass
        live = still


def gather_stream(loc, first, ssem, rsem, base, sent):
    x0, y0, core, _ = place()
    a0, b0 = (x0, y0) if first == "x" else (y0, x0)
    sib = dp_of(x0, y0, 1 - core)

    def xy(a, b):
        return (a % 4, b % 4) if first == "x" else (b % 4, a % 4)

    def at(a, b, part, who=None):
        return loc(core if who is None else who, *xy(a, b), part)

    def to(a, b, block, part, slot):
        ref = at(*block, part)
        sent.append(send(ref, ref, ssem.at[base + slot], rsem.at[base + slot], dp=dp_of(*xy(a, b), core)))

    def got(block, part, slot):
        wait_recv(at(*block, part), rsem.at[base + slot], dp=sib)

    def share(block, slot):
        ref = at(*block, 2)
        sent.append(send(ref, ref, ssem.at[base + slot], rsem.at[base + slot], dp=sib))

    def spread(k, block):
        to(a0, b0 + 1, block, 2, 4 + 4 * k)
        to(a0, b0 - 1, block, 2, 5 + 4 * k)

    offs = (0, -1, 1, 2)
    to(a0 + 1, b0, (a0, b0), 2, 0)
    to(a0 - 1, b0, (a0, b0), 2, 1)
    yield
    spread(0, (a0, b0))
    share((a0, b0), 20)
    yield
    got((a0 - 1, b0), 2, 0)
    to(a0 + 1, b0, (a0 - 1, b0), 0, 2)
    got((a0 + 1, b0), 2, 1)
    to(a0 - 1, b0, (a0 + 1, b0), 1, 3)
    spread(1, (a0 - 1, b0))
    spread(2, (a0 + 1, b0))
    yield
    share((a0 - 1, b0), 21)
    share((a0 + 1, b0), 22)
    got((a0 + 2, b0), 0, 2)
    got((a0 + 2, b0), 1, 3)
    spread(3, (a0 + 2, b0))
    share((a0 + 2, b0), 23)
    yield
    for k in range(4):
        a = a0 + offs[k]
        got((a, b0 - 1), 2, 4 + 4 * k)
        to(a0, b0 + 1, (a, b0 - 1), 0, 6 + 4 * k)
        got((a, b0 + 1), 2, 5 + 4 * k)
        to(a0, b0 - 1, (a, b0 + 1), 1, 7 + 4 * k)
        share((a, b0 - 1), 24 + 3 * k)
        share((a, b0 + 1), 25 + 3 * k)
        yield
    for k in range(4):
        a = a0 + offs[k]
        got((a, b0 + 2), 0, 6 + 4 * k)
        got((a, b0 + 2), 1, 7 + 4 * k)
        share((a, b0 + 2), 26 + 3 * k)
        yield
    for k in range(4):
        a = a0 + offs[k]
        wait_recv(at(a, b0, 2, 1 - core), rsem.at[base + 20 + k], dp=sib)
        for j, b in enumerate((b0 - 1, b0 + 1, b0 + 2)):
            wait_recv(at(a, b, 2, 1 - core), rsem.at[base + 24 + 3 * k + j], dp=sib)
    yield


GATHER_SLOTS = 36
EXCHANGE_SLOTS = 6


def exchange_stream(src, mid, out, s, ssem, rsem, base, sent):
    x, y, core, _ = place()
    sib = dp_of(x, y, 1 - core)
    half = slice(16 * s, 16 * s + 16)

    def part(ref, a):
        return ref.at[a, :, half] if s == 0 else ref.at[:, a, half]

    def swapped(ref, b):
        return ref.at[:, b, half] if s == 0 else ref.at[b, :, half]

    a0, b0 = (x, y) if s == 0 else (y, x)

    def dev(a, b):
        return dp_of(a, b, core) if s == 0 else dp_of(b, a, core)

    mine = pltpu.make_async_copy(part(src, a0), mid.at[s, a0], ssem.at[base + 6])
    mine.start()
    for i in range(3):
        to = (a0 + 1 + i) % 4
        sent.append(send(part(src, to), mid.at[s, a0], ssem.at[base + i], rsem.at[base + i], dp=dev(to, b0)))
    yield
    for i in range(3):
        wait_recv(mid.at[s, (a0 + 3 - i) % 4], rsem.at[base + i], dp=sib)
    mine.wait()
    own = pltpu.make_async_copy(mid.at[s, :, b0], swapped(out, b0), ssem.at[base + 6])
    own.start()
    for i in range(3):
        to = (b0 + 1 + i) % 4
        sent.append(send(
            mid.at[s, :, to], swapped(out, b0), ssem.at[base + 3 + i], rsem.at[base + 3 + i], dp=dev(a0, to)
        ))
    yield
    own.wait()
    for i in range(3):
        wait_recv(swapped(out, (b0 + 3 - i) % 4), rsem.at[base + 3 + i], dp=sib)
    yield


def split(v):
    top = v.astype(BF16)
    return top, (v - top.astype(F32)).astype(BF16)


EX = 4 * GATHER_SLOTS
ZP = EX + 28
OTHER = ZP + 35


def front_kernel(in_ref, gain_ref, g_ref, w_ref, m_ref, r_ref,
                 p_ref, gram_ref, bt_ref, btsib_ref, buf_ref, backall_ref, std_ref, inv_ref,
                 rall, gall, got, std, nrm, exmid, exout, exsib, xt, both, bk, bksib, bsrc, bmid,
                 part, zbuf, gbuf, cbuf, xbuf, ybuf, ssem, rsem):
    x, y, core, z = place()
    chip = x * 4 + y
    sib = dp_of(x, y, 1 - core)
    xs = [(x + d) % 4 for d in (1, 2, 3)]
    ys = [(y + d) % 4 for d in (1, 2, 3)]
    zs = [(z + d) % 8 for d in range(1, 8)]
    greet([{"tensor": q} for q in zs] + plane_peers(x, y, core))
    sent = []
    rows, cols = m_ref.shape
    tokens, width = in_ref.shape
    cut = 1408

    other = pl.multiple_of(256 * (1 - core), 128)
    sent.append(send(r_ref.at[:, pl.ds(other, 256)], got, ssem.at[OTHER], rsem.at[OTHER], dp=sib))
    gall[core, pl.ds(pl.multiple_of(32 * chip, 32), 32)] = g_ref[...]

    def loc_g(s):
        def loc(who, bx, by, part):
            lo, n = ((0, cut), (cut, cols - cut), (0, cols))[part]
            return gall.at[who, pl.ds(pl.multiple_of(32 * (bx * 4 + by) + 16 * s, 16), 16), pl.ds(lo, n)]
        return loc

    def loc_r(s):
        def loc(who, bx, by, part):
            lo, n = ((0, 88), (88, 80), (0, 168))[part]
            row = pl.multiple_of((bx * 4 + by) * 168 + lo, 8)
            return rall.at[pl.ds(row, n), pl.ds(pl.multiple_of(256 * who + 128 * s, 128), 128)]
        return loc

    g_streams = [gather_stream(loc_g(s), "xy"[s], ssem, rsem, (2 + s) * GATHER_SLOTS, sent) for s in (0, 1)]
    for g in g_streams:
        next(g)
    for g in g_streams:
        next(g)

    wide = [in_ref[:, 384 * b:384 * b + 384].astype(F32) for b in range(16)]
    mean = sum(jnp.sum(v, axis=1, keepdims=True) for v in wide) * (1.0 / width)
    centered = [in_ref[:, 384 * b:384 * b + 384].astype(F32) - mean for b in range(16)]
    var = sum(jnp.sum(v * v, axis=1, keepdims=True) for v in centered) * (1.0 / width)
    inv = lax.rsqrt(var + NORM_EPSILON)
    inv_ref[...] = jnp.broadcast_to(inv, inv_ref.shape)
    for b in range(16):
        v = (in_ref[:, 384 * b:384 * b + 384].astype(F32) - mean) * inv
        std[b // 2, b % 2] = v
        nrm[b // 4, b % 4] = (v * gain_ref[:, 384 * b:384 * b + 384]).astype(BF16)
    std_ref[...] = std[z]
    ex = [exchange_stream(nrm, exmid, exout, s, ssem, rsem, EX + 7 * s, sent) for s in (0, 1)]
    for g in ex:
        next(g)

    wait_recv(got, rsem.at[OTHER], dp=sib)
    mine = r_ref[:, pl.ds(pl.multiple_of(256 * core, 128), 256)]
    theirs = got[...]
    rall[pl.ds(pl.multiple_of(chip * 168, 8), 168), pl.ds(pl.multiple_of(256 * core, 128), 256)] = jnp.concatenate(
        [jnp.where(core == 0, mine, theirs), jnp.where(core == 0, theirs, mine)], axis=0
    )
    r_streams = [gather_stream(loc_r(s), "xy"[s], ssem, rsem, s * GATHER_SLOTS, sent) for s in (0, 1)]

    def run(gens):
        live = []
        for g in gens:
            try:
                next(g)
                live.append(g)
            except StopIteration:
                pass
        return live

    def mine192(v):
        return jnp.where(core == 0, v[:, 0:192].astype(F32), v[:, 192:384].astype(F32))

    def after_exchange():
        sent.append(send(exout, exsib, ssem.at[OTHER + 1], rsem.at[OTHER + 1], dp=sib))
        for q in range(4):
            v = exout[q].reshape(4 * tokens, 384)
            xt[core, :, 128 * q:128 * q + 128] = mine192(v).T.astype(BF16)
        yield
        wait_recv(exsib, rsem.at[OTHER + 1], dp=sib)
        for q in range(4):
            v = exsib[q].reshape(4 * tokens, 384)
            xt[1 - core, :, 128 * q:128 * q + 128] = mine192(v).T.astype(BF16)
        yield

    def compute():
        for t in range(0, cols, 384):
            acc = m_ref[:, t:t + 384]
            for c in (0, 1):
                acc = acc + jnp.dot(xt[c], gall[c, :, t:t + 384], preferred_element_type=F32)
            buf_ref[:, t:t + 384] = acc
            top, low = split(acc)
            both[0:rows, t:t + 384] = top
            both[rows:2 * rows, t:t + 384] = low
            bt_ref[t:t + 384, :] = jnp.concatenate([top, low], axis=0).astype(F32).T.astype(BF16)
            yield
        sent.append(send(bt_ref, btsib_ref, ssem.at[OTHER + 2], rsem.at[OTHER + 2], dp=sib))
        for c in (0, 1):
            for q in (0, 256):
                bk[c, q:q + 256, 0:192] = lax.dot_general(
                    gall[c, q:q + 256, :], w_ref[...], (((1,), (1,)), ((), ())), preferred_element_type=F32
                )
                yield
        sent.append(send(bk.at[1 - core], bksib, ssem.at[OTHER + 3], rsem.at[OTHER + 3], dp=sib))
        yield

    bk[:, :, 128:256] = jnp.zeros((2, 512, 128), F32)
    tail = after_exchange()
    work = compute()
    r_live, g_live, x_live = r_streams, g_streams, ex
    r_live = run(r_live)
    turn = 0
    tail_live = [tail]
    while g_live or x_live or tail_live:
        g_live = run(g_live)
        if x_live:
            x_live = run(x_live)
        elif tail_live:
            tail_live = run(tail_live)
        turn += 1
        if turn % 2:
            r_live = run(r_live)
    work_live = [work]
    while r_live or work_live:
        r_live = run(r_live)
        work_live = run(work_live)

    part[...] = jnp.zeros_like(part)
    for t in range(0, cols, 384):
        r_top, r_low = split(rall[t:t + 384, :])
        one = jnp.dot(both[:, t:t + 384], r_top, preferred_element_type=F32)
        two = jnp.dot(both[0:rows, t:t + 384], r_low, preferred_element_type=F32)
        part[...] += one[0:rows] + (one[rows:] + two)

    order = (3, 4, 2, 5, 1, 6, 0)

    def rows24(q):
        return pl.ds(pl.multiple_of(24 * q, 8), 24)

    for i in order:
        sent.append(send(part.at[rows24(zs[i])], zbuf.at[i], ssem.at[ZP + i], rsem.at[ZP + i], tensor=zs[i]))

    wait_recv(bksib, rsem.at[OTHER + 3], dp=sib)
    for q in range(4):
        ours = bk[core, 128 * q:128 * q + 128, 0:192]
        their = bksib[128 * q:128 * q + 128, 0:192]
        bsrc[q] = jnp.concatenate(
            [jnp.where(core == 0, ours, their), jnp.where(core == 0, their, ours)], axis=1
        ).reshape(4, tokens, 384)
    back = [exchange_stream(bsrc, bmid, backall_ref, s, ssem, rsem, EX + 14 + 7 * s, sent) for s in (0, 1)]
    back = run(back)

    total = part[rows24(z), :]
    for i in reversed(order):
        wait_recv(zbuf.at[i], rsem.at[ZP + i], tensor=zs[i])
        total = total + zbuf[i]
    p_ref[rows24(z), :] = total
    mine = p_ref.at[rows24(z)]
    for i in order:
        sent.append(send(mine, mine, ssem.at[ZP + 7 + i], rsem.at[ZP + 7 + i], tensor=zs[i]))
    back = run(back)
    for i in reversed(order):
        src = (z + 7 - i) % 8
        wait_recv(p_ref.at[rows24(src)], rsem.at[ZP + 7 + i], tensor=zs[i])
    gbuf[...] = lax.dot_general(
        p_ref[:, pl.ds(pl.multiple_of(128 * (z // 2), 128), 128)], p_ref[...],
        (((0,), (0,)), ((), ())), precision=HI, preferred_element_type=F32,
    )
    half = 64 * (z % 2)
    away = gbuf.at[pl.ds(pl.multiple_of(half + 32 * (1 - core), 32), 32)]
    sent.append(send(away, cbuf, ssem.at[ZP + 14], rsem.at[ZP + 14], dp=sib))
    wait_recv(cbuf, rsem.at[ZP + 14], dp=sib)
    cbuf[...] += gbuf[pl.ds(pl.multiple_of(half + 32 * core, 32), 32), :]
    for i in range(3):
        sent.append(send(
            cbuf.at[pl.ds(pl.multiple_of(8 * xs[i], 8), 8)], xbuf.at[i], ssem.at[ZP + 15 + i], rsem.at[ZP + 15 + i],
            dp=dp_of(xs[i], y, core),
        ))
    total = cbuf[pl.ds(pl.multiple_of(8 * x, 8), 8), :]
    for i in range(3):
        wait_recv(xbuf.at[i], rsem.at[ZP + 15 + i], dp=sib)
        total = total + xbuf[i]
    ybuf[y] = total
    for i in range(3):
        sent.append(send(
            ybuf.at[y], ybuf.at[y], ssem.at[ZP + 18 + i], rsem.at[ZP + 18 + i], dp=dp_of(x, ys[i], core)
        ))
    for i in range(3):
        wait_recv(ybuf.at[(y + 3 - i) % 4], rsem.at[ZP + 18 + i], dp=sib)
    gram_ref[z, core, x] = (ybuf[0] + ybuf[1]) + (ybuf[2] + ybuf[3])
    mine = gram_ref.at[z, core, x]
    for i in order:
        sent.append(send(mine, mine, ssem.at[ZP + 21 + i], rsem.at[ZP + 21 + i], tensor=zs[i]))
    for i in reversed(order):
        wait_recv(gram_ref.at[(z + 7 - i) % 8, core, x], rsem.at[ZP + 21 + i], tensor=zs[i])
    mine = gram_ref.at[:, core, x]
    for i in range(3):
        sent.append(send(mine, mine, ssem.at[ZP + 28 + i], rsem.at[ZP + 28 + i], dp=dp_of(xs[i], y, core)))
    sent.append(send(mine, mine, ssem.at[ZP + 31], rsem.at[ZP + 31], dp=sib))
    for i in range(3):
        src = (x + 3 - i) % 4
        wait_recv(gram_ref.at[:, core, src], rsem.at[ZP + 28 + i], dp=sib)
        there = gram_ref.at[:, core, src]
        sent.append(send(there, there, ssem.at[ZP + 32 + i], rsem.at[ZP + 32 + i], dp=sib))
    back = run(back)
    wait_recv(gram_ref.at[:, 1 - core, x], rsem.at[ZP + 31], dp=sib)
    for i in range(3):
        wait_recv(gram_ref.at[:, 1 - core, (x + 3 - i) % 4], rsem.at[ZP + 32 + i], dp=sib)
    wait_recv(btsib_ref, rsem.at[OTHER + 2], dp=sib)
    for copy in sent:
        copy.wait_send()


def front(inputs, gain, out_grad, weight, moment, right_basis):
    vm = pl.BlockSpec(memory_space=pltpu.VMEM)
    rows, cols = moment.shape
    tokens = inputs.shape[0]
    return pl.pallas_call(
        front_kernel,
        out_shape=(
            jax.ShapeDtypeStruct((rows, RANK), F32),
            jax.ShapeDtypeStruct((8, 2, 4, 8, RANK), F32),
            jax.ShapeDtypeStruct((cols, 2 * rows), BF16),
            jax.ShapeDtypeStruct((cols, 2 * rows), BF16),
            jax.ShapeDtypeStruct((rows, cols), F32),
            jax.ShapeDtypeStruct((4, 4, tokens, 384), F32),
            jax.ShapeDtypeStruct((2, tokens, 384), F32),
            jax.ShapeDtypeStruct((tokens, 384), F32),
        ),
        in_specs=[vm] * 6,
        out_specs=(vm,) * 8,
        scratch_shapes=[
            pltpu.VMEM((cols, RANK), F32),
            pltpu.VMEM((2, 16 * tokens, cols), BF16),
            pltpu.VMEM((right_basis.shape[0], 256), F32),
            pltpu.VMEM((8, 2, tokens, 384), F32),
            pltpu.VMEM((4, 4, tokens, 384), BF16),
            pltpu.VMEM((2, 4, 4, 16, 384), BF16),
            pltpu.VMEM((4, 4, tokens, 384), BF16),
            pltpu.VMEM((4, 4, tokens, 384), BF16),
            pltpu.VMEM((2, rows, 16 * tokens), BF16),
            pltpu.VMEM((2 * rows, cols), BF16),
            pltpu.VMEM((2, 16 * tokens, 256), F32),
            pltpu.VMEM((16 * tokens, 256), F32),
            pltpu.VMEM((4, 4, tokens, 384), F32),
            pltpu.VMEM((2, 4, 4, 16, 384), F32),
            pltpu.VMEM((rows, RANK), F32),
            pltpu.VMEM((7, 24, RANK), F32),
            pltpu.VMEM((128, RANK), F32),
            pltpu.VMEM((32, RANK), F32),
            pltpu.VMEM((3, 8, RANK), F32),
            pltpu.VMEM((4, 8, RANK), F32),
            pltpu.SemaphoreType.DMA((OTHER + 4,)),
            pltpu.SemaphoreType.DMA((OTHER + 4,)),
        ],
        compiler_params=pltpu.CompilerParams(
            collective_id=1, has_side_effects=True, vmem_limit_bytes=VMEM_LIMIT
        ),
    )(inputs, gain, out_grad, weight, moment, right_basis)


def chol_kernel(g_ref, p_ref, o_ref, s_ref, w_ref):
    n_p = p_ref.shape[0]
    s_ref[:, 0:512] = g_ref[...]
    s_ref[:, 512:512 + n_p] = p_ref[...].T
    s_ref[:, 512 + n_p:] = jnp.zeros((512, s_ref.shape[1] - 512 - n_p), F32)
    lane = lax.broadcasted_iota(jnp.int32, (8, 128), 1)
    sub = lax.broadcasted_iota(jnp.int32, (8, 128), 0)

    def lane_splat(v, j):
        return jnp.broadcast_to(v[:, j:j + 1], (8, 128))

    def row_splat(v, i):
        return jnp.broadcast_to(v[i:i + 1, :], (8, 128))

    def block(kb, carry):
        base = pl.multiple_of(kb * 128, 128)
        tiles = [s_ref[pl.ds(pl.multiple_of(base + 8 * i, 8), 8), pl.ds(base, 128)] for i in range(16)]
        for k in range(16):
            x = tiles[k]
            inside = (lane >= 8 * k) & (lane < 8 * k + 8)
            c = [lane_splat(x, 8 * k + q) for q in range(8)]
            x = jnp.where(inside, (lane - 8 * k == sub).astype(F32), x)
            inv, up, rows = [], [], []
            scale = jnp.ones((8, 128), F32)
            for p in range(8):
                pd = row_splat(c[p], p)
                ip = 1.0 / pd
                scale = jnp.where(sub == p, lax.rsqrt(pd), scale)
                m = jnp.where(sub > p, c[p] * ip, 0.0)
                u = {}
                for q in range(p + 1, 8):
                    u[q] = row_splat(c[q], p)
                    c[q] = c[q] - m * u[q]
                r = row_splat(x, p)
                x = x - m * r
                inv.append(ip)
                up.append(u)
                rows.append(r)
            w_ref[8 * k:8 * k + 8, :] = jnp.where(lane <= sub + 8 * k, x * scale, 0.0)
            for g in range(k + 1, 16):
                v = tiles[g]
                e = [lane_splat(v, 8 * k + q) for q in range(8)]
                v = jnp.where(inside, 0.0, v)
                for p in range(8):
                    m = e[p] * inv[p]
                    for q in range(p + 1, 8):
                        e[q] = e[q] - m * up[p][q]
                    v = v - m * rows[p]
                tiles[g] = v
        rows_k = pl.ds(base, 128)
        s_ref[rows_k, :] = jnp.dot(w_ref[...], s_ref[rows_k, :], precision=HI, preferred_element_type=F32)
        for rb in range(1, 4):
            @pl.when(rb > kb)
            def _():
                ub = s_ref[rows_k, 128 * rb:128 * rb + 128]
                s_ref[128 * rb:128 * rb + 128, 128 * rb:] -= lax.dot_general(
                    ub, s_ref[rows_k, 128 * rb:], (((0,), (0,)), ((), ())), precision=HI,
                    preferred_element_type=F32,
                )
        return carry

    lax.fori_loop(0, 4, block, 0)
    o_ref[...] = s_ref[:, 512:512 + n_p].T


def chol_solve(gram, projected):
    vm = pl.BlockSpec(memory_space=pltpu.VMEM)
    return pl.pallas_call(
        chol_kernel,
        out_shape=jax.ShapeDtypeStruct(projected.shape, F32),
        in_specs=[vm, vm],
        out_specs=vm,
        scratch_shapes=[pltpu.VMEM((RANK, 768), F32), pltpu.VMEM((128, 128), F32)],
        compiler_params=pltpu.CompilerParams(vmem_limit_bytes=VMEM_LIMIT),
    )(gram, projected)


SPLIT = ((0, 96), (96, 80), (0, 176))


def coeff_kernel(bt_ref, btsib_ref, o_ref, back_ref, std_ref, gain_ref, inv_ref,
                 call_ref, cown_ref, csq_ref, ig_ref, gg_ref,
                 osib, rhs, c_ref, sbuf, rbuf, acc, s2, r2, fin, fsib, agb,
                 xsq, ysq, zsq, sqs, ngbuf, stat, gx, gy, gc, ssem, rsem, gs, gr, ns, nr):
    x, y, core, z = place()
    sib = dp_of(x, y, 1 - core)
    xs = [(x + d) % 4 for d in (1, 2, 3)]
    ys = [(y + d) % 4 for d in (1, 2, 3)]
    zs = [(z + d) % 8 for d in range(1, 8)]
    greet(
        [{"tensor": q} for q in zs]
        + [{"dp": dp_of(q, y, core)} for q in xs]
        + [{"dp": dp_of(x, q, core)} for q in ys]
        + [{"dp": sib}]
    )
    sent = []
    first = ("x", "y")

    def half(who):
        return pl.ds(pl.multiple_of(256 * who, 128), 256)

    sent.append(send(o_ref.at[:, half(1 - core)], osib, ssem.at[0], rsem.at[0], dp=sib))
    for i in range(7):
        sent.append(send(back_ref.at[zs[i]], ngbuf.at[i], ns.at[i], nr.at[i], tensor=zs[i]))

    def fill(v):
        top, low = split(v)
        n = v.shape[0]
        rhs[0:n, 0:256] = top
        rhs[n:2 * n, 0:256] = top
        rhs[0:n, 256:512] = low
        rhs[n:2 * n, 256:512] = low

    cols = bt_ref.shape[0]
    fill(o_ref[:, half(core)])
    for t in range(0, cols, 384):
        two = jnp.dot(bt_ref[t:t + 384, :], rhs[...], preferred_element_type=F32)
        c_ref[t:t + 384, :] = two[:, 0:256] + two[:, 256:512]
    wait_recv(osib, rsem.at[0], dp=sib)
    fill(osib[...])
    for t in range(0, cols, 384):
        two = jnp.dot(btsib_ref[t:t + 384, :], rhs[...], preferred_element_type=F32)
        c_ref[t:t + 384, :] += two[:, 0:256] + two[:, 256:512]

    def cols_of(who, s):
        return pl.ds(pl.multiple_of(256 * who + 128 * s, 128), 128)

    a0 = (x, y)
    b0 = (y, x)

    def own(s, off, b):
        a = (a0[s] + off) % 4
        bx, by = (a, b) if s == 0 else (b, a)
        return c_ref[pl.ds(pl.multiple_of(168 * (bx * 4 + by), 8), 168), 128 * s:128 * s + 128]

    def dev(s, a, b):
        a, b = a % 4, b % 4
        return dp_of(a, b, core) if s == 0 else dp_of(b, a, core)

    zero_pad = jnp.zeros((8, 128), F32)

    def padded(v):
        return jnp.concatenate([v, zero_pad], axis=0).astype(BF16)

    def reduce_stream(s):
        base = 8 + 8 * s
        a, b = a0[s], b0[s]
        right, left = dev(s, a + 1, b), dev(s, a - 1, b)
        for j in range(4):
            sbuf[s, 0, j] = padded(own(s, 2, j))
        sent.append(send(sbuf.at[s, 0, 0:2], rbuf.at[s, 0, 0:2], ssem.at[base], rsem.at[base], dp=right))
        sent.append(send(sbuf.at[s, 0, 2:4], rbuf.at[s, 0, 2:4], ssem.at[base + 1], rsem.at[base + 1], dp=left))
        yield
        for j in (2, 3):
            sbuf[s, 1, j] = padded(own(s, 1, j))
        for j in (0, 1):
            sbuf[s, 2, j] = padded(own(s, 3, j))
        yield
        wait_recv(rbuf.at[s, 0, 0:2], rsem.at[base], dp=left)
        for j in (0, 1):
            sbuf[s, 1, j] = padded(own(s, 1, j) + rbuf[s, 0, j, 0:168].astype(F32))
        sent.append(send(sbuf.at[s, 1], rbuf.at[s, 1], ssem.at[base + 2], rsem.at[base + 2], dp=right))
        yield
        wait_recv(rbuf.at[s, 0, 2:4], rsem.at[base + 1], dp=right)
        for j in (2, 3):
            sbuf[s, 2, j] = padded(own(s, 3, j) + rbuf[s, 0, j, 0:168].astype(F32))
        sent.append(send(sbuf.at[s, 2], rbuf.at[s, 2], ssem.at[base + 3], rsem.at[base + 3], dp=left))
        yield
        for j in range(4):
            acc[s, j] = own(s, 0, j)
        yield
        wait_recv(rbuf.at[s, 1], rsem.at[base + 2], dp=left)
        wait_recv(rbuf.at[s, 2], rsem.at[base + 3], dp=right)

        def summed(off):
            j = (b + off) % 4
            return acc[s, j] + (rbuf[s, 1, j, 0:168].astype(F32) + rbuf[s, 2, j, 0:168].astype(F32))

        right, left = dev(s, a, b + 1), dev(s, a, b - 1)
        s2[s, 0] = padded(summed(2))
        sent.append(send(s2.at[s, 0, 0:96], r2.at[s, 0, 0:96], ssem.at[base + 4], rsem.at[base + 4], dp=right))
        sent.append(send(s2.at[s, 0, 96:176], r2.at[s, 0, 96:176], ssem.at[base + 5], rsem.at[base + 5], dp=left))
        yield
        one, three, zero = summed(1), summed(3), summed(0)
        wait_recv(r2.at[s, 0, 0:96], rsem.at[base + 4], dp=left)
        s2[s, 1, 0:96] = (one[0:96] + r2[s, 0, 0:96].astype(F32)).astype(BF16)
        s2[s, 1, 96:176] = padded(one[96:168])
        sent.append(send(s2.at[s, 1], r2.at[s, 1], ssem.at[base + 6], rsem.at[base + 6], dp=right))
        wait_recv(r2.at[s, 0, 96:176], rsem.at[base + 5], dp=right)
        s2[s, 2, 0:96] = three[0:96].astype(BF16)
        s2[s, 2, 96:176] = padded(three[96:168] + r2[s, 0, 96:168].astype(F32))
        sent.append(send(s2.at[s, 2], r2.at[s, 2], ssem.at[base + 7], rsem.at[base + 7], dp=left))
        yield
        wait_recv(r2.at[s, 1], rsem.at[base + 6], dp=left)
        wait_recv(r2.at[s, 2], rsem.at[base + 7], dp=right)
        total = zero + (r2[s, 1, 0:168].astype(F32) + r2[s, 2, 0:168].astype(F32))
        fin[:, 128 * s:128 * s + 128] = total
        agb[x * 4 + y, :, cols_of(core, s)] = padded(total)
        yield

    round_robin([reduce_stream(0), reduce_stream(1)])

    def norms():
        sent.append(send(fin, fsib, ssem.at[24], rsem.at[24], dp=sib))
        v = fin[...]
        xsq[x] = jnp.broadcast_to(jnp.sum(v * v, axis=0, keepdims=True), (8, 256))
        for i in range(3):
            sent.append(send(xsq.at[x], xsq.at[x], ssem.at[25 + i], rsem.at[25 + i], dp=dp_of(xs[i], y, core)))
        yield
        for i in range(3):
            wait_recv(xsq.at[(x + 3 - i) % 4], rsem.at[25 + i], dp=sib)
        ysq[y] = (xsq[0] + xsq[1]) + (xsq[2] + xsq[3])
        for i in range(3):
            sent.append(send(ysq.at[y], ysq.at[y], ssem.at[28 + i], rsem.at[28 + i], dp=dp_of(x, ys[i], core)))
        yield
        for i in range(3):
            wait_recv(ysq.at[(y + 3 - i) % 4], rsem.at[28 + i], dp=sib)
        zsq[z] = (ysq[0] + ysq[1]) + (ysq[2] + ysq[3])
        for i in range(7):
            sent.append(send(zsq.at[z], zsq.at[z], ssem.at[31 + i], rsem.at[31 + i], tensor=zs[i]))
        yield
        for i in range(7):
            wait_recv(zsq.at[(z + 7 - i) % 8], rsem.at[31 + i], tensor=zs[i])
        total = zsq[0]
        for i in range(1, 8):
            total = total + zsq[i]
        sqs[core] = total
        sent.append(send(sqs.at[core], sqs.at[core], ssem.at[38], rsem.at[38], dp=sib))
        yield
        wait_recv(fsib, rsem.at[24], dp=sib)
        left = jnp.where(core == 0, fin[0:84], fsib[84:168])
        right = jnp.where(core == 0, fsib[0:84], fin[84:168])
        cown_ref[:, 0:256] = left
        cown_ref[:, 256:512] = right
        yield
        wait_recv(sqs.at[1 - core], rsem.at[38], dp=sib)
        csq_ref[:, 0:256] = sqs[0]
        csq_ref[:, 256:512] = sqs[1]
        yield

    def input_grad():
        total = back_ref[z]
        for i in range(7):
            wait_recv(ngbuf.at[i], nr.at[i], tensor=zs[i])
            total = total + ngbuf[i]
        std = std_ref[...]
        scaled = total * gain_ref[z]
        lane = lax.broadcasted_iota(jnp.int32, (32, 128), 1)

        def per_token(v):
            return jnp.sum(jnp.sum(v, axis=0), axis=1, keepdims=True)

        stat[z] = jnp.where(lane < 64, per_token(scaled), per_token(scaled * std))
        for i in range(7):
            sent.append(send(stat.at[z], stat.at[z], ns.at[7 + i], nr.at[7 + i], tensor=zs[i]))
        gx[x] = jnp.broadcast_to(jnp.sum(total * std, axis=1, keepdims=True), gx.shape[1:])
        for i in range(3):
            sent.append(send(gx.at[x], gx.at[x], ns.at[14 + i], nr.at[14 + i], dp=dp_of(xs[i], y, core)))
        yield
        for i in range(3):
            wait_recv(gx.at[(x + 3 - i) % 4], nr.at[14 + i], dp=sib)
        gy[y] = (gx[0] + gx[1]) + (gx[2] + gx[3])
        for i in range(3):
            sent.append(send(gy.at[y], gy.at[y], ns.at[17 + i], nr.at[17 + i], dp=dp_of(x, ys[i], core)))
        for i in range(7):
            wait_recv(stat.at[(z + 7 - i) % 8], nr.at[7 + i], tensor=zs[i])
        sums = stat[0]
        for i in range(1, 8):
            sums = sums + stat[i]
        sums = sums * (1.0 / (16 * 384))
        full = inv_ref[...] * (scaled - sums[:, 0:1] - std * sums[:, 64:65])
        ig_ref[:, 0:384] = full[0].astype(BF16)
        ig_ref[:, 384:768] = full[1].astype(BF16)
        yield
        for i in range(3):
            wait_recv(gy.at[(y + 3 - i) % 4], nr.at[17 + i], dp=sib)
        gc[core] = (gy[0] + gy[1]) + (gy[2] + gy[3])
        sent.append(send(gc.at[core], gc.at[core], ns.at[20], nr.at[20], dp=sib))
        yield
        wait_recv(gc.at[1 - core], nr.at[20], dp=sib)
        gg_ref[:, 0:384] = gc[0, 0] + gc[1, 0]
        gg_ref[:, 384:768] = gc[0, 1] + gc[1, 1]
        yield

    def loc(s):
        def at(who, bx, by, part):
            lo, rows = SPLIT[part]
            return agb.at[bx * 4 + by, pl.ds(lo, rows), cols_of(who, s)]
        return at

    round_robin([
        gather_stream(loc(0), first[0], gs, gr, 0, sent),
        gather_stream(loc(1), first[1], gs, gr, GATHER_SLOTS, sent),
        norms(),
        input_grad(),
    ])
    for j in range(8):
        two = jnp.concatenate([agb[2 * j, 0:168].astype(F32), agb[2 * j + 1, 0:168].astype(F32)], axis=0)
        call_ref[336 * j:336 * j + 336, :] = two.astype(BF16)
    for copy in sent:
        copy.wait_send()


def coeff_sum(bt, bt_sib, ortho, back, standard, gain, inv_std):
    vm = pl.BlockSpec(memory_space=pltpu.VMEM)
    block = standard.shape
    return pl.pallas_call(
        coeff_kernel,
        out_shape=(
            jax.ShapeDtypeStruct((2688, RANK), BF16),
            jax.ShapeDtypeStruct((84, RANK), F32),
            jax.ShapeDtypeStruct((8, RANK), F32),
            jax.ShapeDtypeStruct((32, 768), BF16),
            jax.ShapeDtypeStruct((8, 768), F32),
        ),
        in_specs=[vm] * 7,
        out_specs=(vm,) * 5,
        scratch_shapes=[
            pltpu.VMEM((192, 256), F32),
            pltpu.VMEM((384, RANK), BF16),
            pltpu.VMEM((2688, 256), F32),
            pltpu.VMEM((2, 3, 4, 176, 128), BF16),
            pltpu.VMEM((2, 3, 4, 176, 128), BF16),
            pltpu.VMEM((2, 4, 168, 128), F32),
            pltpu.VMEM((2, 3, 176, 128), BF16),
            pltpu.VMEM((2, 3, 176, 128), BF16),
            pltpu.VMEM((168, 256), F32),
            pltpu.VMEM((168, 256), F32),
            pltpu.VMEM((16, 176, RANK), BF16),
            pltpu.VMEM((4, 8, 256), F32),
            pltpu.VMEM((4, 8, 256), F32),
            pltpu.VMEM((8, 8, 256), F32),
            pltpu.VMEM((2, 8, 256), F32),
            pltpu.VMEM((7,) + block, F32),
            pltpu.VMEM((8, 32, 128), F32),
            pltpu.VMEM((4, 2, 8, 384), F32),
            pltpu.VMEM((4, 2, 8, 384), F32),
            pltpu.VMEM((2, 2, 8, 384), F32),
            pltpu.SemaphoreType.DMA((39,)),
            pltpu.SemaphoreType.DMA((39,)),
            pltpu.SemaphoreType.DMA((2 * GATHER_SLOTS,)),
            pltpu.SemaphoreType.DMA((2 * GATHER_SLOTS,)),
            pltpu.SemaphoreType.DMA((21,)),
            pltpu.SemaphoreType.DMA((21,)),
        ],
        compiler_params=pltpu.CompilerParams(
            collective_id=3, has_side_effects=True, vmem_limit_bytes=VMEM_LIMIT
        ),
    )(bt, bt_sib, ortho, back, standard, gain, inv_std)


def final_kernel(group, qkv_scale, mlp_scale, o_ref, csq_ref, c_ref, buf_ref, cown_ref, ig_ref, gg_ref,
                 mom_ref, upd_ref, basis_ref, igo_ref, ggo_ref, lhs):
    rows = o_ref.shape[0]
    step = pl.program_id(0)

    @pl.when(step == 0)
    def _():
        inv = 1.0 / (jnp.sqrt(csq_ref[0:1]) + 1e-08)
        o = o_ref[...]
        lhs[0:rows, :] = o.astype(BF16)
        top, low = split(o * inv)
        lhs[rows:2 * rows, :] = top
        lhs[2 * rows:3 * rows, :] = low
        basis_ref[...] = cown_ref[...] * inv
        igo_ref[...] = ig_ref[...]
        ggo_ref[...] = gg_ref[0:1]

    out = lax.dot_general(lhs[...], c_ref[...], (((1,), (1,)), ((), ())), preferred_element_type=F32)
    tile = out.shape[1]
    position = lax.broadcasted_iota(jnp.int32, (1, tile), 1) + step * tile
    scale = jnp.where(position < group, qkv_scale, mlp_scale)
    mom_ref[...] = buf_ref[...] - (1.0 - MOMENTUM) * out[0:rows]
    upd_ref[...] = (out[rows:2 * rows] + out[2 * rows:3 * rows]) * scale


def final_products(o, squares, coeffs, buffer, coeff_own, input_grad, gain_grad, *scales):
    rows, cols = buffer.shape
    tile = 896

    def whole(v):
        return pl.BlockSpec(v.shape, lambda i: (0,) * v.ndim)

    by_col = pl.BlockSpec((rows, tile), lambda i: (0, i))
    gain_out = jax.ShapeDtypeStruct((1, gain_grad.shape[1]), F32)
    return pl.pallas_call(
        lambda *refs: final_kernel(*scales, *refs),
        grid=(cols // tile,),
        out_shape=(
            jax.ShapeDtypeStruct(buffer.shape, F32),
            jax.ShapeDtypeStruct(buffer.shape, F32),
            jax.ShapeDtypeStruct(coeff_own.shape, F32),
            jax.ShapeDtypeStruct(input_grad.shape, BF16),
            gain_out,
        ),
        in_specs=[
            whole(o),
            whole(squares),
            pl.BlockSpec((tile, RANK), lambda i: (i, 0)),
            by_col,
            whole(coeff_own),
            whole(input_grad),
            whole(gain_grad),
        ],
        out_specs=(by_col, by_col, whole(coeff_own), whole(input_grad), whole(gain_out)),
        scratch_shapes=[pltpu.VMEM((3 * rows, RANK), BF16)],
        compiler_params=pltpu.CompilerParams(vmem_limit_bytes=VMEM_LIMIT),
    )(o, squares, coeffs, buffer, coeff_own, input_grad, gain_grad)


def per_device(inputs, norm_gain, out_grad, weight, moment, right_basis):
    tensor_count = lax.axis_size("tensor")
    gain = norm_gain[None, :]
    projected, gram, bt, bt_sib, buffer, back_all, standard, inv_std = front(
        inputs, gain, out_grad, weight, moment, right_basis
    )
    ortho = chol_solve(gram.reshape(RANK, RANK), projected)
    coeffs, coeff_own, squares, input_grad, gain_grad = coeff_sum(
        bt, bt_sib, ortho, back_all.reshape(tensor_count, 2, inputs.shape[0], 384),
        standard, gain.reshape(tensor_count, 2, 1, 384), inv_std,
    )
    qkv_group = 3 * HEADS * HEAD_DIM // tensor_count
    qkv_scale = 0.2 * math.sqrt(D * (3 * HEADS * HEAD_DIM) / RANK)
    mlp_scale = 0.2 * math.sqrt(D * FF / RANK)
    moment_new, update, basis_new, input_grad, gain_grad = final_products(
        ortho, squares, coeffs, buffer, coeff_own, input_grad, gain_grad, qkv_group, qkv_scale, mlp_scale
    )
    return (input_grad, gain_grad.reshape(gain_grad.shape[1]), moment_new, basis_new, update)


def solution(mesh):
    in_specs = (
        P("dp", None),
        P(),
        P("dp", "tensor"),
        P("dp", "tensor"),
        P("dp", "tensor"),
        P(("tensor", "dp"), None),
    )
    out_specs = (
        P("dp", "tensor"),
        P("tensor"),
        P("dp", "tensor"),
        P(("tensor", "dp"), None),
        P("dp", "tensor"),
    )
    return jax.shard_map(
        per_device, mesh=mesh, in_specs=in_specs, out_specs=out_specs, check_vma=False
    )
```

```python
import math

import jax
import jax.numpy as jnp
from jax import lax
from jax.experimental import pallas as pl
from jax.experimental.pallas import tpu as pltpu
from jax.sharding import PartitionSpec as P

D = 6144
HEADS = 24
HEAD_DIM = 128
FF = 12288
RANK = 512
MOMENTUM = 0.8
NORM_EPSILON = 1e-06

HI = lax.Precision.HIGHEST
MESH = pl.DeviceIdType.MESH
VMEM_LIMIT = 56 * 1024 * 1024
F32 = jnp.float32
BF16 = jnp.bfloat16


def dp_of(x, y, core):
    return (x * 4 + y) * 2 + core


def place():
    dp = lax.axis_index("dp")
    return dp // 8, (dp // 2) % 4, dp % 2, lax.axis_index("tensor")


def send(src, dst, send_sem, recv_sem, **peer):
    copy = pltpu.make_async_remote_copy(
        src_ref=src, dst_ref=dst, send_sem=send_sem, recv_sem=recv_sem,
        device_id=peer, device_id_type=MESH,
    )
    copy.start()
    return copy


def wait_recv(dst, recv_sem, **peer):
    pltpu.make_async_remote_copy(
        src_ref=dst, dst_ref=dst, send_sem=recv_sem, recv_sem=recv_sem,
        device_id=peer, device_id_type=MESH,
    ).wait_recv()


def greet(peers):
    barrier = pltpu.get_barrier_semaphore()
    for peer in peers:
        pl.semaphore_signal(barrier, inc=1, device_id=peer, device_id_type=MESH)
    pl.semaphore_wait(barrier, len(peers))


def plane_peers(x, y, core):
    return (
        [{"dp": dp_of((x + d) % 4, y, core)} for d in (1, 2, 3)]
        + [{"dp": dp_of(x, (y + d) % 4, core)} for d in (1, 2, 3)]
        + [{"dp": dp_of(x, y, 1 - core)}]
    )


def round_robin(generators):
    live = list(generators)
    while live:
        still = []
        for g in live:
            try:
                next(g)
                still.append(g)
            except StopIteration:
                pass
        live = still


def gather_stream(loc, first, ssem, rsem, base, sent):
    x0, y0, core, _ = place()
    a0, b0 = (x0, y0) if first == "x" else (y0, x0)
    sib = dp_of(x0, y0, 1 - core)

    def xy(a, b):
        return (a % 4, b % 4) if first == "x" else (b % 4, a % 4)

    def at(a, b, part, who=None):
        return loc(core if who is None else who, *xy(a, b), part)

    def to(a, b, block, part, slot):
        ref = at(*block, part)
        sent.append(send(ref, ref, ssem.at[base + slot], rsem.at[base + slot], dp=dp_of(*xy(a, b), core)))

    def got(block, part, slot):
        wait_recv(at(*block, part), rsem.at[base + slot], dp=sib)

    def share(block, slot):
        ref = at(*block, 2)
        sent.append(send(ref, ref, ssem.at[base + slot], rsem.at[base + slot], dp=sib))

    def spread(k, block):
        to(a0, b0 + 1, block, 2, 4 + 4 * k)
        to(a0, b0 - 1, block, 2, 5 + 4 * k)

    offs = (0, -1, 1, 2)
    to(a0 + 1, b0, (a0, b0), 2, 0)
    to(a0 - 1, b0, (a0, b0), 2, 1)
    yield
    spread(0, (a0, b0))
    share((a0, b0), 20)
    yield
    got((a0 - 1, b0), 2, 0)
    to(a0 + 1, b0, (a0 - 1, b0), 0, 2)
    got((a0 + 1, b0), 2, 1)
    to(a0 - 1, b0, (a0 + 1, b0), 1, 3)
    spread(1, (a0 - 1, b0))
    spread(2, (a0 + 1, b0))
    yield
    share((a0 - 1, b0), 21)
    share((a0 + 1, b0), 22)
    got((a0 + 2, b0), 0, 2)
    got((a0 + 2, b0), 1, 3)
    spread(3, (a0 + 2, b0))
    share((a0 + 2, b0), 23)
    yield
    for k in range(4):
        a = a0 + offs[k]
        got((a, b0 - 1), 2, 4 + 4 * k)
        to(a0, b0 + 1, (a, b0 - 1), 0, 6 + 4 * k)
        got((a, b0 + 1), 2, 5 + 4 * k)
        to(a0, b0 - 1, (a, b0 + 1), 1, 7 + 4 * k)
        share((a, b0 - 1), 24 + 3 * k)
        share((a, b0 + 1), 25 + 3 * k)
        yield
    for k in range(4):
        a = a0 + offs[k]
        got((a, b0 + 2), 0, 6 + 4 * k)
        got((a, b0 + 2), 1, 7 + 4 * k)
        share((a, b0 + 2), 26 + 3 * k)
        yield
    for k in range(4):
        a = a0 + offs[k]
        wait_recv(at(a, b0, 2, 1 - core), rsem.at[base + 20 + k], dp=sib)
        for j, b in enumerate((b0 - 1, b0 + 1, b0 + 2)):
            wait_recv(at(a, b, 2, 1 - core), rsem.at[base + 24 + 3 * k + j], dp=sib)
    yield


GATHER_SLOTS = 36
EXCHANGE_SLOTS = 6


def exchange_stream(src, mid, out, s, ssem, rsem, base, sent):
    x, y, core, _ = place()
    sib = dp_of(x, y, 1 - core)
    half = slice(16 * s, 16 * s + 16)

    def part(ref, a):
        return ref.at[a, :, half] if s == 0 else ref.at[:, a, half]

    def swapped(ref, b):
        return ref.at[:, b, half] if s == 0 else ref.at[b, :, half]

    a0, b0 = (x, y) if s == 0 else (y, x)

    def dev(a, b):
        return dp_of(a, b, core) if s == 0 else dp_of(b, a, core)

    mine = pltpu.make_async_copy(part(src, a0), mid.at[s, a0], ssem.at[base + 6])
    mine.start()
    for i in range(3):
        to = (a0 + 1 + i) % 4
        sent.append(send(part(src, to), mid.at[s, a0], ssem.at[base + i], rsem.at[base + i], dp=dev(to, b0)))
    yield
    for i in range(3):
        wait_recv(mid.at[s, (a0 + 3 - i) % 4], rsem.at[base + i], dp=sib)
    mine.wait()
    own = pltpu.make_async_copy(mid.at[s, :, b0], swapped(out, b0), ssem.at[base + 6])
    own.start()
    for i in range(3):
        to = (b0 + 1 + i) % 4
        sent.append(send(
            mid.at[s, :, to], swapped(out, b0), ssem.at[base + 3 + i], rsem.at[base + 3 + i], dp=dev(a0, to)
        ))
    yield
    own.wait()
    for i in range(3):
        wait_recv(swapped(out, (b0 + 3 - i) % 4), rsem.at[base + 3 + i], dp=sib)
    yield


def split(v):
    top = v.astype(BF16)
    return top, (v - top.astype(F32)).astype(BF16)


EX = 4 * GATHER_SLOTS
ZP = EX + 28
OTHER = ZP + 39


def front_kernel(in_ref, gain_ref, g_ref, w_ref, m_ref, r_ref,
                 p_ref, gram_ref, bt_ref, btsib_ref, buf_ref, backall_ref, std_ref, inv_ref,
                 rall, gall, got, std, nrm, exmid, exout, exsib, xt, both, bk, bksib, bsrc, bmid,
                 part, zbuf, gbuf, cbuf, xbuf, ybuf, ssem, rsem):
    x, y, core, z = place()
    chip = x * 4 + y
    sib = dp_of(x, y, 1 - core)
    xs = [(x + d) % 4 for d in (1, 2, 3)]
    ys = [(y + d) % 4 for d in (1, 2, 3)]
    zs = [(z + d) % 8 for d in range(1, 8)]
    greet([{"tensor": q} for q in zs] + plane_peers(x, y, core))
    sent = []
    rows, cols = m_ref.shape
    tokens, width = in_ref.shape
    cut = 1408

    other = pl.multiple_of(256 * (1 - core), 128)
    sent.append(send(r_ref.at[:, pl.ds(other, 256)], got, ssem.at[OTHER], rsem.at[OTHER], dp=sib))
    gall[core, pl.ds(pl.multiple_of(32 * chip, 32), 32)] = g_ref[...]

    def loc_g(s):
        def loc(who, bx, by, part):
            lo, n = ((0, cut), (cut, cols - cut), (0, cols))[part]
            return gall.at[who, pl.ds(pl.multiple_of(32 * (bx * 4 + by) + 16 * s, 16), 16), pl.ds(lo, n)]
        return loc

    def loc_r(s):
        def loc(who, bx, by, part):
            lo, n = ((0, 88), (88, 80), (0, 168))[part]
            row = pl.multiple_of((bx * 4 + by) * 168 + lo, 8)
            return rall.at[pl.ds(row, n), pl.ds(pl.multiple_of(256 * who + 128 * s, 128), 128)]
        return loc

    g_streams = [gather_stream(loc_g(s), "xy"[s], ssem, rsem, (2 + s) * GATHER_SLOTS, sent) for s in (0, 1)]
    for g in g_streams:
        next(g)
    for g in g_streams:
        next(g)

    wide = [in_ref[:, 384 * b:384 * b + 384].astype(F32) for b in range(16)]
    mean = sum(jnp.sum(v, axis=1, keepdims=True) for v in wide) * (1.0 / width)
    centered = [in_ref[:, 384 * b:384 * b + 384].astype(F32) - mean for b in range(16)]
    var = sum(jnp.sum(v * v, axis=1, keepdims=True) for v in centered) * (1.0 / width)
    inv = lax.rsqrt(var + NORM_EPSILON)
    inv_ref[...] = jnp.broadcast_to(inv, inv_ref.shape)
    for b in range(16):
        v = (in_ref[:, 384 * b:384 * b + 384].astype(F32) - mean) * inv
        std[b // 2, b % 2] = v
        nrm[b // 4, b % 4] = (v * gain_ref[:, 384 * b:384 * b + 384]).astype(BF16)
    std_ref[...] = std[z]
    ex = [exchange_stream(nrm, exmid, exout, s, ssem, rsem, EX + 7 * s, sent) for s in (0, 1)]
    for g in ex:
        next(g)

    wait_recv(got, rsem.at[OTHER], dp=sib)
    mine = r_ref[:, pl.ds(pl.multiple_of(256 * core, 128), 256)]
    theirs = got[...]
    rall[pl.ds(pl.multiple_of(chip * 168, 8), 168), pl.ds(pl.multiple_of(256 * core, 128), 256)] = jnp.concatenate(
        [jnp.where(core == 0, mine, theirs), jnp.where(core == 0, theirs, mine)], axis=0
    )
    r_streams = [gather_stream(loc_r(s), "xy"[s], ssem, rsem, s * GATHER_SLOTS, sent) for s in (0, 1)]

    def run(gens):
        live = []
        for g in gens:
            try:
                next(g)
                live.append(g)
            except StopIteration:
                pass
        return live

    def mine192(v):
        return jnp.where(core == 0, v[:, 0:192].astype(F32), v[:, 192:384].astype(F32))

    def after_exchange():
        sent.append(send(exout, exsib, ssem.at[OTHER + 1], rsem.at[OTHER + 1], dp=sib))
        for q in range(4):
            v = exout[q].reshape(4 * tokens, 384)
            xt[core, :, 128 * q:128 * q + 128] = mine192(v).T.astype(BF16)
        yield
        wait_recv(exsib, rsem.at[OTHER + 1], dp=sib)
        for q in range(4):
            v = exsib[q].reshape(4 * tokens, 384)
            xt[1 - core, :, 128 * q:128 * q + 128] = mine192(v).T.astype(BF16)
        yield

    def compute():
        for c in (0, 1):
            for q in (0, 256):
                bk[c, q:q + 256, 0:192] = lax.dot_general(
                    gall[c, q:q + 256, :], w_ref[...], (((1,), (1,)), ((), ())), preferred_element_type=F32
                )
                yield
        sent.append(send(bk.at[1 - core], bksib, ssem.at[OTHER + 3], rsem.at[OTHER + 3], dp=sib))
        for t in range(0, cols, 384):
            acc = m_ref[:, t:t + 384]
            for c in (0, 1):
                acc = acc + jnp.dot(xt[c], gall[c, :, t:t + 384], preferred_element_type=F32)
            buf_ref[:, t:t + 384] = acc
            top, low = split(acc)
            both[0:rows, t:t + 384] = top
            both[rows:2 * rows, t:t + 384] = low
            bt_ref[t:t + 384, :] = jnp.concatenate([top, low], axis=0).astype(F32).T.astype(BF16)
            yield
        sent.append(send(bt_ref, btsib_ref, ssem.at[OTHER + 2], rsem.at[OTHER + 2], dp=sib))
        wait_recv(bksib, rsem.at[OTHER + 3], dp=sib)
        for q in range(4):
            ours = bk[core, 128 * q:128 * q + 128, 0:192]
            their = bksib[128 * q:128 * q + 128, 0:192]
            bsrc[q] = jnp.concatenate(
                [jnp.where(core == 0, ours, their), jnp.where(core == 0, their, ours)], axis=1
            ).reshape(4, tokens, 384)
        yield

    bk[:, :, 128:256] = jnp.zeros((2, 512, 128), F32)
    tail = after_exchange()
    work = compute()
    r_live, g_live, x_live = r_streams, g_streams, ex
    r_live = run(r_live)
    tail_live = [tail]
    while g_live or x_live or tail_live:
        g_live = run(g_live)
        if x_live:
            x_live = run(x_live)
        elif tail_live:
            tail_live = run(tail_live)
        r_live = run(r_live)
    work_live = [work]
    while r_live or work_live:
        r_live = run(r_live)
        work_live = run(work_live)

    part[...] = jnp.zeros_like(part)
    for t in range(0, cols, 384):
        r_top, r_low = split(rall[t:t + 384, :])
        one = jnp.dot(both[:, t:t + 384], r_top, preferred_element_type=F32)
        two = jnp.dot(both[0:rows, t:t + 384], r_low, preferred_element_type=F32)
        part[...] += one[0:rows] + (one[rows:] + two)

    order = (3, 4, 2, 5, 1, 6, 0)

    def rows24(q):
        return pl.ds(pl.multiple_of(24 * q, 8), 24)

    for i in order:
        sent.append(send(part.at[rows24(zs[i])], zbuf.at[i], ssem.at[ZP + i], rsem.at[ZP + i], tensor=zs[i]))

    back = [exchange_stream(bsrc, bmid, backall_ref, s, ssem, rsem, EX + 14 + 7 * s, sent) for s in (0, 1)]
    back = run(back)

    total = part[rows24(z), :]
    for i in reversed(order):
        wait_recv(zbuf.at[i], rsem.at[ZP + i], tensor=zs[i])
        total = total + zbuf[i]
    p_ref[rows24(z), :] = total
    mine = p_ref.at[rows24(z)]
    for i in order:
        sent.append(send(mine, mine, ssem.at[ZP + 7 + i], rsem.at[ZP + 7 + i], tensor=zs[i]))
    back = run(back)
    for i in reversed(order):
        src = (z + 7 - i) % 8
        wait_recv(p_ref.at[rows24(src)], rsem.at[ZP + 7 + i], tensor=zs[i])
    gbuf[...] = lax.dot_general(
        p_ref[:, pl.ds(pl.multiple_of(128 * (z // 2), 128), 128)], p_ref[...],
        (((0,), (0,)), ((), ())), precision=HI, preferred_element_type=F32,
    )
    half = 64 * (z % 2)
    away = gbuf.at[pl.ds(pl.multiple_of(half + 32 * (1 - core), 32), 32)]
    sent.append(send(away, cbuf, ssem.at[ZP + 14], rsem.at[ZP + 14], dp=sib))
    wait_recv(cbuf, rsem.at[ZP + 14], dp=sib)
    cbuf[...] += gbuf[pl.ds(pl.multiple_of(half + 32 * core, 32), 32), :]
    for i in range(3):
        sent.append(send(
            cbuf.at[pl.ds(pl.multiple_of(8 * xs[i], 8), 8)], xbuf.at[i], ssem.at[ZP + 15 + i], rsem.at[ZP + 15 + i],
            dp=dp_of(xs[i], y, core),
        ))
    total = cbuf[pl.ds(pl.multiple_of(8 * x, 8), 8), :]
    for i in range(3):
        wait_recv(xbuf.at[i], rsem.at[ZP + 15 + i], dp=sib)
        total = total + xbuf[i]
    ybuf[y] = total
    for i in range(3):
        sent.append(send(
            ybuf.at[y], ybuf.at[y], ssem.at[ZP + 18 + i], rsem.at[ZP + 18 + i], dp=dp_of(x, ys[i], core)
        ))
    for i in range(3):
        wait_recv(ybuf.at[(y + 3 - i) % 4], rsem.at[ZP + 18 + i], dp=sib)
    gram_ref[z, core, x] = (ybuf[0] + ybuf[1]) + (ybuf[2] + ybuf[3])
    mine = gram_ref.at[z, core, x]
    for i in range(3):
        sent.append(send(mine, mine, ssem.at[ZP + 21 + i], rsem.at[ZP + 21 + i], dp=dp_of(xs[i], y, core)))
    for i in range(3):
        wait_recv(gram_ref.at[z, core, (x + 3 - i) % 4], rsem.at[ZP + 21 + i], dp=sib)
    mine = gram_ref.at[z, core]
    for i in order:
        sent.append(send(mine, mine, ssem.at[ZP + 24 + i], rsem.at[ZP + 24 + i], tensor=zs[i]))
    sent.append(send(mine, mine, ssem.at[ZP + 31], rsem.at[ZP + 31], dp=sib))
    for i in reversed(order):
        there = gram_ref.at[(z + 7 - i) % 8, core]
        wait_recv(there, rsem.at[ZP + 24 + i], tensor=zs[i])
        sent.append(send(there, there, ssem.at[ZP + 32 + i], rsem.at[ZP + 32 + i], dp=sib))
    back = run(back)
    wait_recv(gram_ref.at[z, 1 - core], rsem.at[ZP + 31], dp=sib)
    for i in reversed(order):
        wait_recv(gram_ref.at[(z + 7 - i) % 8, 1 - core], rsem.at[ZP + 32 + i], dp=sib)
    wait_recv(btsib_ref, rsem.at[OTHER + 2], dp=sib)
    for copy in sent:
        copy.wait_send()


def front(inputs, gain, out_grad, weight, moment, right_basis):
    vm = pl.BlockSpec(memory_space=pltpu.VMEM)
    rows, cols = moment.shape
    tokens = inputs.shape[0]
    return pl.pallas_call(
        front_kernel,
        out_shape=(
            jax.ShapeDtypeStruct((rows, RANK), F32),
            jax.ShapeDtypeStruct((8, 2, 4, 8, RANK), F32),
            jax.ShapeDtypeStruct((cols, 2 * rows), BF16),
            jax.ShapeDtypeStruct((cols, 2 * rows), BF16),
            jax.ShapeDtypeStruct((rows, cols), F32),
            jax.ShapeDtypeStruct((4, 4, tokens, 384), F32),
            jax.ShapeDtypeStruct((2, tokens, 384), F32),
            jax.ShapeDtypeStruct((tokens, 384), F32),
        ),
        in_specs=[vm] * 6,
        out_specs=(vm,) * 8,
        scratch_shapes=[
            pltpu.VMEM((cols, RANK), F32),
            pltpu.VMEM((2, 16 * tokens, cols), BF16),
            pltpu.VMEM((right_basis.shape[0], 256), F32),
            pltpu.VMEM((8, 2, tokens, 384), F32),
            pltpu.VMEM((4, 4, tokens, 384), BF16),
            pltpu.VMEM((2, 4, 4, 16, 384), BF16),
            pltpu.VMEM((4, 4, tokens, 384), BF16),
            pltpu.VMEM((4, 4, tokens, 384), BF16),
            pltpu.VMEM((2, rows, 16 * tokens), BF16),
            pltpu.VMEM((2 * rows, cols), BF16),
            pltpu.VMEM((2, 16 * tokens, 256), F32),
            pltpu.VMEM((16 * tokens, 256), F32),
            pltpu.VMEM((4, 4, tokens, 384), F32),
            pltpu.VMEM((2, 4, 4, 16, 384), F32),
            pltpu.VMEM((rows, RANK), F32),
            pltpu.VMEM((7, 24, RANK), F32),
            pltpu.VMEM((128, RANK), F32),
            pltpu.VMEM((32, RANK), F32),
            pltpu.VMEM((3, 8, RANK), F32),
            pltpu.VMEM((4, 8, RANK), F32),
            pltpu.SemaphoreType.DMA((OTHER + 4,)),
            pltpu.SemaphoreType.DMA((OTHER + 4,)),
        ],
        compiler_params=pltpu.CompilerParams(
            collective_id=1, has_side_effects=True, vmem_limit_bytes=VMEM_LIMIT
        ),
    )(inputs, gain, out_grad, weight, moment, right_basis)


def chol_kernel(g_ref, p_ref, o_ref, s_ref, w_ref):
    n_p = p_ref.shape[0]
    s_ref[:, 0:512] = g_ref[...]
    s_ref[:, 512:512 + n_p] = p_ref[...].T
    s_ref[:, 512 + n_p:] = jnp.zeros((512, s_ref.shape[1] - 512 - n_p), F32)
    lane = lax.broadcasted_iota(jnp.int32, (8, 128), 1)
    sub = lax.broadcasted_iota(jnp.int32, (8, 128), 0)

    def lane_splat(v, j):
        return jnp.broadcast_to(v[:, j:j + 1], (8, 128))

    def row_splat(v, i):
        return jnp.broadcast_to(v[i:i + 1, :], (8, 128))

    def block(kb, carry):
        base = pl.multiple_of(kb * 128, 128)
        tiles = [s_ref[pl.ds(pl.multiple_of(base + 8 * i, 8), 8), pl.ds(base, 128)] for i in range(16)]
        for k in range(16):
            x = tiles[k]
            inside = (lane >= 8 * k) & (lane < 8 * k + 8)
            c = [lane_splat(x, 8 * k + q) for q in range(8)]
            x = jnp.where(inside, (lane - 8 * k == sub).astype(F32), x)
            inv, up, rows = [], [], []
            scale = jnp.ones((8, 128), F32)
            for p in range(8):
                pd = row_splat(c[p], p)
                ip = 1.0 / pd
                scale = jnp.where(sub == p, lax.rsqrt(pd), scale)
                m = jnp.where(sub > p, c[p] * ip, 0.0)
                u = {}
                for q in range(p + 1, 8):
                    u[q] = row_splat(c[q], p)
                    c[q] = c[q] - (c[p] * u[q]) * ip
                r = row_splat(x, p)
                x = x - m * r
                inv.append(ip)
                up.append(u)
                rows.append(r)
            w_ref[8 * k:8 * k + 8, :] = jnp.where(lane <= sub + 8 * k, x * scale, 0.0)
            for g in range(k + 1, 16):
                v = tiles[g]
                e = [lane_splat(v, 8 * k + q) for q in range(8)]
                v = jnp.where(inside, 0.0, v)
                for p in range(8):
                    m = e[p] * inv[p]
                    for q in range(p + 1, 8):
                        e[q] = e[q] - m * up[p][q]
                    v = v - m * rows[p]
                tiles[g] = v
        rows_k = pl.ds(base, 128)
        s_ref[rows_k, :] = jnp.dot(w_ref[...], s_ref[rows_k, :], precision=HI, preferred_element_type=F32)
        for rb in range(1, 4):
            @pl.when(rb > kb)
            def _():
                ub = s_ref[rows_k, 128 * rb:128 * rb + 128]
                s_ref[128 * rb:128 * rb + 128, 128 * rb:] -= lax.dot_general(
                    ub, s_ref[rows_k, 128 * rb:], (((0,), (0,)), ((), ())), precision=HI,
                    preferred_element_type=F32,
                )
        return carry

    lax.fori_loop(0, 4, block, 0)
    o_ref[...] = s_ref[:, 512:512 + n_p].T


def chol_solve(gram, projected):
    vm = pl.BlockSpec(memory_space=pltpu.VMEM)
    return pl.pallas_call(
        chol_kernel,
        out_shape=jax.ShapeDtypeStruct(projected.shape, F32),
        in_specs=[vm, vm],
        out_specs=vm,
        scratch_shapes=[pltpu.VMEM((RANK, 768), F32), pltpu.VMEM((128, 128), F32)],
        compiler_params=pltpu.CompilerParams(vmem_limit_bytes=VMEM_LIMIT),
    )(gram, projected)


SPLIT = ((0, 96), (96, 80), (0, 176))


def coeff_kernel(bt_ref, btsib_ref, o_ref, back_ref, std_ref, gain_ref, inv_ref,
                 call_ref, cown_ref, csq_ref, ig_ref, gg_ref,
                 osib, rhs, c_ref, sbuf, rbuf, acc, s2, r2, fin, fsib, agb,
                 xsq, ysq, zsq, sqs, ngbuf, stat, gx, gy, gc, ssem, rsem, gs, gr, ns, nr):
    x, y, core, z = place()
    sib = dp_of(x, y, 1 - core)
    xs = [(x + d) % 4 for d in (1, 2, 3)]
    ys = [(y + d) % 4 for d in (1, 2, 3)]
    zs = [(z + d) % 8 for d in range(1, 8)]
    greet(
        [{"tensor": q} for q in zs]
        + [{"dp": dp_of(q, y, core)} for q in xs]
        + [{"dp": dp_of(x, q, core)} for q in ys]
        + [{"dp": sib}]
    )
    sent = []
    first = ("x", "y")

    def half(who):
        return pl.ds(pl.multiple_of(256 * who, 128), 256)

    sent.append(send(o_ref.at[:, half(1 - core)], osib, ssem.at[0], rsem.at[0], dp=sib))
    for i in range(7):
        sent.append(send(back_ref.at[zs[i]], ngbuf.at[i], ns.at[i], nr.at[i], tensor=zs[i]))

    def fill(v):
        top, low = split(v)
        n = v.shape[0]
        rhs[0:n, 0:256] = top
        rhs[n:2 * n, 0:256] = top
        rhs[0:n, 256:512] = low
        rhs[n:2 * n, 256:512] = low

    cols = bt_ref.shape[0]
    fill(o_ref[:, half(core)])
    for t in range(0, cols, 384):
        two = jnp.dot(bt_ref[t:t + 384, :], rhs[...], preferred_element_type=F32)
        c_ref[t:t + 384, :] = two[:, 0:256] + two[:, 256:512]
    wait_recv(osib, rsem.at[0], dp=sib)
    fill(osib[...])
    for t in range(0, cols, 384):
        two = jnp.dot(btsib_ref[t:t + 384, :], rhs[...], preferred_element_type=F32)
        c_ref[t:t + 384, :] += two[:, 0:256] + two[:, 256:512]

    def cols_of(who, s):
        return pl.ds(pl.multiple_of(256 * who + 128 * s, 128), 128)

    a0 = (x, y)
    b0 = (y, x)

    def own(s, off, b):
        a = (a0[s] + off) % 4
        bx, by = (a, b) if s == 0 else (b, a)
        return c_ref[pl.ds(pl.multiple_of(168 * (bx * 4 + by), 8), 168), 128 * s:128 * s + 128]

    def dev(s, a, b):
        a, b = a % 4, b % 4
        return dp_of(a, b, core) if s == 0 else dp_of(b, a, core)

    zero_pad = jnp.zeros((8, 128), F32)

    def padded(v):
        return jnp.concatenate([v, zero_pad], axis=0).astype(BF16)

    def reduce_direct(s):
        base = 8 + 6 * s
        a, b = a0[s], b0[s]
        offs = (2, 1, 3)
        for i in range(3):
            for j in range(4):
                sbuf[s, i, j] = padded(own(s, offs[i], j))
            sent.append(send(
                sbuf.at[s, i], rbuf.at[s, i], ssem.at[base + i], rsem.at[base + i], dp=dev(s, a + offs[i], b)
            ))
            yield
        for j in range(4):
            acc[s, j] = own(s, 0, j)
        for i in (1, 2, 0):
            wait_recv(rbuf.at[s, i], rsem.at[base + i], dp=sib)
        yield

        def summed(off):
            j = (b + off) % 4
            return (acc[s, j] + rbuf[s, 0, j, 0:168].astype(F32)) + (
                rbuf[s, 1, j, 0:168].astype(F32) + rbuf[s, 2, j, 0:168].astype(F32)
            )

        for i in range(3):
            s2[s, i] = padded(summed(offs[i]))
            sent.append(send(
                s2.at[s, i], r2.at[s, i], ssem.at[base + 3 + i], rsem.at[base + 3 + i], dp=dev(s, a, b + offs[i])
            ))
        yield
        total = summed(0)
        for i in (1, 2, 0):
            wait_recv(r2.at[s, i], rsem.at[base + 3 + i], dp=sib)
            total = total + r2[s, i, 0:168].astype(F32)
        fin[:, 128 * s:128 * s + 128] = total
        agb[x * 4 + y, :, cols_of(core, s)] = padded(total)
        yield

    round_robin([reduce_direct(0), reduce_direct(1)])

    def norms():
        sent.append(send(fin, fsib, ssem.at[24], rsem.at[24], dp=sib))
        v = fin[...]
        xsq[x] = jnp.broadcast_to(jnp.sum(v * v, axis=0, keepdims=True), (8, 256))
        for i in range(3):
            sent.append(send(xsq.at[x], xsq.at[x], ssem.at[25 + i], rsem.at[25 + i], dp=dp_of(xs[i], y, core)))
        yield
        for i in range(3):
            wait_recv(xsq.at[(x + 3 - i) % 4], rsem.at[25 + i], dp=sib)
        ysq[y] = (xsq[0] + xsq[1]) + (xsq[2] + xsq[3])
        for i in range(3):
            sent.append(send(ysq.at[y], ysq.at[y], ssem.at[28 + i], rsem.at[28 + i], dp=dp_of(x, ys[i], core)))
        yield
        for i in range(3):
            wait_recv(ysq.at[(y + 3 - i) % 4], rsem.at[28 + i], dp=sib)
        zsq[z] = (ysq[0] + ysq[1]) + (ysq[2] + ysq[3])
        for i in range(7):
            sent.append(send(zsq.at[z], zsq.at[z], ssem.at[31 + i], rsem.at[31 + i], tensor=zs[i]))
        yield
        for i in range(7):
            wait_recv(zsq.at[(z + 7 - i) % 8], rsem.at[31 + i], tensor=zs[i])
        total = zsq[0]
        for i in range(1, 8):
            total = total + zsq[i]
        sqs[core] = total
        sent.append(send(sqs.at[core], sqs.at[core], ssem.at[38], rsem.at[38], dp=sib))
        yield
        wait_recv(fsib, rsem.at[24], dp=sib)
        left = jnp.where(core == 0, fin[0:84], fsib[84:168])
        right = jnp.where(core == 0, fsib[0:84], fin[84:168])
        cown_ref[:, 0:256] = left
        cown_ref[:, 256:512] = right
        yield
        wait_recv(sqs.at[1 - core], rsem.at[38], dp=sib)
        csq_ref[:, 0:256] = sqs[0]
        csq_ref[:, 256:512] = sqs[1]
        yield

    def input_grad():
        total = back_ref[z]
        for i in range(7):
            wait_recv(ngbuf.at[i], nr.at[i], tensor=zs[i])
            total = total + ngbuf[i]
        std = std_ref[...]
        scaled = total * gain_ref[z]
        lane = lax.broadcasted_iota(jnp.int32, (32, 128), 1)

        def per_token(v):
            return jnp.sum(jnp.sum(v, axis=0), axis=1, keepdims=True)

        stat[z] = jnp.where(lane < 64, per_token(scaled), per_token(scaled * std))
        for i in range(7):
            sent.append(send(stat.at[z], stat.at[z], ns.at[7 + i], nr.at[7 + i], tensor=zs[i]))
        gx[x] = jnp.broadcast_to(jnp.sum(total * std, axis=1, keepdims=True), gx.shape[1:])
        for i in range(3):
            sent.append(send(gx.at[x], gx.at[x], ns.at[14 + i], nr.at[14 + i], dp=dp_of(xs[i], y, core)))
        yield
        for i in range(3):
            wait_recv(gx.at[(x + 3 - i) % 4], nr.at[14 + i], dp=sib)
        gy[y] = (gx[0] + gx[1]) + (gx[2] + gx[3])
        for i in range(3):
            sent.append(send(gy.at[y], gy.at[y], ns.at[17 + i], nr.at[17 + i], dp=dp_of(x, ys[i], core)))
        for i in range(7):
            wait_recv(stat.at[(z + 7 - i) % 8], nr.at[7 + i], tensor=zs[i])
        sums = stat[0]
        for i in range(1, 8):
            sums = sums + stat[i]
        sums = sums * (1.0 / (16 * 384))
        full = inv_ref[...] * (scaled - sums[:, 0:1] - std * sums[:, 64:65])
        ig_ref[:, 0:384] = full[0].astype(BF16)
        ig_ref[:, 384:768] = full[1].astype(BF16)
        yield
        for i in range(3):
            wait_recv(gy.at[(y + 3 - i) % 4], nr.at[17 + i], dp=sib)
        gc[core] = (gy[0] + gy[1]) + (gy[2] + gy[3])
        sent.append(send(gc.at[core], gc.at[core], ns.at[20], nr.at[20], dp=sib))
        yield
        wait_recv(gc.at[1 - core], nr.at[20], dp=sib)
        gg_ref[:, 0:384] = gc[0, 0] + gc[1, 0]
        gg_ref[:, 384:768] = gc[0, 1] + gc[1, 1]
        yield

    def loc(s):
        def at(who, bx, by, part):
            lo, rows = SPLIT[part]
            return agb.at[bx * 4 + by, pl.ds(lo, rows), cols_of(who, s)]
        return at

    round_robin([
        gather_stream(loc(0), first[0], gs, gr, 0, sent),
        gather_stream(loc(1), first[1], gs, gr, GATHER_SLOTS, sent),
        norms(),
        input_grad(),
    ])
    for j in range(8):
        two = jnp.concatenate([agb[2 * j, 0:168].astype(F32), agb[2 * j + 1, 0:168].astype(F32)], axis=0)
        call_ref[336 * j:336 * j + 336, :] = two.astype(BF16)
    for copy in sent:
        copy.wait_send()


def coeff_sum(bt, bt_sib, ortho, back, standard, gain, inv_std):
    vm = pl.BlockSpec(memory_space=pltpu.VMEM)
    block = standard.shape
    return pl.pallas_call(
        coeff_kernel,
        out_shape=(
            jax.ShapeDtypeStruct((2688, RANK), BF16),
            jax.ShapeDtypeStruct((84, RANK), F32),
            jax.ShapeDtypeStruct((8, RANK), F32),
            jax.ShapeDtypeStruct((32, 768), BF16),
            jax.ShapeDtypeStruct((8, 768), F32),
        ),
        in_specs=[vm] * 7,
        out_specs=(vm,) * 5,
        scratch_shapes=[
            pltpu.VMEM((192, 256), F32),
            pltpu.VMEM((384, RANK), BF16),
            pltpu.VMEM((2688, 256), F32),
            pltpu.VMEM((2, 3, 4, 176, 128), BF16),
            pltpu.VMEM((2, 3, 4, 176, 128), BF16),
            pltpu.VMEM((2, 4, 168, 128), F32),
            pltpu.VMEM((2, 3, 176, 128), BF16),
            pltpu.VMEM((2, 3, 176, 128), BF16),
            pltpu.VMEM((168, 256), F32),
            pltpu.VMEM((168, 256), F32),
            pltpu.VMEM((16, 176, RANK), BF16),
            pltpu.VMEM((4, 8, 256), F32),
            pltpu.VMEM((4, 8, 256), F32),
            pltpu.VMEM((8, 8, 256), F32),
            pltpu.VMEM((2, 8, 256), F32),
            pltpu.VMEM((7,) + block, F32),
            pltpu.VMEM((8, 32, 128), F32),
            pltpu.VMEM((4, 2, 8, 384), F32),
            pltpu.VMEM((4, 2, 8, 384), F32),
            pltpu.VMEM((2, 2, 8, 384), F32),
            pltpu.SemaphoreType.DMA((39,)),
            pltpu.SemaphoreType.DMA((39,)),
            pltpu.SemaphoreType.DMA((2 * GATHER_SLOTS,)),
            pltpu.SemaphoreType.DMA((2 * GATHER_SLOTS,)),
            pltpu.SemaphoreType.DMA((21,)),
            pltpu.SemaphoreType.DMA((21,)),
        ],
        compiler_params=pltpu.CompilerParams(
            collective_id=3, has_side_effects=True, vmem_limit_bytes=VMEM_LIMIT
        ),
    )(bt, bt_sib, ortho, back, standard, gain, inv_std)


def final_kernel(group, qkv_scale, mlp_scale, o_ref, csq_ref, c_ref, buf_ref, cown_ref, ig_ref, gg_ref,
                 mom_ref, upd_ref, basis_ref, igo_ref, ggo_ref, lhs):
    rows = o_ref.shape[0]
    step = pl.program_id(0)

    @pl.when(step == 0)
    def _():
        inv = 1.0 / (jnp.sqrt(csq_ref[0:1]) + 1e-08)
        o = o_ref[...]
        lhs[0:rows, :] = o.astype(BF16)
        top, low = split(o * inv)
        lhs[rows:2 * rows, :] = top
        lhs[2 * rows:3 * rows, :] = low
        basis_ref[...] = cown_ref[...] * inv
        igo_ref[...] = ig_ref[...]
        ggo_ref[...] = gg_ref[0]

    out = lax.dot_general(lhs[...], c_ref[...], (((1,), (1,)), ((), ())), preferred_element_type=F32)
    tile = out.shape[1]
    position = lax.broadcasted_iota(jnp.int32, (1, tile), 1) + step * tile
    scale = jnp.where(position < group, qkv_scale, mlp_scale)
    mom_ref[...] = buf_ref[...] - (1.0 - MOMENTUM) * out[0:rows]
    upd_ref[...] = (out[rows:2 * rows] + out[2 * rows:3 * rows]) * scale


def final_products(o, squares, coeffs, buffer, coeff_own, input_grad, gain_grad, *scales):
    rows, cols = buffer.shape
    tile = 896

    def whole(v):
        return pl.BlockSpec(v.shape, lambda i: (0,) * v.ndim)

    by_col = pl.BlockSpec((rows, tile), lambda i: (0, i))
    gain_out = jax.ShapeDtypeStruct((gain_grad.shape[1],), F32)
    return pl.pallas_call(
        lambda *refs: final_kernel(*scales, *refs),
        grid=(cols // tile,),
        out_shape=(
            jax.ShapeDtypeStruct(buffer.shape, F32),
            jax.ShapeDtypeStruct(buffer.shape, F32),
            jax.ShapeDtypeStruct(coeff_own.shape, F32),
            jax.ShapeDtypeStruct(input_grad.shape, BF16),
            gain_out,
        ),
        in_specs=[
            whole(o),
            whole(squares),
            pl.BlockSpec((tile, RANK), lambda i: (i, 0)),
            by_col,
            whole(coeff_own),
            whole(input_grad),
            whole(gain_grad),
        ],
        out_specs=(by_col, by_col, whole(coeff_own), whole(input_grad), whole(gain_out)),
        scratch_shapes=[pltpu.VMEM((3 * rows, RANK), BF16)],
        compiler_params=pltpu.CompilerParams(vmem_limit_bytes=VMEM_LIMIT),
    )(o, squares, coeffs, buffer, coeff_own, input_grad, gain_grad)


def per_device(inputs, norm_gain, out_grad, weight, moment, right_basis):
    tensor_count = lax.axis_size("tensor")
    gain = norm_gain[None, :]
    projected, gram, bt, bt_sib, buffer, back_all, standard, inv_std = front(
        inputs, gain, out_grad, weight, moment, right_basis
    )
    ortho = chol_solve(gram.reshape(RANK, RANK), projected)
    coeffs, coeff_own, squares, input_grad, gain_grad = coeff_sum(
        bt, bt_sib, ortho, back_all.reshape(tensor_count, 2, inputs.shape[0], 384),
        standard, gain.reshape(tensor_count, 2, 1, 384), inv_std,
    )
    qkv_group = 3 * HEADS * HEAD_DIM // tensor_count
    qkv_scale = 0.2 * math.sqrt(D * (3 * HEADS * HEAD_DIM) / RANK)
    mlp_scale = 0.2 * math.sqrt(D * FF / RANK)
    moment_new, update, basis_new, input_grad, gain_grad = final_products(
        ortho, squares, coeffs, buffer, coeff_own, input_grad, gain_grad, qkv_group, qkv_scale, mlp_scale
    )
    return (input_grad, gain_grad, moment_new, basis_new, update)


def solution(mesh):
    in_specs = (
        P("dp", None),
        P(),
        P("dp", "tensor"),
        P("dp", "tensor"),
        P("dp", "tensor"),
        P(("tensor", "dp"), None),
    )
    out_specs = (
        P("dp", "tensor"),
        P("tensor"),
        P("dp", "tensor"),
        P(("tensor", "dp"), None),
        P("dp", "tensor"),
    )
    return jax.shard_map(
        per_device, mesh=mesh, in_specs=in_specs, out_specs=out_specs, check_vma=False
    )
```

```python
import math

import jax
import jax.numpy as jnp
from jax import lax
from jax.experimental import pallas as pl
from jax.experimental.pallas import tpu as pltpu
from jax.sharding import PartitionSpec as P

D = 6144
HEADS = 24
HEAD_DIM = 128
FF = 12288
RANK = 512
MOMENTUM = 0.8
NORM_EPSILON = 1e-06

HI = lax.Precision.HIGHEST
MESH = pl.DeviceIdType.MESH
VMEM_LIMIT = 56 * 1024 * 1024
F32 = jnp.float32
BF16 = jnp.bfloat16


def dp_of(x, y, core):
    return (x * 4 + y) * 2 + core


def place():
    dp = lax.axis_index("dp")
    return dp // 8, (dp // 2) % 4, dp % 2, lax.axis_index("tensor")


def send(src, dst, send_sem, recv_sem, **peer):
    copy = pltpu.make_async_remote_copy(
        src_ref=src, dst_ref=dst, send_sem=send_sem, recv_sem=recv_sem,
        device_id=peer, device_id_type=MESH,
    )
    copy.start()
    return copy


def wait_recv(dst, recv_sem, **peer):
    pltpu.make_async_remote_copy(
        src_ref=dst, dst_ref=dst, send_sem=recv_sem, recv_sem=recv_sem,
        device_id=peer, device_id_type=MESH,
    ).wait_recv()


def greet(peers):
    barrier = pltpu.get_barrier_semaphore()
    for peer in peers:
        pl.semaphore_signal(barrier, inc=1, device_id=peer, device_id_type=MESH)
    pl.semaphore_wait(barrier, len(peers))


def plane_peers(x, y, core):
    return (
        [{"dp": dp_of((x + d) % 4, y, core)} for d in (1, 2, 3)]
        + [{"dp": dp_of(x, (y + d) % 4, core)} for d in (1, 2, 3)]
        + [{"dp": dp_of(x, y, 1 - core)}]
    )


def round_robin(generators):
    live = list(generators)
    while live:
        still = []
        for g in live:
            try:
                next(g)
                still.append(g)
            except StopIteration:
                pass
        live = still


def gather_stream(loc, first, ssem, rsem, base, sent):
    x0, y0, core, _ = place()
    a0, b0 = (x0, y0) if first == "x" else (y0, x0)
    sib = dp_of(x0, y0, 1 - core)

    def xy(a, b):
        return (a % 4, b % 4) if first == "x" else (b % 4, a % 4)

    def at(a, b, part, who=None):
        return loc(core if who is None else who, *xy(a, b), part)

    def to(a, b, block, part, slot):
        ref = at(*block, part)
        sent.append(send(ref, ref, ssem.at[base + slot], rsem.at[base + slot], dp=dp_of(*xy(a, b), core)))

    def got(block, part, slot):
        wait_recv(at(*block, part), rsem.at[base + slot], dp=sib)

    def share(block, slot):
        ref = at(*block, 2)
        sent.append(send(ref, ref, ssem.at[base + slot], rsem.at[base + slot], dp=sib))

    def spread(k, block):
        to(a0, b0 + 1, block, 2, 4 + 4 * k)
        to(a0, b0 - 1, block, 2, 5 + 4 * k)

    offs = (0, -1, 1, 2)
    to(a0 + 1, b0, (a0, b0), 2, 0)
    to(a0 - 1, b0, (a0, b0), 2, 1)
    yield
    spread(0, (a0, b0))
    share((a0, b0), 20)
    yield
    got((a0 - 1, b0), 2, 0)
    to(a0 + 1, b0, (a0 - 1, b0), 0, 2)
    got((a0 + 1, b0), 2, 1)
    to(a0 - 1, b0, (a0 + 1, b0), 1, 3)
    spread(1, (a0 - 1, b0))
    spread(2, (a0 + 1, b0))
    yield
    share((a0 - 1, b0), 21)
    share((a0 + 1, b0), 22)
    got((a0 + 2, b0), 0, 2)
    got((a0 + 2, b0), 1, 3)
    spread(3, (a0 + 2, b0))
    share((a0 + 2, b0), 23)
    yield
    for k in range(4):
        a = a0 + offs[k]
        got((a, b0 - 1), 2, 4 + 4 * k)
        to(a0, b0 + 1, (a, b0 - 1), 0, 6 + 4 * k)
        got((a, b0 + 1), 2, 5 + 4 * k)
        to(a0, b0 - 1, (a, b0 + 1), 1, 7 + 4 * k)
        share((a, b0 - 1), 24 + 3 * k)
        share((a, b0 + 1), 25 + 3 * k)
        yield
    for k in range(4):
        a = a0 + offs[k]
        got((a, b0 + 2), 0, 6 + 4 * k)
        got((a, b0 + 2), 1, 7 + 4 * k)
        share((a, b0 + 2), 26 + 3 * k)
        yield
    for k in range(4):
        a = a0 + offs[k]
        wait_recv(at(a, b0, 2, 1 - core), rsem.at[base + 20 + k], dp=sib)
        for j, b in enumerate((b0 - 1, b0 + 1, b0 + 2)):
            wait_recv(at(a, b, 2, 1 - core), rsem.at[base + 24 + 3 * k + j], dp=sib)
    yield


GATHER_SLOTS = 36
EXCHANGE_SLOTS = 6


def exchange_stream(src, mid, out, s, ssem, rsem, base, sent):
    x, y, core, _ = place()
    sib = dp_of(x, y, 1 - core)
    half = slice(16 * s, 16 * s + 16)

    def part(ref, a):
        return ref.at[a, :, half] if s == 0 else ref.at[:, a, half]

    def swapped(ref, b):
        return ref.at[:, b, half] if s == 0 else ref.at[b, :, half]

    a0, b0 = (x, y) if s == 0 else (y, x)

    def dev(a, b):
        return dp_of(a, b, core) if s == 0 else dp_of(b, a, core)

    mine = pltpu.make_async_copy(part(src, a0), mid.at[s, a0], ssem.at[base + 6])
    mine.start()
    for i in range(3):
        to = (a0 + 1 + i) % 4
        sent.append(send(part(src, to), mid.at[s, a0], ssem.at[base + i], rsem.at[base + i], dp=dev(to, b0)))
    yield
    for i in range(3):
        wait_recv(mid.at[s, (a0 + 3 - i) % 4], rsem.at[base + i], dp=sib)
    mine.wait()
    own = pltpu.make_async_copy(mid.at[s, :, b0], swapped(out, b0), ssem.at[base + 6])
    own.start()
    for i in range(3):
        to = (b0 + 1 + i) % 4
        sent.append(send(
            mid.at[s, :, to], swapped(out, b0), ssem.at[base + 3 + i], rsem.at[base + 3 + i], dp=dev(a0, to)
        ))
    yield
    own.wait()
    for i in range(3):
        wait_recv(swapped(out, (b0 + 3 - i) % 4), rsem.at[base + 3 + i], dp=sib)
    yield


def split(v):
    top = v.astype(BF16)
    return top, (v - top.astype(F32)).astype(BF16)


EX = 4 * GATHER_SLOTS
ZP = EX + 28
OTHER = ZP + 35


def front_steps(sent, in_ref, gain_ref, g_ref, w_ref, m_ref, r_ref,
                p_ref, gram_ref, bt_ref, btsib_ref, buf_ref, backall_ref, std_ref, inv_ref,
                rall, gall, got, std, nrm, exmid, exout, exsib, xt, both, bk, bksib, bsrc, bmid,
                part, zbuf, gbuf, cbuf, xbuf, ybuf, ssem, rsem):
    x, y, core, z = place()
    chip = x * 4 + y
    sib = dp_of(x, y, 1 - core)
    xs = [(x + d) % 4 for d in (1, 2, 3)]
    ys = [(y + d) % 4 for d in (1, 2, 3)]
    zs = [(z + d) % 8 for d in range(1, 8)]
    rows, cols = m_ref.shape
    tokens, width = in_ref.shape
    cut = 1408

    other = pl.multiple_of(256 * (1 - core), 128)
    sent.append(send(r_ref.at[:, pl.ds(other, 256)], got, ssem.at[OTHER], rsem.at[OTHER], dp=sib))
    gall[core, pl.ds(pl.multiple_of(32 * chip, 32), 32)] = g_ref[...]

    def loc_g(s):
        def loc(who, bx, by, part):
            lo, n = ((0, cut), (cut, cols - cut), (0, cols))[part]
            return gall.at[who, pl.ds(pl.multiple_of(32 * (bx * 4 + by) + 16 * s, 16), 16), pl.ds(lo, n)]
        return loc

    def loc_r(s):
        def loc(who, bx, by, part):
            lo, n = ((0, 88), (88, 80), (0, 168))[part]
            row = pl.multiple_of((bx * 4 + by) * 168 + lo, 8)
            return rall.at[pl.ds(row, n), pl.ds(pl.multiple_of(256 * who + 128 * s, 128), 128)]
        return loc

    g_streams = [gather_stream(loc_g(s), "xy"[s], ssem, rsem, (2 + s) * GATHER_SLOTS, sent) for s in (0, 1)]
    for g in g_streams:
        next(g)
    for g in g_streams:
        next(g)

    wide = [in_ref[:, 384 * b:384 * b + 384].astype(F32) for b in range(16)]
    mean = sum(jnp.sum(v, axis=1, keepdims=True) for v in wide) * (1.0 / width)
    centered = [in_ref[:, 384 * b:384 * b + 384].astype(F32) - mean for b in range(16)]
    var = sum(jnp.sum(v * v, axis=1, keepdims=True) for v in centered) * (1.0 / width)
    inv = lax.rsqrt(var + NORM_EPSILON)
    inv_ref[...] = jnp.broadcast_to(inv, inv_ref.shape)
    for b in range(16):
        v = (in_ref[:, 384 * b:384 * b + 384].astype(F32) - mean) * inv
        std[b // 2, b % 2] = v
        nrm[b // 4, b % 4] = (v * gain_ref[:, 384 * b:384 * b + 384]).astype(BF16)
    std_ref[...] = std[z]
    ex = [exchange_stream(nrm, exmid, exout, s, ssem, rsem, EX + 7 * s, sent) for s in (0, 1)]
    for g in ex:
        next(g)

    wait_recv(got, rsem.at[OTHER], dp=sib)
    mine = r_ref[:, pl.ds(pl.multiple_of(256 * core, 128), 256)]
    theirs = got[...]
    rall[pl.ds(pl.multiple_of(chip * 168, 8), 168), pl.ds(pl.multiple_of(256 * core, 128), 256)] = jnp.concatenate(
        [jnp.where(core == 0, mine, theirs), jnp.where(core == 0, theirs, mine)], axis=0
    )
    r_streams = [gather_stream(loc_r(s), "xy"[s], ssem, rsem, s * GATHER_SLOTS, sent) for s in (0, 1)]

    def run(gens):
        live = []
        for g in gens:
            try:
                next(g)
                live.append(g)
            except StopIteration:
                pass
        return live

    def mine192(v):
        return jnp.where(core == 0, v[:, 0:192].astype(F32), v[:, 192:384].astype(F32))

    def after_exchange():
        sent.append(send(exout, exsib, ssem.at[OTHER + 1], rsem.at[OTHER + 1], dp=sib))
        for q in range(4):
            v = exout[q].reshape(4 * tokens, 384)
            xt[core, :, 128 * q:128 * q + 128] = mine192(v).T.astype(BF16)
        yield
        wait_recv(exsib, rsem.at[OTHER + 1], dp=sib)
        for q in range(4):
            v = exsib[q].reshape(4 * tokens, 384)
            xt[1 - core, :, 128 * q:128 * q + 128] = mine192(v).T.astype(BF16)
        yield

    def compute():
        for t in range(0, cols, 384):
            acc = m_ref[:, t:t + 384]
            for c in (0, 1):
                acc = acc + jnp.dot(xt[c], gall[c, :, t:t + 384], preferred_element_type=F32)
            buf_ref[:, t:t + 384] = acc
            top, low = split(acc)
            both[0:rows, t:t + 384] = top
            both[rows:2 * rows, t:t + 384] = low
            yield

    bk[:, :, 128:256] = jnp.zeros((2, 512, 128), F32)
    tail = after_exchange()
    work = compute()
    r_live, g_live, x_live = r_streams, g_streams, ex
    r_live = run(r_live)
    tail_live = [tail]
    while g_live or x_live or tail_live:
        g_live = run(g_live)
        if x_live:
            x_live = run(x_live)
        elif tail_live:
            tail_live = run(tail_live)
        r_live = run(r_live)
    work_live = [work]
    while r_live or work_live:
        r_live = run(r_live)
        work_live = run(work_live)

    part[...] = jnp.zeros_like(part)
    for t in range(0, cols, 384):
        r_top, r_low = split(rall[t:t + 384, :])
        one = jnp.dot(both[:, t:t + 384], r_top, preferred_element_type=F32)
        two = jnp.dot(both[0:rows, t:t + 384], r_low, preferred_element_type=F32)
        part[...] += one[0:rows] + (one[rows:] + two)

    order = (3, 4, 2, 5, 1, 6, 0)

    def rows24(q):
        return pl.ds(pl.multiple_of(24 * q, 8), 24)

    for i in order:
        sent.append(send(part.at[rows24(zs[i])], zbuf.at[i], ssem.at[ZP + i], rsem.at[ZP + i], tensor=zs[i]))

    for c in (0, 1):
        for q in (0, 256):
            bk[c, q:q + 256, 0:192] = lax.dot_general(
                gall[c, q:q + 256, :], w_ref[...], (((1,), (1,)), ((), ())), preferred_element_type=F32
            )
    sent.append(send(bk.at[1 - core], bksib, ssem.at[OTHER + 3], rsem.at[OTHER + 3], dp=sib))
    for t in range(0, cols, 384):
        bt_ref[t:t + 384, :] = both[:, t:t + 384].astype(F32).T.astype(BF16)
    wait_recv(bksib, rsem.at[OTHER + 3], dp=sib)
    for q in range(4):
        ours = bk[core, 128 * q:128 * q + 128, 0:192]
        their = bksib[128 * q:128 * q + 128, 0:192]
        bsrc[q] = jnp.concatenate(
            [jnp.where(core == 0, ours, their), jnp.where(core == 0, their, ours)], axis=1
        ).reshape(4, tokens, 384)
    sent.append(send(bt_ref, btsib_ref, ssem.at[OTHER + 2], rsem.at[OTHER + 2], dp=sib))
    back = [exchange_stream(bsrc, bmid, backall_ref, s, ssem, rsem, EX + 14 + 7 * s, sent) for s in (0, 1)]
    back = run(back)

    total = part[rows24(z), :]
    for i in reversed(order):
        wait_recv(zbuf.at[i], rsem.at[ZP + i], tensor=zs[i])
        total = total + zbuf[i]
    p_ref[rows24(z), :] = total
    mine = p_ref.at[rows24(z)]
    for i in order:
        sent.append(send(mine, mine, ssem.at[ZP + 7 + i], rsem.at[ZP + 7 + i], tensor=zs[i]))
    back = run(back)
    for i in reversed(order):
        src = (z + 7 - i) % 8
        wait_recv(p_ref.at[rows24(src)], rsem.at[ZP + 7 + i], tensor=zs[i])
    gbuf[...] = lax.dot_general(
        p_ref[:, pl.ds(pl.multiple_of(128 * (z // 2), 128), 128)], p_ref[...],
        (((0,), (0,)), ((), ())), precision=HI, preferred_element_type=F32,
    )
    half = 64 * (z % 2)
    away = gbuf.at[pl.ds(pl.multiple_of(half + 32 * (1 - core), 32), 32)]
    sent.append(send(away, cbuf, ssem.at[ZP + 14], rsem.at[ZP + 14], dp=sib))
    wait_recv(cbuf, rsem.at[ZP + 14], dp=sib)
    cbuf[...] += gbuf[pl.ds(pl.multiple_of(half + 32 * core, 32), 32), :]
    for i in range(3):
        sent.append(send(
            cbuf.at[pl.ds(pl.multiple_of(8 * xs[i], 8), 8)], xbuf.at[i], ssem.at[ZP + 15 + i], rsem.at[ZP + 15 + i],
            dp=dp_of(xs[i], y, core),
        ))
    total = cbuf[pl.ds(pl.multiple_of(8 * x, 8), 8), :]
    for i in range(3):
        wait_recv(xbuf.at[i], rsem.at[ZP + 15 + i], dp=sib)
        total = total + xbuf[i]
    ybuf[y] = total
    for i in range(3):
        sent.append(send(
            ybuf.at[y], ybuf.at[y], ssem.at[ZP + 18 + i], rsem.at[ZP + 18 + i], dp=dp_of(x, ys[i], core)
        ))
    for i in range(3):
        wait_recv(ybuf.at[(y + 3 - i) % 4], rsem.at[ZP + 18 + i], dp=sib)
    gram_ref[z, core, x] = (ybuf[0] + ybuf[1]) + (ybuf[2] + ybuf[3])
    mine = gram_ref.at[z, core, x]
    for i in order:
        sent.append(send(mine, mine, ssem.at[ZP + 21 + i], rsem.at[ZP + 21 + i], tensor=zs[i]))
    back = run(back)
    for i in reversed(order):
        wait_recv(gram_ref.at[(z + 7 - i) % 8, core, x], rsem.at[ZP + 21 + i], tensor=zs[i])
    mine = gram_ref.at[:, core, x]
    for i in range(3):
        sent.append(send(mine, mine, ssem.at[ZP + 28 + i], rsem.at[ZP + 28 + i], dp=dp_of(xs[i], y, core)))
    sent.append(send(mine, mine, ssem.at[ZP + 31], rsem.at[ZP + 31], dp=sib))
    for i in range(3):
        src = (x + 3 - i) % 4
        there = gram_ref.at[:, core, src]
        wait_recv(there, rsem.at[ZP + 28 + i], dp=sib)
        sent.append(send(there, there, ssem.at[ZP + 32 + i], rsem.at[ZP + 32 + i], dp=sib))
    wait_recv(gram_ref.at[:, 1 - core, x], rsem.at[ZP + 31], dp=sib)
    for i in range(3):
        wait_recv(gram_ref.at[:, 1 - core, (x + 3 - i) % 4], rsem.at[ZP + 32 + i], dp=sib)
    wait_recv(btsib_ref, rsem.at[OTHER + 2], dp=sib)


def chol_steps(g_ref, p_ref, o_ref, s_ref, w_ref):
    n_p = p_ref.shape[0]
    s_ref[:, 0:512] = g_ref[...].reshape(512, 512)
    s_ref[:, 512:512 + n_p] = p_ref[...].T
    s_ref[:, 512 + n_p:] = jnp.zeros((512, s_ref.shape[1] - 512 - n_p), F32)
    lane = lax.broadcasted_iota(jnp.int32, (8, 128), 1)
    sub = lax.broadcasted_iota(jnp.int32, (8, 128), 0)

    def lane_splat(v, j):
        return jnp.broadcast_to(v[:, j:j + 1], (8, 128))

    def row_splat(v, i):
        return jnp.broadcast_to(v[i:i + 1, :], (8, 128))

    def block(kb, carry):
        base = pl.multiple_of(kb * 128, 128)
        rest = s_ref[pl.ds(base, 128), pl.ds(base, 128)]
        for k in range(16):
            x = rest[0:8]
            below = rest[8:]
            inside = (lane >= 8 * k) & (lane < 8 * k + 8)
            c = [lane_splat(x, 8 * k + q) for q in range(8)]
            x = jnp.where(inside, (lane - 8 * k == sub).astype(F32), x)
            inv, up, rows = [], [], []
            scale = jnp.ones((8, 128), F32)
            for p in range(8):
                pd = row_splat(c[p], p)
                ip = 1.0 / pd
                scale = jnp.where(sub == p, lax.rsqrt(pd), scale)
                m = jnp.where(sub > p, c[p] * ip, 0.0)
                u = {}
                for q in range(p + 1, 8):
                    u[q] = c[q][p:p + 1]
                    c[q] = c[q] - (c[p] * row_splat(c[q], p)) * ip
                r = x[p:p + 1]
                x = x - m * r
                inv.append(ip[0:1])
                up.append(u)
                rows.append(r)
            w_ref[8 * k:8 * k + 8, :] = jnp.where(lane <= sub + 8 * k, x * scale, 0.0)
            if k < 15:
                n = below.shape[0]
                e = [jnp.broadcast_to(below[:, 8 * k + q:8 * k + q + 1], (n, 128)) for q in range(8)]
                below = jnp.where(inside[0:1], 0.0, below)
                for p in range(8):
                    m = e[p] * inv[p]
                    for q in range(p + 1, 8):
                        e[q] = e[q] - m * up[p][q]
                    below = below - m * rows[p]
                rest = below
        rows_k = pl.ds(base, 128)
        s_ref[rows_k, :] = jnp.dot(w_ref[...], s_ref[rows_k, :], precision=HI, preferred_element_type=F32)
        for rb in range(1, 4):
            @pl.when(rb > kb)
            def _():
                ub = s_ref[rows_k, 128 * rb:128 * rb + 128]
                s_ref[128 * rb:128 * rb + 128, 128 * rb:] -= lax.dot_general(
                    ub, s_ref[rows_k, 128 * rb:], (((0,), (0,)), ((), ())), precision=HI,
                    preferred_element_type=F32,
                )
        return carry

    lax.fori_loop(0, 4, block, 0)
    o_ref[...] = s_ref[:, 512:512 + n_p].T


SPLIT = ((0, 96), (96, 80), (0, 176))


def coeff_steps(sent, bt_ref, btsib_ref, o_ref, back_ref, std_ref, gain_ref, inv_ref,
                call_ref, cown_ref, csq_ref, ig_ref, gg_ref,
                osib, rhs, c_ref, sbuf, rbuf, acc, s2, r2, fin, fsib, agb,
                xsq, ysq, zsq, sqs, ngbuf, stat, gx, gy, gc, ssem, rsem, gs, gr, ns, nr):
    x, y, core, z = place()
    sib = dp_of(x, y, 1 - core)
    xs = [(x + d) % 4 for d in (1, 2, 3)]
    ys = [(y + d) % 4 for d in (1, 2, 3)]
    zs = [(z + d) % 8 for d in range(1, 8)]
    first = ("x", "y")

    def half(who):
        return pl.ds(pl.multiple_of(256 * who, 128), 256)

    sent.append(send(o_ref.at[:, half(1 - core)], osib, ssem.at[0], rsem.at[0], dp=sib))
    for i in range(7):
        sent.append(send(back_ref.at[zs[i] // 2, pl.ds(2 * (zs[i] % 2), 2)], ngbuf.at[i], ns.at[i], nr.at[i], tensor=zs[i]))

    def fill(v):
        top, low = split(v)
        n = v.shape[0]
        rhs[0:n, 0:256] = top
        rhs[n:2 * n, 0:256] = top
        rhs[0:n, 256:512] = low
        rhs[n:2 * n, 256:512] = low

    cols = bt_ref.shape[0]
    fill(o_ref[:, half(core)])
    for t in range(0, cols, 384):
        two = jnp.dot(bt_ref[t:t + 384, :], rhs[...], preferred_element_type=F32)
        c_ref[t:t + 384, :] = two[:, 0:256] + two[:, 256:512]
    wait_recv(osib, rsem.at[0], dp=sib)
    fill(osib[...])
    for t in range(0, cols, 384):
        two = jnp.dot(btsib_ref[t:t + 384, :], rhs[...], preferred_element_type=F32)
        c_ref[t:t + 384, :] += two[:, 0:256] + two[:, 256:512]

    def cols_of(who, s):
        return pl.ds(pl.multiple_of(256 * who + 128 * s, 128), 128)

    a0 = (x, y)
    b0 = (y, x)

    def own(s, off, b):
        a = (a0[s] + off) % 4
        bx, by = (a, b) if s == 0 else (b, a)
        return c_ref[pl.ds(pl.multiple_of(168 * (bx * 4 + by), 8), 168), 128 * s:128 * s + 128]

    def dev(s, a, b):
        a, b = a % 4, b % 4
        return dp_of(a, b, core) if s == 0 else dp_of(b, a, core)

    zero_pad = jnp.zeros((8, 128), F32)

    def padded(v):
        return jnp.concatenate([v, zero_pad], axis=0).astype(BF16)

    def reduce_direct(s):
        base = 8 + 6 * s
        a, b = a0[s], b0[s]
        offs = (2, 1, 3)
        for i in range(3):
            for j in range(4):
                sbuf[s, i, j] = padded(own(s, offs[i], j))
            sent.append(send(
                sbuf.at[s, i], rbuf.at[s, i], ssem.at[base + i], rsem.at[base + i], dp=dev(s, a + offs[i], b)
            ))
            yield
        for j in range(4):
            acc[s, j] = own(s, 0, j)
        for i in (1, 2, 0):
            wait_recv(rbuf.at[s, i], rsem.at[base + i], dp=sib)
        yield

        def summed(off):
            j = (b + off) % 4
            return (acc[s, j] + rbuf[s, 0, j, 0:168].astype(F32)) + (
                rbuf[s, 1, j, 0:168].astype(F32) + rbuf[s, 2, j, 0:168].astype(F32)
            )

        for i in range(3):
            s2[s, i] = padded(summed(offs[i]))
            sent.append(send(
                s2.at[s, i], r2.at[s, i], ssem.at[base + 3 + i], rsem.at[base + 3 + i], dp=dev(s, a, b + offs[i])
            ))
        yield
        total = summed(0)
        for i in (1, 2, 0):
            wait_recv(r2.at[s, i], rsem.at[base + 3 + i], dp=sib)
            total = total + r2[s, i, 0:168].astype(F32)
        fin[:, 128 * s:128 * s + 128] = total
        agb[x * 4 + y, :, cols_of(core, s)] = padded(total)
        yield

    round_robin([reduce_direct(0), reduce_direct(1)])

    def norms():
        sent.append(send(fin, fsib, ssem.at[24], rsem.at[24], dp=sib))
        v = fin[...]
        xsq[x] = jnp.broadcast_to(jnp.sum(v * v, axis=0, keepdims=True), (8, 256))
        for i in range(3):
            sent.append(send(xsq.at[x], xsq.at[x], ssem.at[25 + i], rsem.at[25 + i], dp=dp_of(xs[i], y, core)))
        yield
        for i in range(3):
            wait_recv(xsq.at[(x + 3 - i) % 4], rsem.at[25 + i], dp=sib)
        ysq[y] = (xsq[0] + xsq[1]) + (xsq[2] + xsq[3])
        for i in range(3):
            sent.append(send(ysq.at[y], ysq.at[y], ssem.at[28 + i], rsem.at[28 + i], dp=dp_of(x, ys[i], core)))
        yield
        for i in range(3):
            wait_recv(ysq.at[(y + 3 - i) % 4], rsem.at[28 + i], dp=sib)
        zsq[z] = (ysq[0] + ysq[1]) + (ysq[2] + ysq[3])
        for i in range(7):
            sent.append(send(zsq.at[z], zsq.at[z], ssem.at[31 + i], rsem.at[31 + i], tensor=zs[i]))
        yield
        for i in range(7):
            wait_recv(zsq.at[(z + 7 - i) % 8], rsem.at[31 + i], tensor=zs[i])
        total = zsq[0]
        for i in range(1, 8):
            total = total + zsq[i]
        sqs[core] = total
        sent.append(send(sqs.at[core], sqs.at[core], ssem.at[38], rsem.at[38], dp=sib))
        yield
        wait_recv(fsib, rsem.at[24], dp=sib)
        left = jnp.where(core == 0, fin[0:84], fsib[84:168])
        right = jnp.where(core == 0, fsib[0:84], fin[84:168])
        cown_ref[:, 0:256] = left
        cown_ref[:, 256:512] = right
        yield
        wait_recv(sqs.at[1 - core], rsem.at[38], dp=sib)
        csq_ref[:, 0:256] = sqs[0]
        csq_ref[:, 256:512] = sqs[1]
        yield

    def input_grad():
        total = back_ref[z // 2, pl.ds(2 * (z % 2), 2)]
        for i in range(7):
            wait_recv(ngbuf.at[i], nr.at[i], tensor=zs[i])
            total = total + ngbuf[i]
        std = std_ref[...]
        gain = gain_ref[:, pl.ds(pl.multiple_of(768 * z, 128), 768)]
        scaled = total * jnp.stack([gain[:, 0:384], gain[:, 384:768]])
        lane = lax.broadcasted_iota(jnp.int32, (32, 128), 1)

        def per_token(v):
            return jnp.sum(jnp.sum(v, axis=0), axis=1, keepdims=True)

        stat[z] = jnp.where(lane < 64, per_token(scaled), per_token(scaled * std))
        for i in range(7):
            sent.append(send(stat.at[z], stat.at[z], ns.at[7 + i], nr.at[7 + i], tensor=zs[i]))
        gx[x] = jnp.broadcast_to(jnp.sum(total * std, axis=1, keepdims=True), gx.shape[1:])
        for i in range(3):
            sent.append(send(gx.at[x], gx.at[x], ns.at[14 + i], nr.at[14 + i], dp=dp_of(xs[i], y, core)))
        yield
        for i in range(3):
            wait_recv(gx.at[(x + 3 - i) % 4], nr.at[14 + i], dp=sib)
        gy[y] = (gx[0] + gx[1]) + (gx[2] + gx[3])
        for i in range(3):
            sent.append(send(gy.at[y], gy.at[y], ns.at[17 + i], nr.at[17 + i], dp=dp_of(x, ys[i], core)))
        for i in range(7):
            wait_recv(stat.at[(z + 7 - i) % 8], nr.at[7 + i], tensor=zs[i])
        sums = stat[0]
        for i in range(1, 8):
            sums = sums + stat[i]
        sums = sums * (1.0 / (16 * 384))
        full = inv_ref[...] * (scaled - sums[:, 0:1] - std * sums[:, 64:65])
        ig_ref[:, 0:384] = full[0].astype(BF16)
        ig_ref[:, 384:768] = full[1].astype(BF16)
        yield
        for i in range(3):
            wait_recv(gy.at[(y + 3 - i) % 4], nr.at[17 + i], dp=sib)
        gc[core] = (gy[0] + gy[1]) + (gy[2] + gy[3])
        sent.append(send(gc.at[core], gc.at[core], ns.at[20], nr.at[20], dp=sib))
        yield
        wait_recv(gc.at[1 - core], nr.at[20], dp=sib)
        gg_ref[:, 0:384] = gc[0, 0] + gc[1, 0]
        gg_ref[:, 384:768] = gc[0, 1] + gc[1, 1]
        yield

    def loc(s):
        def at(who, bx, by, part):
            lo, rows = SPLIT[part]
            return agb.at[bx * 4 + by, pl.ds(lo, rows), cols_of(who, s)]
        return at

    round_robin([
        gather_stream(loc(0), first[0], gs, gr, 0, sent),
        gather_stream(loc(1), first[1], gs, gr, GATHER_SLOTS, sent),
        norms(),
        input_grad(),
    ])
    for j in range(8):
        two = jnp.concatenate([agb[2 * j, 0:168].astype(F32), agb[2 * j + 1, 0:168].astype(F32)], axis=0)
        call_ref[336 * j:336 * j + 336, :] = two.astype(BF16)


def whole_kernel(*refs):
    ins, refs = refs[:6], refs[6:]
    buf, ortho, call, cown, csq, ig, gg = refs[:7]
    refs = refs[7:]
    front_scratch, refs = refs[:29], refs[29:]
    s_scr, w_scr, refs = refs[0], refs[1], refs[2:]
    p, gram, bt, btsib, backall, stdz, inv = front_scratch[:7]
    x, y, core, z = place()
    greet([{"tensor": (z + d) % 8} for d in range(1, 8)] + plane_peers(x, y, core))
    sent = []
    front_steps(sent, *ins, p, gram, bt, btsib, buf, backall, stdz, inv, *front_scratch[7:])
    chol_steps(gram, p, ortho, s_scr, w_scr)
    coeff_steps(sent, bt, btsib, ortho, backall, stdz, ins[1], inv, call, cown, csq, ig, gg, *refs)
    for copy in sent:
        copy.wait_send()


def whole(inputs, gain, out_grad, weight, moment, right_basis):
    vm = pl.BlockSpec(memory_space=pltpu.VMEM)
    rows, cols = moment.shape
    tokens = inputs.shape[0]
    block = (2, tokens, 384)

    def f32(*shape):
        return pltpu.VMEM(shape, F32)

    def bf16(*shape):
        return pltpu.VMEM(shape, BF16)

    dma = pltpu.SemaphoreType.DMA
    front_scratch = [
        f32(rows, RANK),
        f32(8, 2, 4, 8, RANK),
        bf16(cols, 2 * rows),
        bf16(cols, 2 * rows),
        f32(4, 4, tokens, 384),
        f32(*block),
        f32(tokens, 384),
        f32(cols, RANK),
        bf16(2, 16 * tokens, cols),
        f32(right_basis.shape[0], 256),
        f32(8, 2, tokens, 384),
        bf16(4, 4, tokens, 384),
        bf16(2, 4, 4, 16, 384),
        bf16(4, 4, tokens, 384),
        bf16(4, 4, tokens, 384),
        bf16(2, rows, 16 * tokens),
        bf16(2 * rows, cols),
        f32(2, 16 * tokens, 256),
        f32(16 * tokens, 256),
        f32(4, 4, tokens, 384),
        f32(2, 4, 4, 16, 384),
        f32(rows, RANK),
        f32(7, 24, RANK),
        f32(128, RANK),
        f32(32, RANK),
        f32(3, 8, RANK),
        f32(4, 8, RANK),
        dma((OTHER + 4,)),
        dma((OTHER + 4,)),
    ]
    chol_scratch = [f32(RANK, 768), f32(128, 128)]
    coeff_scratch = [
        f32(192, 256),
        bf16(384, RANK),
        f32(2688, 256),
        bf16(2, 3, 4, 176, 128),
        bf16(2, 3, 4, 176, 128),
        f32(2, 4, 168, 128),
        bf16(2, 3, 176, 128),
        bf16(2, 3, 176, 128),
        f32(168, 256),
        f32(168, 256),
        bf16(16, 176, RANK),
        f32(4, 8, 256),
        f32(4, 8, 256),
        f32(8, 8, 256),
        f32(2, 8, 256),
        f32(7, *block),
        f32(8, 32, 128),
        f32(4, 2, 8, 384),
        f32(4, 2, 8, 384),
        f32(2, 2, 8, 384),
        dma((39,)),
        dma((39,)),
        dma((2 * GATHER_SLOTS,)),
        dma((2 * GATHER_SLOTS,)),
        dma((21,)),
        dma((21,)),
    ]
    return pl.pallas_call(
        whole_kernel,
        out_shape=(
            jax.ShapeDtypeStruct((rows, cols), F32),
            jax.ShapeDtypeStruct((rows, RANK), F32),
            jax.ShapeDtypeStruct((cols, RANK), BF16),
            jax.ShapeDtypeStruct((84, RANK), F32),
            jax.ShapeDtypeStruct((8, RANK), F32),
            jax.ShapeDtypeStruct((tokens, 768), BF16),
            jax.ShapeDtypeStruct((8, 768), F32),
        ),
        in_specs=[vm] * 6,
        out_specs=(vm,) * 7,
        scratch_shapes=front_scratch + chol_scratch + coeff_scratch,
        compiler_params=pltpu.CompilerParams(
            collective_id=1, has_side_effects=True, vmem_limit_bytes=VMEM_LIMIT
        ),
    )(inputs, gain, out_grad, weight, moment, right_basis)


def final_kernel(group, qkv_scale, mlp_scale, o_ref, csq_ref, c_ref, buf_ref, cown_ref, ig_ref, gg_ref,
                 mom_ref, upd_ref, basis_ref, igo_ref, ggo_ref, lhs):
    rows = o_ref.shape[0]
    step = pl.program_id(0)

    @pl.when(step == 0)
    def _():
        inv = 1.0 / (jnp.sqrt(csq_ref[0:1]) + 1e-08)
        o = o_ref[...]
        lhs[0:rows, :] = o.astype(BF16)
        top, low = split(o * inv)
        lhs[rows:2 * rows, :] = top
        lhs[2 * rows:3 * rows, :] = low
        basis_ref[...] = cown_ref[...] * inv
        igo_ref[...] = ig_ref[...]
        ggo_ref[...] = gg_ref[0]

    out = lax.dot_general(lhs[...], c_ref[...], (((1,), (1,)), ((), ())), preferred_element_type=F32)
    tile = out.shape[1]
    position = lax.broadcasted_iota(jnp.int32, (1, tile), 1) + step * tile
    scale = jnp.where(position < group, qkv_scale, mlp_scale)
    mom_ref[...] = buf_ref[...] - (1.0 - MOMENTUM) * out[0:rows]
    upd_ref[...] = (out[rows:2 * rows] + out[2 * rows:3 * rows]) * scale


def final_products(o, squares, coeffs, buffer, coeff_own, input_grad, gain_grad, *scales):
    rows, cols = buffer.shape
    tile = 896

    def all_of(v):
        return pl.BlockSpec(v.shape, lambda i: (0,) * v.ndim)

    by_col = pl.BlockSpec((rows, tile), lambda i: (0, i))
    gain_out = jax.ShapeDtypeStruct((gain_grad.shape[1],), F32)
    return pl.pallas_call(
        lambda *refs: final_kernel(*scales, *refs),
        grid=(cols // tile,),
        out_shape=(
            jax.ShapeDtypeStruct(buffer.shape, F32),
            jax.ShapeDtypeStruct(buffer.shape, F32),
            jax.ShapeDtypeStruct(coeff_own.shape, F32),
            jax.ShapeDtypeStruct(input_grad.shape, BF16),
            gain_out,
        ),
        in_specs=[
            all_of(o),
            all_of(squares),
            pl.BlockSpec((tile, RANK), lambda i: (i, 0)),
            by_col,
            all_of(coeff_own),
            all_of(input_grad),
            all_of(gain_grad),
        ],
        out_specs=(by_col, by_col, all_of(coeff_own), all_of(input_grad), all_of(gain_out)),
        scratch_shapes=[pltpu.VMEM((3 * rows, RANK), BF16)],
        compiler_params=pltpu.CompilerParams(vmem_limit_bytes=VMEM_LIMIT),
    )(o, squares, coeffs, buffer, coeff_own, input_grad, gain_grad)


def per_device(inputs, norm_gain, out_grad, weight, moment, right_basis):
    tensor_count = lax.axis_size("tensor")
    gain = norm_gain[None, :]
    buffer, ortho, coeffs, coeff_own, squares, input_grad, gain_grad = whole(
        inputs, gain, out_grad, weight, moment, right_basis
    )
    qkv_group = 3 * HEADS * HEAD_DIM // tensor_count
    qkv_scale = 0.2 * math.sqrt(D * (3 * HEADS * HEAD_DIM) / RANK)
    mlp_scale = 0.2 * math.sqrt(D * FF / RANK)
    moment_new, update, basis_new, input_grad, gain_grad = final_products(
        ortho, squares, coeffs, buffer, coeff_own, input_grad, gain_grad, qkv_group, qkv_scale, mlp_scale
    )
    return (input_grad, gain_grad, moment_new, basis_new, update)


def solution(mesh):
    in_specs = (
        P("dp", None),
        P(),
        P("dp", "tensor"),
        P("dp", "tensor"),
        P("dp", "tensor"),
        P(("tensor", "dp"), None),
    )
    out_specs = (
        P("dp", "tensor"),
        P("tensor"),
        P("dp", "tensor"),
        P(("tensor", "dp"), None),
        P("dp", "tensor"),
    )
    return jax.shard_map(
        per_device, mesh=mesh, in_specs=in_specs, out_specs=out_specs, check_vma=False
    )
```

```python
import math

import jax
import jax.numpy as jnp
from jax import lax
from jax.experimental import pallas as pl
from jax.experimental.pallas import tpu as pltpu
from jax.sharding import PartitionSpec as P

D = 6144
HEADS = 24
HEAD_DIM = 128
FF = 12288
RANK = 512
MOMENTUM = 0.8
NORM_EPSILON = 1e-06

HI = lax.Precision.HIGHEST
MESH = pl.DeviceIdType.MESH
VMEM_LIMIT = 56 * 1024 * 1024
F32 = jnp.float32
BF16 = jnp.bfloat16


def dp_of(x, y, core):
    return (x * 4 + y) * 2 + core


def place():
    dp = lax.axis_index("dp")
    return dp // 8, (dp // 2) % 4, dp % 2, lax.axis_index("tensor")


def send(src, dst, send_sem, recv_sem, **peer):
    copy = pltpu.make_async_remote_copy(
        src_ref=src, dst_ref=dst, send_sem=send_sem, recv_sem=recv_sem,
        device_id=peer, device_id_type=MESH,
    )
    copy.start()
    return copy


def wait_recv(dst, recv_sem, **peer):
    pltpu.make_async_remote_copy(
        src_ref=dst, dst_ref=dst, send_sem=recv_sem, recv_sem=recv_sem,
        device_id=peer, device_id_type=MESH,
    ).wait_recv()


def greet(peers):
    barrier = pltpu.get_barrier_semaphore()
    for peer in peers:
        pl.semaphore_signal(barrier, inc=1, device_id=peer, device_id_type=MESH)
    pl.semaphore_wait(barrier, len(peers))


def plane_peers(x, y, core):
    return (
        [{"dp": dp_of((x + d) % 4, y, core)} for d in (1, 2, 3)]
        + [{"dp": dp_of(x, (y + d) % 4, core)} for d in (1, 2, 3)]
        + [{"dp": dp_of(x, y, 1 - core)}]
    )


def round_robin(generators):
    live = list(generators)
    while live:
        still = []
        for g in live:
            try:
                next(g)
                still.append(g)
            except StopIteration:
                pass
        live = still


def gather_stream(loc, first, ssem, rsem, base, sent):
    x0, y0, core, _ = place()
    a0, b0 = (x0, y0) if first == "x" else (y0, x0)
    sib = dp_of(x0, y0, 1 - core)

    def xy(a, b):
        return (a % 4, b % 4) if first == "x" else (b % 4, a % 4)

    def at(a, b, part, who=None):
        return loc(core if who is None else who, *xy(a, b), part)

    def to(a, b, block, part, slot):
        ref = at(*block, part)
        sent.append(send(ref, ref, ssem.at[base + slot], rsem.at[base + slot], dp=dp_of(*xy(a, b), core)))

    def got(block, part, slot):
        wait_recv(at(*block, part), rsem.at[base + slot], dp=sib)

    def share(block, slot):
        ref = at(*block, 2)
        sent.append(send(ref, ref, ssem.at[base + slot], rsem.at[base + slot], dp=sib))

    def spread(k, block):
        to(a0, b0 + 1, block, 2, 4 + 4 * k)
        to(a0, b0 - 1, block, 2, 5 + 4 * k)

    offs = (0, -1, 1, 2)
    to(a0 + 1, b0, (a0, b0), 2, 0)
    to(a0 - 1, b0, (a0, b0), 2, 1)
    yield
    spread(0, (a0, b0))
    share((a0, b0), 20)
    yield
    got((a0 - 1, b0), 2, 0)
    to(a0 + 1, b0, (a0 - 1, b0), 0, 2)
    got((a0 + 1, b0), 2, 1)
    to(a0 - 1, b0, (a0 + 1, b0), 1, 3)
    spread(1, (a0 - 1, b0))
    spread(2, (a0 + 1, b0))
    yield
    share((a0 - 1, b0), 21)
    share((a0 + 1, b0), 22)
    got((a0 + 2, b0), 0, 2)
    got((a0 + 2, b0), 1, 3)
    spread(3, (a0 + 2, b0))
    share((a0 + 2, b0), 23)
    yield
    for k in range(4):
        a = a0 + offs[k]
        got((a, b0 - 1), 2, 4 + 4 * k)
        to(a0, b0 + 1, (a, b0 - 1), 0, 6 + 4 * k)
        got((a, b0 + 1), 2, 5 + 4 * k)
        to(a0, b0 - 1, (a, b0 + 1), 1, 7 + 4 * k)
        share((a, b0 - 1), 24 + 3 * k)
        share((a, b0 + 1), 25 + 3 * k)
        yield
    for k in range(4):
        a = a0 + offs[k]
        got((a, b0 + 2), 0, 6 + 4 * k)
        got((a, b0 + 2), 1, 7 + 4 * k)
        share((a, b0 + 2), 26 + 3 * k)
        yield
    for k in range(4):
        a = a0 + offs[k]
        wait_recv(at(a, b0, 2, 1 - core), rsem.at[base + 20 + k], dp=sib)
        for j, b in enumerate((b0 - 1, b0 + 1, b0 + 2)):
            wait_recv(at(a, b, 2, 1 - core), rsem.at[base + 24 + 3 * k + j], dp=sib)
    yield


GATHER_SLOTS = 36
EXCHANGE_SLOTS = 6


def exchange_stream(src, mid, out, s, ssem, rsem, base, sent):
    x, y, core, _ = place()
    sib = dp_of(x, y, 1 - core)
    half = slice(16 * s, 16 * s + 16)

    def part(ref, a):
        return ref.at[a, :, half] if s == 0 else ref.at[:, a, half]

    def swapped(ref, b):
        return ref.at[:, b, half] if s == 0 else ref.at[b, :, half]

    a0, b0 = (x, y) if s == 0 else (y, x)

    def dev(a, b):
        return dp_of(a, b, core) if s == 0 else dp_of(b, a, core)

    mine = pltpu.make_async_copy(part(src, a0), mid.at[s, a0], ssem.at[base + 6])
    mine.start()
    for i in range(3):
        to = (a0 + 1 + i) % 4
        sent.append(send(part(src, to), mid.at[s, a0], ssem.at[base + i], rsem.at[base + i], dp=dev(to, b0)))
    yield
    for i in range(3):
        wait_recv(mid.at[s, (a0 + 3 - i) % 4], rsem.at[base + i], dp=sib)
    mine.wait()
    own = pltpu.make_async_copy(mid.at[s, :, b0], swapped(out, b0), ssem.at[base + 6])
    own.start()
    for i in range(3):
        to = (b0 + 1 + i) % 4
        sent.append(send(
            mid.at[s, :, to], swapped(out, b0), ssem.at[base + 3 + i], rsem.at[base + 3 + i], dp=dev(a0, to)
        ))
    yield
    own.wait()
    for i in range(3):
        wait_recv(swapped(out, (b0 + 3 - i) % 4), rsem.at[base + 3 + i], dp=sib)
    yield


def split(v):
    top = v.astype(BF16)
    return top, (v - top.astype(F32)).astype(BF16)


EX = 4 * GATHER_SLOTS
ZP = EX + 28
OTHER = ZP + 35
ZA = OTHER + 4


def front_steps(sent, fetch, store, in_ref, gain_ref, g_ref, w_ref, m_ref, r_ref,
                p_ref, gram_ref, bt_ref, btsib_ref, buf_ref, backall_ref, std_ref, inv_ref,
                rall, gall, got, std, nrm, exmid, exout, exsib, xt, both, bk, bksib, bsrc, bmid,
                part, zbuf, gbuf, cbuf, xbuf, ybuf, ssem, rsem):
    x, y, core, z = place()
    chip = x * 4 + y
    sib = dp_of(x, y, 1 - core)
    xs = [(x + d) % 4 for d in (1, 2, 3)]
    ys = [(y + d) % 4 for d in (1, 2, 3)]
    zs = [(z + d) % 8 for d in range(1, 8)]
    rows, cols = m_ref.shape
    tokens, width = in_ref.shape
    cut = 1408

    other = pl.multiple_of(256 * (1 - core), 128)
    sent.append(send(r_ref.at[:, pl.ds(other, 256)], got, ssem.at[OTHER], rsem.at[OTHER], dp=sib))
    gall[core, pl.ds(pl.multiple_of(32 * chip, 32), 32)] = g_ref[...]

    def loc_g(s):
        def loc(who, bx, by, part):
            lo, n = ((0, cut), (cut, cols - cut), (0, cols))[part]
            return gall.at[who, pl.ds(pl.multiple_of(32 * (bx * 4 + by) + 16 * s, 16), 16), pl.ds(lo, n)]
        return loc

    def loc_r(s):
        def loc(who, bx, by, part):
            lo, n = ((0, 88), (88, 80), (0, 168))[part]
            row = pl.multiple_of((bx * 4 + by) * 168 + lo, 8)
            return rall.at[pl.ds(row, n), pl.ds(pl.multiple_of(256 * who + 128 * s, 128), 128)]
        return loc

    g_streams = [gather_stream(loc_g(s), "xy"[s], ssem, rsem, (2 + s) * GATHER_SLOTS, sent) for s in (0, 1)]
    for g in g_streams:
        next(g)
    for g in g_streams:
        next(g)

    wide = [in_ref[:, 384 * b:384 * b + 384].astype(F32) for b in range(16)]
    mean = sum(jnp.sum(v, axis=1, keepdims=True) for v in wide) * (1.0 / width)
    centered = [in_ref[:, 384 * b:384 * b + 384].astype(F32) - mean for b in range(16)]
    var = sum(jnp.sum(v * v, axis=1, keepdims=True) for v in centered) * (1.0 / width)
    inv = lax.rsqrt(var + NORM_EPSILON)
    inv_ref[...] = jnp.broadcast_to(inv, inv_ref.shape)
    for b in range(16):
        v = (in_ref[:, 384 * b:384 * b + 384].astype(F32) - mean) * inv
        std[b // 2, b % 2] = v
        nrm[b // 4, b % 4] = (v * gain_ref[:, 384 * b:384 * b + 384]).astype(BF16)
    std_ref[...] = std[z]
    ex = [exchange_stream(nrm, exmid, exout, s, ssem, rsem, EX + 7 * s, sent) for s in (0, 1)]
    for g in ex:
        next(g)

    wait_recv(got, rsem.at[OTHER], dp=sib)
    mine = r_ref[:, pl.ds(pl.multiple_of(256 * core, 128), 256)]
    theirs = got[...]
    rall[pl.ds(pl.multiple_of(chip * 168, 8), 168), pl.ds(pl.multiple_of(256 * core, 128), 256)] = jnp.concatenate(
        [jnp.where(core == 0, mine, theirs), jnp.where(core == 0, theirs, mine)], axis=0
    )
    r_streams = [gather_stream(loc_r(s), "xy"[s], ssem, rsem, s * GATHER_SLOTS, sent) for s in (0, 1)]

    def run(gens):
        live = []
        for g in gens:
            try:
                next(g)
                live.append(g)
            except StopIteration:
                pass
        return live

    def mine192(v):
        return jnp.where(core == 0, v[:, 0:192].astype(F32), v[:, 192:384].astype(F32))

    def after_exchange():
        sent.append(send(exout, exsib, ssem.at[OTHER + 1], rsem.at[OTHER + 1], dp=sib))
        for q in range(4):
            v = exout[q].reshape(4 * tokens, 384)
            xt[core, :, 128 * q:128 * q + 128] = mine192(v).T.astype(BF16)
        yield
        wait_recv(exsib, rsem.at[OTHER + 1], dp=sib)
        for q in range(4):
            v = exsib[q].reshape(4 * tokens, 384)
            xt[1 - core, :, 128 * q:128 * q + 128] = mine192(v).T.astype(BF16)
        yield

    def compute():
        for copy in fetch:
            copy.wait()
        for t in range(0, cols, 384):
            acc = m_ref[:, t:t + 384]
            for c in (0, 1):
                acc = acc + jnp.dot(xt[c], gall[c, :, t:t + 384], preferred_element_type=F32)
            buf_ref[:, t:t + 384] = acc
            top, low = split(acc)
            both[0:rows, t:t + 384] = top
            both[rows:2 * rows, t:t + 384] = low
            yield
        store.start()

    bk[:, :, 128:256] = jnp.zeros((2, 512, 128), F32)
    tail = after_exchange()
    work = compute()
    r_live, g_live, x_live = r_streams, g_streams, ex
    r_live = run(r_live)
    tail_live = [tail]
    while g_live or x_live or tail_live:
        g_live = run(g_live)
        if x_live:
            x_live = run(x_live)
        elif tail_live:
            tail_live = run(tail_live)
        r_live = run(r_live)
    work_live = [work]
    while r_live or work_live:
        r_live = run(r_live)
        work_live = run(work_live)

    order = (3, 4, 2, 5, 1, 6, 0)

    def rows24(q):
        return pl.ds(pl.multiple_of(24 * (q % 8), 8), 24)

    halves = [slice(0, 256), slice(256, 512)]
    for h, hc in enumerate(halves):
        acc = jnp.zeros((rows, 256), F32)
        for t in range(0, cols, 384):
            r_top, r_low = split(rall[t:t + 384, hc])
            one = jnp.dot(both[:, t:t + 384], r_top, preferred_element_type=F32)
            two = jnp.dot(both[0:rows, t:t + 384], r_low, preferred_element_type=F32)
            acc = acc + (one[0:rows] + (one[rows:] + two))
        part[:, hc] = acc
        for i in order:
            sent.append(send(
                part.at[rows24(zs[i]), hc], zbuf.at[i, :, hc], ssem.at[ZP + 7 * h + i], rsem.at[ZP + 7 * h + i],
                tensor=zs[i],
            ))
    for c in (0, 1):
        for q in (0, 256):
            bk[c, q:q + 256, 0:192] = lax.dot_general(
                gall[c, q:q + 256, :], w_ref[...], (((1,), (1,)), ((), ())), preferred_element_type=F32
            )
    sent.append(send(bk.at[1 - core], bksib, ssem.at[OTHER + 3], rsem.at[OTHER + 3], dp=sib))
    for t in range(0, cols, 384):
        bt_ref[t:t + 384, :] = both[:, t:t + 384].astype(F32).T.astype(BF16)
    wait_recv(bksib, rsem.at[OTHER + 3], dp=sib)
    for q in range(4):
        ours = bk[core, 128 * q:128 * q + 128, 0:192]
        their = bksib[128 * q:128 * q + 128, 0:192]
        bsrc[q] = jnp.concatenate(
            [jnp.where(core == 0, ours, their), jnp.where(core == 0, their, ours)], axis=1
        ).reshape(4, tokens, 384)
    sent.append(send(bt_ref, btsib_ref, ssem.at[OTHER + 2], rsem.at[OTHER + 2], dp=sib))
    back = [exchange_stream(bsrc, bmid, backall_ref, s, ssem, rsem, EX + 14 + 7 * s, sent) for s in (0, 1)]
    back = run(back)

    def planes(h):
        hc = halves[h]
        quarters = (slice(256 * h, 256 * h + 128), slice(256 * h + 128, 256 * h + 256))

        def pass_on(source, to, slot, cut=hc):
            ref = p_ref.at[rows24(source), cut]
            sent.append(send(ref, ref, ssem.at[ZA + 8 * h + slot], rsem.at[ZA + 8 * h + slot], tensor=(to + 8) % 8))

        def arrived(source, slot, cut=hc):
            wait_recv(p_ref.at[rows24(source + 8), cut], rsem.at[ZA + 8 * h + slot], tensor=(z + 1) % 8)

        total = part[rows24(z), hc]
        for i in reversed(order):
            wait_recv(zbuf.at[i, :, hc], rsem.at[ZP + 7 * h + i], tensor=zs[i])
            total = total + zbuf[i, :, hc]
        p_ref[rows24(z), hc] = total
        pass_on(z, z + 2, 2)
        pass_on(z, z - 2, 3)
        pass_on(z, z + 1, 0)
        pass_on(z, z - 1, 1)
        yield
        arrived(z - 2, 2)
        pass_on(z + 6, z + 2, 6, quarters[0])
        pass_on(z + 6, z + 1, 4)
        arrived(z + 2, 3)
        pass_on(z + 2, z - 2, 7, quarters[1])
        pass_on(z + 2, z - 1, 5)
        yield
        arrived(z - 1, 0)
        arrived(z + 1, 1)
        arrived(z - 3, 4)
        arrived(z + 3, 5)
        arrived(z - 4, 6, quarters[0])
        arrived(z - 4, 7, quarters[1])
        yield

    gathers = [planes(0), planes(1)]
    gathers = run(gathers)
    back = run(back)
    gathers = run(gathers)
    gathers = run(gathers)
    gbuf[...] = lax.dot_general(
        p_ref[:, pl.ds(pl.multiple_of(128 * (z // 2), 128), 128)], p_ref[...],
        (((0,), (0,)), ((), ())), precision=HI, preferred_element_type=F32,
    )
    half = 64 * (z % 2)
    away = gbuf.at[pl.ds(pl.multiple_of(half + 32 * (1 - core), 32), 32)]
    sent.append(send(away, cbuf, ssem.at[ZP + 14], rsem.at[ZP + 14], dp=sib))
    wait_recv(cbuf, rsem.at[ZP + 14], dp=sib)
    cbuf[...] += gbuf[pl.ds(pl.multiple_of(half + 32 * core, 32), 32), :]
    for i in range(3):
        sent.append(send(
            cbuf.at[pl.ds(pl.multiple_of(8 * xs[i], 8), 8)], xbuf.at[i], ssem.at[ZP + 15 + i], rsem.at[ZP + 15 + i],
            dp=dp_of(xs[i], y, core),
        ))
    total = cbuf[pl.ds(pl.multiple_of(8 * x, 8), 8), :]
    for i in range(3):
        wait_recv(xbuf.at[i], rsem.at[ZP + 15 + i], dp=sib)
        total = total + xbuf[i]
    ybuf[y] = total
    for i in range(3):
        sent.append(send(
            ybuf.at[y], ybuf.at[y], ssem.at[ZP + 18 + i], rsem.at[ZP + 18 + i], dp=dp_of(x, ys[i], core)
        ))
    for i in range(3):
        wait_recv(ybuf.at[(y + 3 - i) % 4], rsem.at[ZP + 18 + i], dp=sib)
    gram_ref[z, core, x] = (ybuf[0] + ybuf[1]) + (ybuf[2] + ybuf[3])
    mine = gram_ref.at[z, core, x]
    for i in order:
        sent.append(send(mine, mine, ssem.at[ZP + 21 + i], rsem.at[ZP + 21 + i], tensor=zs[i]))
    back = run(back)
    for i in reversed(order):
        wait_recv(gram_ref.at[(z + 7 - i) % 8, core, x], rsem.at[ZP + 21 + i], tensor=zs[i])
    mine = gram_ref.at[:, core, x]
    for i in range(3):
        sent.append(send(mine, mine, ssem.at[ZP + 28 + i], rsem.at[ZP + 28 + i], dp=dp_of(xs[i], y, core)))
    sent.append(send(mine, mine, ssem.at[ZP + 31], rsem.at[ZP + 31], dp=sib))
    for i in range(3):
        src = (x + 3 - i) % 4
        there = gram_ref.at[:, core, src]
        wait_recv(there, rsem.at[ZP + 28 + i], dp=sib)
        sent.append(send(there, there, ssem.at[ZP + 32 + i], rsem.at[ZP + 32 + i], dp=sib))
    wait_recv(gram_ref.at[:, 1 - core, x], rsem.at[ZP + 31], dp=sib)
    for i in range(3):
        wait_recv(gram_ref.at[:, 1 - core, (x + 3 - i) % 4], rsem.at[ZP + 32 + i], dp=sib)
    wait_recv(btsib_ref, rsem.at[OTHER + 2], dp=sib)


def chol_steps(g_ref, p_ref, o_ref, s_ref, w_ref):
    n_p = p_ref.shape[0]
    s_ref[:, 0:512] = g_ref[...].reshape(512, 512)
    s_ref[:, 512:512 + n_p] = p_ref[...].T
    s_ref[:, 512 + n_p:] = jnp.zeros((512, s_ref.shape[1] - 512 - n_p), F32)
    lane = lax.broadcasted_iota(jnp.int32, (8, 128), 1)
    sub = lax.broadcasted_iota(jnp.int32, (8, 128), 0)

    def lane_splat(v, j):
        return jnp.broadcast_to(v[:, j:j + 1], (8, 128))

    def row_splat(v, i):
        return jnp.broadcast_to(v[i:i + 1, :], (8, 128))

    def block(kb, carry):
        base = pl.multiple_of(kb * 128, 128)
        rest = s_ref[pl.ds(base, 128), pl.ds(base, 128)]
        for k in range(16):
            x = rest[0:8]
            below = rest[8:]
            inside = (lane >= 8 * k) & (lane < 8 * k + 8)
            c = [lane_splat(x, 8 * k + q) for q in range(8)]
            x = jnp.where(inside, (lane - 8 * k == sub).astype(F32), x)
            inv, up, rows = [], [], []
            scale = jnp.ones((8, 128), F32)
            for p in range(8):
                pd = row_splat(c[p], p)
                ip = 1.0 / pd
                scale = jnp.where(sub == p, lax.rsqrt(pd), scale)
                m = jnp.where(sub > p, c[p] * ip, 0.0)
                u = {}
                for q in range(p + 1, 8):
                    u[q] = c[q][p:p + 1]
                    c[q] = c[q] - (c[p] * row_splat(c[q], p)) * ip
                r = x[p:p + 1]
                x = x - m * r
                inv.append(ip[0:1])
                up.append(u)
                rows.append(r)
            w_ref[8 * k:8 * k + 8, :] = jnp.where(lane <= sub + 8 * k, x * scale, 0.0)
            if k < 15:
                n = below.shape[0]
                e = [jnp.broadcast_to(below[:, 8 * k + q:8 * k + q + 1], (n, 128)) for q in range(8)]
                below = jnp.where(inside[0:1], 0.0, below)
                for p in range(8):
                    m = e[p] * inv[p]
                    for q in range(p + 1, 8):
                        e[q] = e[q] - m * up[p][q]
                    below = below - m * rows[p]
                rest = below
        rows_k = pl.ds(base, 128)
        s_ref[rows_k, :] = jnp.dot(w_ref[...], s_ref[rows_k, :], precision=HI, preferred_element_type=F32)
        for rb in range(1, 4):
            @pl.when(rb > kb)
            def _():
                ub = s_ref[rows_k, 128 * rb:128 * rb + 128]
                s_ref[128 * rb:128 * rb + 128, 128 * rb:] -= lax.dot_general(
                    ub, s_ref[rows_k, 128 * rb:], (((0,), (0,)), ((), ())), precision=HI,
                    preferred_element_type=F32,
                )
        return carry

    lax.fori_loop(0, 4, block, 0)
    o_ref[...] = s_ref[:, 512:512 + n_p].T


SPLIT = ((0, 96), (96, 80), (0, 176))


def coeff_steps(sent, bt_ref, btsib_ref, o_ref, back_ref, std_ref, gain_ref, inv_ref,
                call_ref, cown_ref, csq_ref, ig_ref, gg_ref,
                osib, rhs, c_ref, sbuf, rbuf, acc, s2, r2, fin, fsib, agb,
                xsq, ysq, zsq, sqs, ngbuf, stat, gx, gy, gc, ssem, rsem, gs, gr, ns, nr):
    x, y, core, z = place()
    sib = dp_of(x, y, 1 - core)
    xs = [(x + d) % 4 for d in (1, 2, 3)]
    ys = [(y + d) % 4 for d in (1, 2, 3)]
    zs = [(z + d) % 8 for d in range(1, 8)]
    first = ("x", "y")

    def half(who):
        return pl.ds(pl.multiple_of(256 * who, 128), 256)

    sent.append(send(o_ref.at[:, half(1 - core)], osib, ssem.at[0], rsem.at[0], dp=sib))

    def fill(v):
        top, low = split(v)
        n = v.shape[0]
        rhs[0:n, 0:256] = top
        rhs[n:2 * n, 0:256] = top
        rhs[0:n, 256:512] = low
        rhs[n:2 * n, 256:512] = low

    cols = bt_ref.shape[0]
    fill(o_ref[:, half(core)])
    for t in range(0, cols, 384):
        two = jnp.dot(bt_ref[t:t + 384, :], rhs[...], preferred_element_type=F32)
        c_ref[t:t + 384, :] = two[:, 0:256] + two[:, 256:512]
    wait_recv(osib, rsem.at[0], dp=sib)
    fill(osib[...])
    for t in range(0, cols, 384):
        two = jnp.dot(btsib_ref[t:t + 384, :], rhs[...], preferred_element_type=F32)
        c_ref[t:t + 384, :] += two[:, 0:256] + two[:, 256:512]

    def cols_of(who, s):
        return pl.ds(pl.multiple_of(256 * who + 128 * s, 128), 128)

    a0 = (x, y)
    b0 = (y, x)

    def own(s, off, b):
        a = (a0[s] + off) % 4
        bx, by = (a, b) if s == 0 else (b, a)
        return c_ref[pl.ds(pl.multiple_of(168 * (bx * 4 + by), 8), 168), 128 * s:128 * s + 128]

    def dev(s, a, b):
        a, b = a % 4, b % 4
        return dp_of(a, b, core) if s == 0 else dp_of(b, a, core)

    zero_pad = jnp.zeros((8, 128), F32)

    def padded(v):
        return jnp.concatenate([v, zero_pad], axis=0).astype(BF16)

    def reduce_direct(s):
        base = 8 + 6 * s
        a, b = a0[s], b0[s]
        offs = (2, 1, 3)
        for i in range(3):
            for j in range(4):
                sbuf[s, i, j] = padded(own(s, offs[i], j))
            sent.append(send(
                sbuf.at[s, i], rbuf.at[s, i], ssem.at[base + i], rsem.at[base + i], dp=dev(s, a + offs[i], b)
            ))
            yield
        for j in range(4):
            acc[s, j] = own(s, 0, j)
        for i in (1, 2, 0):
            wait_recv(rbuf.at[s, i], rsem.at[base + i], dp=sib)
        yield

        def summed(off):
            j = (b + off) % 4
            return (acc[s, j] + rbuf[s, 0, j, 0:168].astype(F32)) + (
                rbuf[s, 1, j, 0:168].astype(F32) + rbuf[s, 2, j, 0:168].astype(F32)
            )

        for i in range(3):
            s2[s, i] = padded(summed(offs[i]))
            sent.append(send(
                s2.at[s, i], r2.at[s, i], ssem.at[base + 3 + i], rsem.at[base + 3 + i], dp=dev(s, a, b + offs[i])
            ))
        yield
        total = summed(0)
        for i in (1, 2, 0):
            wait_recv(r2.at[s, i], rsem.at[base + 3 + i], dp=sib)
            total = total + r2[s, i, 0:168].astype(F32)
        fin[:, 128 * s:128 * s + 128] = total
        agb[x * 4 + y, :, cols_of(core, s)] = padded(total)
        yield

    round_robin([reduce_direct(0), reduce_direct(1)])

    def norms():
        sent.append(send(fin, fsib, ssem.at[24], rsem.at[24], dp=sib))
        v = fin[...]
        xsq[x] = jnp.broadcast_to(jnp.sum(v * v, axis=0, keepdims=True), (8, 256))
        for i in range(3):
            sent.append(send(xsq.at[x], xsq.at[x], ssem.at[25 + i], rsem.at[25 + i], dp=dp_of(xs[i], y, core)))
        yield
        for i in range(3):
            wait_recv(xsq.at[(x + 3 - i) % 4], rsem.at[25 + i], dp=sib)
        ysq[y] = (xsq[0] + xsq[1]) + (xsq[2] + xsq[3])
        for i in range(3):
            sent.append(send(ysq.at[y], ysq.at[y], ssem.at[28 + i], rsem.at[28 + i], dp=dp_of(x, ys[i], core)))
        yield
        for i in range(3):
            wait_recv(ysq.at[(y + 3 - i) % 4], rsem.at[28 + i], dp=sib)
        zsq[z] = (ysq[0] + ysq[1]) + (ysq[2] + ysq[3])
        for i in range(7):
            sent.append(send(zsq.at[z], zsq.at[z], ssem.at[31 + i], rsem.at[31 + i], tensor=zs[i]))
        yield
        for i in range(7):
            wait_recv(zsq.at[(z + 7 - i) % 8], rsem.at[31 + i], tensor=zs[i])
        total = zsq[0]
        for i in range(1, 8):
            total = total + zsq[i]
        sqs[core] = total
        sent.append(send(sqs.at[core], sqs.at[core], ssem.at[38], rsem.at[38], dp=sib))
        yield
        wait_recv(fsib, rsem.at[24], dp=sib)
        left = jnp.where(core == 0, fin[0:84], fsib[84:168])
        right = jnp.where(core == 0, fsib[0:84], fin[84:168])
        cown_ref[:, 0:256] = left
        cown_ref[:, 256:512] = right
        yield
        wait_recv(sqs.at[1 - core], rsem.at[38], dp=sib)
        csq_ref[:, 0:256] = sqs[0]
        csq_ref[:, 256:512] = sqs[1]
        yield

    def input_grad():
        total = back_ref[z // 2, pl.ds(2 * (z % 2), 2)]
        for i in range(7):
            wait_recv(ngbuf.at[i], nr.at[i], tensor=zs[i])
            total = total + ngbuf[i]
        std = std_ref[...]
        gain = gain_ref[:, pl.ds(pl.multiple_of(768 * z, 128), 768)]
        scaled = total * jnp.stack([gain[:, 0:384], gain[:, 384:768]])
        lane = lax.broadcasted_iota(jnp.int32, (32, 128), 1)

        def per_token(v):
            return jnp.sum(jnp.sum(v, axis=0), axis=1, keepdims=True)

        stat[z] = jnp.where(lane < 64, per_token(scaled), per_token(scaled * std))
        for i in range(7):
            sent.append(send(stat.at[z], stat.at[z], ns.at[7 + i], nr.at[7 + i], tensor=zs[i]))
        gx[x] = jnp.broadcast_to(jnp.sum(total * std, axis=1, keepdims=True), gx.shape[1:])
        for i in range(3):
            sent.append(send(gx.at[x], gx.at[x], ns.at[14 + i], nr.at[14 + i], dp=dp_of(xs[i], y, core)))
        yield
        for i in range(3):
            wait_recv(gx.at[(x + 3 - i) % 4], nr.at[14 + i], dp=sib)
        gy[y] = (gx[0] + gx[1]) + (gx[2] + gx[3])
        for i in range(3):
            sent.append(send(gy.at[y], gy.at[y], ns.at[17 + i], nr.at[17 + i], dp=dp_of(x, ys[i], core)))
        for i in range(7):
            wait_recv(stat.at[(z + 7 - i) % 8], nr.at[7 + i], tensor=zs[i])
        sums = stat[0]
        for i in range(1, 8):
            sums = sums + stat[i]
        sums = sums * (1.0 / (16 * 384))
        full = inv_ref[...] * (scaled - sums[:, 0:1] - std * sums[:, 64:65])
        ig_ref[:, 0:384] = full[0].astype(BF16)
        ig_ref[:, 384:768] = full[1].astype(BF16)
        yield
        for i in range(3):
            wait_recv(gy.at[(y + 3 - i) % 4], nr.at[17 + i], dp=sib)
        gc[core] = (gy[0] + gy[1]) + (gy[2] + gy[3])
        sent.append(send(gc.at[core], gc.at[core], ns.at[20], nr.at[20], dp=sib))
        yield
        wait_recv(gc.at[1 - core], nr.at[20], dp=sib)
        gg_ref[:, 0:384] = gc[0, 0] + gc[1, 0]
        gg_ref[:, 384:768] = gc[0, 1] + gc[1, 1]
        yield

    def loc(s):
        def at(who, bx, by, part):
            lo, rows = SPLIT[part]
            return agb.at[bx * 4 + by, pl.ds(lo, rows), cols_of(who, s)]
        return at

    round_robin([
        gather_stream(loc(0), first[0], gs, gr, 0, sent),
        gather_stream(loc(1), first[1], gs, gr, GATHER_SLOTS, sent),
        norms(),
        input_grad(),
    ])
    for j in range(8):
        two = jnp.concatenate([agb[2 * j, 0:168].astype(F32), agb[2 * j + 1, 0:168].astype(F32)], axis=0)
        call_ref[336 * j:336 * j + 336, :] = two.astype(BF16)


def whole_kernel(*refs):
    ins, refs = list(refs[:6]), refs[6:]
    buf_out, ortho, call, cown, csq, ig, gg = refs[:7]
    buf, weight, moment, local, refs = refs[7], refs[8], refs[9], refs[10], refs[11:]
    fetch = [
        pltpu.make_async_copy(ins[3], weight, local.at[0]),
        pltpu.make_async_copy(ins[4], moment, local.at[1]),
    ]
    for copy in fetch:
        copy.start()
    ins[3], ins[4] = weight, moment
    store = pltpu.make_async_copy(buf, buf_out, local.at[2])
    front_scratch, refs = refs[:29], refs[29:]
    s_scr, w_scr, refs = refs[0], refs[1], refs[2:]
    p, gram, bt, btsib, backall, stdz, inv = front_scratch[:7]
    x, y, core, z = place()
    greet([{"tensor": (z + d) % 8} for d in range(1, 8)] + plane_peers(x, y, core))
    sent = []
    front_steps(sent, fetch, store, *ins, p, gram, bt, btsib, buf, backall, stdz, inv, *front_scratch[7:])
    ngbuf, ns, nr = refs[15], refs[-2], refs[-1]
    for i in (3, 4, 2, 5, 1, 6, 0):
        to = (z + 1 + i) % 8
        sent.append(send(backall.at[to // 2, pl.ds(2 * (to % 2), 2)], ngbuf.at[i], ns.at[i], nr.at[i], tensor=to))
    chol_steps(gram, p, ortho, s_scr, w_scr)
    store.wait()
    coeff_steps(sent, bt, btsib, ortho, backall, stdz, ins[1], inv, call, cown, csq, ig, gg, *refs)
    for copy in sent:
        copy.wait_send()


def whole(inputs, gain, out_grad, weight, moment, right_basis):
    vm = pl.BlockSpec(memory_space=pltpu.VMEM)
    rows, cols = moment.shape
    tokens = inputs.shape[0]
    anywhere = pl.BlockSpec(memory_space=pl.ANY)
    block = (2, tokens, 384)

    def f32(*shape):
        return pltpu.VMEM(shape, F32)

    def bf16(*shape):
        return pltpu.VMEM(shape, BF16)

    dma = pltpu.SemaphoreType.DMA
    front_scratch = [
        f32(rows, RANK),
        f32(8, 2, 4, 8, RANK),
        bf16(cols, 2 * rows),
        bf16(cols, 2 * rows),
        f32(4, 4, tokens, 384),
        f32(*block),
        f32(tokens, 384),
        f32(cols, RANK),
        bf16(2, 16 * tokens, cols),
        f32(right_basis.shape[0], 256),
        f32(8, 2, tokens, 384),
        bf16(4, 4, tokens, 384),
        bf16(2, 4, 4, 16, 384),
        bf16(4, 4, tokens, 384),
        bf16(4, 4, tokens, 384),
        bf16(2, rows, 16 * tokens),
        bf16(2 * rows, cols),
        f32(2, 16 * tokens, 256),
        f32(16 * tokens, 256),
        f32(4, 4, tokens, 384),
        f32(2, 4, 4, 16, 384),
        f32(rows, RANK),
        f32(7, 24, RANK),
        f32(128, RANK),
        f32(32, RANK),
        f32(3, 8, RANK),
        f32(4, 8, RANK),
        dma((ZA + 16,)),
        dma((ZA + 16,)),
    ]
    chol_scratch = [f32(RANK, 768), f32(128, 128)]
    coeff_scratch = [
        f32(192, 256),
        bf16(384, RANK),
        f32(2688, 256),
        bf16(2, 3, 4, 176, 128),
        bf16(2, 3, 4, 176, 128),
        f32(2, 4, 168, 128),
        bf16(2, 3, 176, 128),
        bf16(2, 3, 176, 128),
        f32(168, 256),
        f32(168, 256),
        bf16(16, 176, RANK),
        f32(4, 8, 256),
        f32(4, 8, 256),
        f32(8, 8, 256),
        f32(2, 8, 256),
        f32(7, *block),
        f32(8, 32, 128),
        f32(4, 2, 8, 384),
        f32(4, 2, 8, 384),
        f32(2, 2, 8, 384),
        dma((39,)),
        dma((39,)),
        dma((2 * GATHER_SLOTS,)),
        dma((2 * GATHER_SLOTS,)),
        dma((21,)),
        dma((21,)),
    ]
    return pl.pallas_call(
        whole_kernel,
        out_shape=(
            jax.ShapeDtypeStruct((rows, cols), F32),
            jax.ShapeDtypeStruct((rows, RANK), F32),
            jax.ShapeDtypeStruct((cols, RANK), BF16),
            jax.ShapeDtypeStruct((84, RANK), F32),
            jax.ShapeDtypeStruct((8, RANK), F32),
            jax.ShapeDtypeStruct((tokens, 768), BF16),
            jax.ShapeDtypeStruct((8, 768), F32),
        ),
        in_specs=[vm, vm, vm, anywhere, anywhere, vm],
        out_specs=(anywhere,) + (vm,) * 6,
        scratch_shapes=[f32(rows, cols), bf16(rows, cols), f32(rows, cols), dma((3,))] + front_scratch + chol_scratch + coeff_scratch,
        compiler_params=pltpu.CompilerParams(
            collective_id=1, has_side_effects=True, vmem_limit_bytes=VMEM_LIMIT
        ),
    )(inputs, gain, out_grad, weight, moment, right_basis)


def final_kernel(group, qkv_scale, mlp_scale, o_ref, csq_ref, c_ref, buf_ref, cown_ref, ig_ref, gg_ref,
                 mom_ref, upd_ref, basis_ref, igo_ref, ggo_ref, lhs):
    rows = o_ref.shape[0]
    step = pl.program_id(0)

    @pl.when(step == 0)
    def _():
        inv = 1.0 / (jnp.sqrt(csq_ref[0:1]) + 1e-08)
        o = o_ref[...]
        lhs[0:rows, :] = o.astype(BF16)
        top, low = split(o * inv)
        lhs[rows:2 * rows, :] = top
        lhs[2 * rows:3 * rows, :] = low
        basis_ref[...] = cown_ref[...] * inv
        igo_ref[...] = ig_ref[...]
        ggo_ref[...] = gg_ref[0]

    out = lax.dot_general(lhs[...], c_ref[...], (((1,), (1,)), ((), ())), preferred_element_type=F32)
    tile = out.shape[1]
    position = lax.broadcasted_iota(jnp.int32, (1, tile), 1) + step * tile
    scale = jnp.where(position < group, qkv_scale, mlp_scale)
    mom_ref[...] = buf_ref[...] - (1.0 - MOMENTUM) * out[0:rows]
    upd_ref[...] = (out[rows:2 * rows] + out[2 * rows:3 * rows]) * scale


def final_products(o, squares, coeffs, buffer, coeff_own, input_grad, gain_grad, *scales):
    rows, cols = buffer.shape
    tile = 896

    def all_of(v):
        return pl.BlockSpec(v.shape, lambda i: (0,) * v.ndim)

    by_col = pl.BlockSpec((rows, tile), lambda i: (0, i))
    gain_out = jax.ShapeDtypeStruct((gain_grad.shape[1],), F32)
    return pl.pallas_call(
        lambda *refs: final_kernel(*scales, *refs),
        grid=(cols // tile,),
        out_shape=(
            jax.ShapeDtypeStruct(buffer.shape, F32),
            jax.ShapeDtypeStruct(buffer.shape, F32),
            jax.ShapeDtypeStruct(coeff_own.shape, F32),
            jax.ShapeDtypeStruct(input_grad.shape, BF16),
            gain_out,
        ),
        in_specs=[
            all_of(o),
            all_of(squares),
            pl.BlockSpec((tile, RANK), lambda i: (i, 0)),
            by_col,
            all_of(coeff_own),
            all_of(input_grad),
            all_of(gain_grad),
        ],
        out_specs=(by_col, by_col, all_of(coeff_own), all_of(input_grad), all_of(gain_out)),
        scratch_shapes=[pltpu.VMEM((3 * rows, RANK), BF16)],
        compiler_params=pltpu.CompilerParams(vmem_limit_bytes=VMEM_LIMIT),
    )(o, squares, coeffs, buffer, coeff_own, input_grad, gain_grad)


def per_device(inputs, norm_gain, out_grad, weight, moment, right_basis):
    tensor_count = lax.axis_size("tensor")
    gain = norm_gain[None, :]
    buffer, ortho, coeffs, coeff_own, squares, input_grad, gain_grad = whole(
        inputs, gain, out_grad, weight, moment, right_basis
    )
    qkv_group = 3 * HEADS * HEAD_DIM // tensor_count
    qkv_scale = 0.2 * math.sqrt(D * (3 * HEADS * HEAD_DIM) / RANK)
    mlp_scale = 0.2 * math.sqrt(D * FF / RANK)
    moment_new, update, basis_new, input_grad, gain_grad = final_products(
        ortho, squares, coeffs, buffer, coeff_own, input_grad, gain_grad, qkv_group, qkv_scale, mlp_scale
    )
    return (input_grad, gain_grad, moment_new, basis_new, update)


def solution(mesh):
    in_specs = (
        P("dp", None),
        P(),
        P("dp", "tensor"),
        P("dp", "tensor"),
        P("dp", "tensor"),
        P(("tensor", "dp"), None),
    )
    out_specs = (
        P("dp", "tensor"),
        P("tensor"),
        P("dp", "tensor"),
        P(("tensor", "dp"), None),
        P("dp", "tensor"),
    )
    return jax.shard_map(
        per_device, mesh=mesh, in_specs=in_specs, out_specs=out_specs, check_vma=False
    )
```

```python
import math

import jax
import jax.numpy as jnp
from jax import lax
from jax.experimental import pallas as pl
from jax.experimental.pallas import tpu as pltpu
from jax.sharding import PartitionSpec as P

D = 6144
HEADS = 24
HEAD_DIM = 128
FF = 12288
RANK = 512
MOMENTUM = 0.8
NORM_EPSILON = 1e-06

HI = lax.Precision.HIGHEST
MESH = pl.DeviceIdType.MESH
VMEM_LIMIT = 56 * 1024 * 1024
F32 = jnp.float32
BF16 = jnp.bfloat16


def dp_of(x, y, core):
    return (x * 4 + y) * 2 + core


def place():
    dp = lax.axis_index("dp")
    return dp // 8, (dp // 2) % 4, dp % 2, lax.axis_index("tensor")


def copy_to(src, dst, send_sem, recv_sem, **peer):
    return pltpu.make_async_remote_copy(
        src_ref=src, dst_ref=dst, send_sem=send_sem, recv_sem=recv_sem,
        device_id=peer, device_id_type=MESH,
    )


def send(src, dst, send_sem, recv_sem, **peer):
    copy = copy_to(src, dst, send_sem, recv_sem, **peer)
    copy.start()
    return copy


def wait_recv(dst, recv_sem, **peer):
    pltpu.make_async_remote_copy(
        src_ref=dst, dst_ref=dst, send_sem=recv_sem, recv_sem=recv_sem,
        device_id=peer, device_id_type=MESH,
    ).wait_recv()


def greet(peers):
    barrier = pltpu.get_barrier_semaphore()
    for peer in peers:
        pl.semaphore_signal(barrier, inc=1, device_id=peer, device_id_type=MESH)
    pl.semaphore_wait(barrier, len(peers))


def plane_peers(x, y, core):
    return (
        [{"dp": dp_of((x + d) % 4, y, core)} for d in (1, 2, 3)]
        + [{"dp": dp_of(x, (y + d) % 4, core)} for d in (1, 2, 3)]
        + [{"dp": dp_of(x, y, 1 - core)}]
    )


def round_robin(generators):
    live = list(generators)
    while live:
        still = []
        for g in live:
            try:
                next(g)
                still.append(g)
            except StopIteration:
                pass
        live = still


def gather_stream(loc, first, ssem, rsem, base, sent):
    x0, y0, core, _ = place()
    a0, b0 = (x0, y0) if first == "x" else (y0, x0)
    sib = dp_of(x0, y0, 1 - core)

    def xy(a, b):
        return (a % 4, b % 4) if first == "x" else (b % 4, a % 4)

    def at(a, b, part, who=None):
        return loc(core if who is None else who, *xy(a, b), part)

    def to(a, b, block, part, slot):
        ref = at(*block, part)
        sent.append(send(ref, ref, ssem.at[base + slot], rsem.at[base + slot], dp=dp_of(*xy(a, b), core)))

    def got(block, part, slot):
        wait_recv(at(*block, part), rsem.at[base + slot], dp=sib)

    def share(block, slot):
        ref = at(*block, 2)
        sent.append(send(ref, ref, ssem.at[base + slot], rsem.at[base + slot], dp=sib))

    def spread(k, block):
        to(a0, b0 + 1, block, 2, 4 + 4 * k)
        to(a0, b0 - 1, block, 2, 5 + 4 * k)

    offs = (0, -1, 1, 2)
    to(a0 + 1, b0, (a0, b0), 2, 0)
    to(a0 - 1, b0, (a0, b0), 2, 1)
    yield
    spread(0, (a0, b0))
    share((a0, b0), 20)
    yield
    got((a0 - 1, b0), 2, 0)
    to(a0 + 1, b0, (a0 - 1, b0), 0, 2)
    got((a0 + 1, b0), 2, 1)
    to(a0 - 1, b0, (a0 + 1, b0), 1, 3)
    spread(1, (a0 - 1, b0))
    spread(2, (a0 + 1, b0))
    yield
    share((a0 - 1, b0), 21)
    share((a0 + 1, b0), 22)
    got((a0 + 2, b0), 0, 2)
    got((a0 + 2, b0), 1, 3)
    spread(3, (a0 + 2, b0))
    share((a0 + 2, b0), 23)
    yield
    for k in range(4):
        a = a0 + offs[k]
        got((a, b0 - 1), 2, 4 + 4 * k)
        to(a0, b0 + 1, (a, b0 - 1), 0, 6 + 4 * k)
        got((a, b0 + 1), 2, 5 + 4 * k)
        to(a0, b0 - 1, (a, b0 + 1), 1, 7 + 4 * k)
        share((a, b0 - 1), 24 + 3 * k)
        share((a, b0 + 1), 25 + 3 * k)
        yield
    for k in range(4):
        a = a0 + offs[k]
        got((a, b0 + 2), 0, 6 + 4 * k)
        got((a, b0 + 2), 1, 7 + 4 * k)
        share((a, b0 + 2), 26 + 3 * k)
        yield
    for k in range(4):
        a = a0 + offs[k]
        wait_recv(at(a, b0, 2, 1 - core), rsem.at[base + 20 + k], dp=sib)
        for j, b in enumerate((b0 - 1, b0 + 1, b0 + 2)):
            wait_recv(at(a, b, 2, 1 - core), rsem.at[base + 24 + 3 * k + j], dp=sib)
    yield


GATHER_SLOTS = 36
EXCHANGE_SLOTS = 6


def exchange_stream(src, mid, out, s, ssem, rsem, base, sent):
    x, y, core, _ = place()
    sib = dp_of(x, y, 1 - core)
    half = slice(16 * s, 16 * s + 16)

    def part(ref, a):
        return ref.at[a, :, half] if s == 0 else ref.at[:, a, half]

    def swapped(ref, b):
        return ref.at[:, b, half] if s == 0 else ref.at[b, :, half]

    a0, b0 = (x, y) if s == 0 else (y, x)

    def dev(a, b):
        return dp_of(a, b, core) if s == 0 else dp_of(b, a, core)

    mine = pltpu.make_async_copy(part(src, a0), mid.at[s, a0], ssem.at[base + 6])
    mine.start()
    for i in range(3):
        to = (a0 + 1 + i) % 4
        sent.append(send(part(src, to), mid.at[s, a0], ssem.at[base + i], rsem.at[base + i], dp=dev(to, b0)))
    yield
    for i in range(3):
        wait_recv(mid.at[s, (a0 + 3 - i) % 4], rsem.at[base + i], dp=sib)
    mine.wait()
    own = pltpu.make_async_copy(mid.at[s, :, b0], swapped(out, b0), ssem.at[base + 6])
    own.start()
    for i in range(3):
        to = (b0 + 1 + i) % 4
        sent.append(send(
            mid.at[s, :, to], swapped(out, b0), ssem.at[base + 3 + i], rsem.at[base + 3 + i], dp=dev(a0, to)
        ))
    yield
    own.wait()
    for i in range(3):
        wait_recv(swapped(out, (b0 + 3 - i) % 4), rsem.at[base + 3 + i], dp=sib)
    yield


def split(v):
    top = v.astype(BF16)
    return top, (v - top.astype(F32)).astype(BF16)


EX = 4 * GATHER_SLOTS
ZP = EX + 28
OTHER = ZP + 35
ZA = OTHER + 4
GP = ZA + 16


def front_steps(sent, fetch, store, in_ref, gain_ref, g_ref, w_ref, m_ref, r_ref,
                p_ref, gram_ref, bt_ref, btsib_ref, buf_ref, backall_ref, std_ref, inv_ref,
                rall, gall, got, std, nrm, exmid, exout, exsib, xt, both, bk, bksib, bsrc, bmid,
                part, zbuf, gbuf, cbuf, xbuf, ybuf, ssem, rsem):
    x, y, core, z = place()
    chip = x * 4 + y
    sib = dp_of(x, y, 1 - core)
    xs = [(x + d) % 4 for d in (1, 2, 3)]
    ys = [(y + d) % 4 for d in (1, 2, 3)]
    zs = [(z + d) % 8 for d in range(1, 8)]
    rows, cols = m_ref.shape
    tokens, width = in_ref.shape
    cut = 1408

    other = pl.multiple_of(256 * (1 - core), 128)
    sent.append(send(r_ref.at[:, pl.ds(other, 256)], got, ssem.at[OTHER], rsem.at[OTHER], dp=sib))
    gall[core, pl.ds(pl.multiple_of(32 * chip, 32), 32)] = g_ref[...]

    def loc_g(s):
        def loc(who, bx, by, part):
            lo, n = ((0, cut), (cut, cols - cut), (0, cols))[part]
            return gall.at[who, pl.ds(pl.multiple_of(32 * (bx * 4 + by) + 16 * s, 16), 16), pl.ds(lo, n)]
        return loc

    def loc_r(s):
        def loc(who, bx, by, part):
            lo, n = ((0, 88), (88, 80), (0, 168))[part]
            row = pl.multiple_of((bx * 4 + by) * 168 + lo, 8)
            return rall.at[pl.ds(row, n), pl.ds(pl.multiple_of(256 * who + 128 * s, 128), 128)]
        return loc

    g_streams = [gather_stream(loc_g(s), "xy"[s], ssem, rsem, (2 + s) * GATHER_SLOTS, sent) for s in (0, 1)]
    for g in g_streams:
        next(g)
    for g in g_streams:
        next(g)

    wide = [in_ref[:, 384 * b:384 * b + 384].astype(F32) for b in range(16)]
    mean = sum(jnp.sum(v, axis=1, keepdims=True) for v in wide) * (1.0 / width)
    centered = [in_ref[:, 384 * b:384 * b + 384].astype(F32) - mean for b in range(16)]
    var = sum(jnp.sum(v * v, axis=1, keepdims=True) for v in centered) * (1.0 / width)
    inv = lax.rsqrt(var + NORM_EPSILON)
    inv_ref[...] = jnp.broadcast_to(inv, inv_ref.shape)
    for b in range(16):
        v = (in_ref[:, 384 * b:384 * b + 384].astype(F32) - mean) * inv
        std[b // 2, b % 2] = v
        nrm[b // 4, b % 4] = (v * gain_ref[:, 384 * b:384 * b + 384]).astype(BF16)
    std_ref[...] = std[z]
    ex = [exchange_stream(nrm, exmid, exout, s, ssem, rsem, EX + 7 * s, sent) for s in (0, 1)]
    for g in ex:
        next(g)

    wait_recv(got, rsem.at[OTHER], dp=sib)
    mine = r_ref[:, pl.ds(pl.multiple_of(256 * core, 128), 256)]
    theirs = got[...]
    rall[pl.ds(pl.multiple_of(chip * 168, 8), 168), pl.ds(pl.multiple_of(256 * core, 128), 256)] = jnp.concatenate(
        [jnp.where(core == 0, mine, theirs), jnp.where(core == 0, theirs, mine)], axis=0
    )
    r_streams = [gather_stream(loc_r(s), "xy"[s], ssem, rsem, s * GATHER_SLOTS, sent) for s in (0, 1)]

    def run(gens):
        live = []
        for g in gens:
            try:
                next(g)
                live.append(g)
            except StopIteration:
                pass
        return live

    def mine192(v):
        return jnp.where(core == 0, v[:, 0:192].astype(F32), v[:, 192:384].astype(F32))

    def after_exchange():
        sent.append(send(exout, exsib, ssem.at[OTHER + 1], rsem.at[OTHER + 1], dp=sib))
        for q in range(4):
            v = exout[q].reshape(4 * tokens, 384)
            xt[core, :, 128 * q:128 * q + 128] = mine192(v).T.astype(BF16)
        yield
        wait_recv(exsib, rsem.at[OTHER + 1], dp=sib)
        for q in range(4):
            v = exsib[q].reshape(4 * tokens, 384)
            xt[1 - core, :, 128 * q:128 * q + 128] = mine192(v).T.astype(BF16)
        yield

    def compute():
        for copy in fetch:
            copy.wait()
        for t in range(0, cols, 384):
            acc = m_ref[:, t:t + 384]
            for c in (0, 1):
                acc = acc + jnp.dot(xt[c], gall[c, :, t:t + 384], preferred_element_type=F32)
            buf_ref[:, t:t + 384] = acc
            top, low = split(acc)
            both[0:rows, t:t + 384] = top
            both[rows:2 * rows, t:t + 384] = low
            yield
        store.start()

    bk[:, :, 128:256] = jnp.zeros((2, 512, 128), F32)
    tail = after_exchange()
    work = compute()
    r_live, g_live, x_live = r_streams, g_streams, ex
    r_live = run(r_live)
    tail_live = [tail]
    while g_live or x_live or tail_live:
        g_live = run(g_live)
        if x_live:
            x_live = run(x_live)
        elif tail_live:
            tail_live = run(tail_live)
        r_live = run(r_live)
    work_live = [work]
    while r_live or work_live:
        r_live = run(r_live)
        work_live = run(work_live)

    order = (3, 4, 2, 5, 1, 6, 0)

    def rows24(q):
        return pl.ds(pl.multiple_of(24 * (q % 8), 8), 24)

    halves = [slice(0, 256), slice(256, 512)]
    for h, hc in enumerate(halves):
        acc = jnp.zeros((rows, 256), F32)
        for t in range(0, cols, 384):
            r_top, r_low = split(rall[t:t + 384, hc])
            one = jnp.dot(both[:, t:t + 384], r_top, preferred_element_type=F32)
            two = jnp.dot(both[0:rows, t:t + 384], r_low, preferred_element_type=F32)
            acc = acc + (one[0:rows] + (one[rows:] + two))
        part[:, hc] = acc
        for i in order:
            sent.append(send(
                part.at[rows24(zs[i]), hc], zbuf.at[i, :, hc], ssem.at[ZP + 7 * h + i], rsem.at[ZP + 7 * h + i],
                tensor=zs[i],
            ))
    for c in (0, 1):
        for q in (0, 256):
            bk[c, q:q + 256, 0:192] = lax.dot_general(
                gall[c, q:q + 256, :], w_ref[...], (((1,), (1,)), ((), ())), preferred_element_type=F32
            )
    sent.append(send(bk.at[1 - core], bksib, ssem.at[OTHER + 3], rsem.at[OTHER + 3], dp=sib))
    for t in range(0, cols, 384):
        bt_ref[t:t + 384, :] = both[:, t:t + 384].astype(F32).T.astype(BF16)
    wait_recv(bksib, rsem.at[OTHER + 3], dp=sib)
    for q in range(4):
        ours = bk[core, 128 * q:128 * q + 128, 0:192]
        their = bksib[128 * q:128 * q + 128, 0:192]
        bsrc[q] = jnp.concatenate(
            [jnp.where(core == 0, ours, their), jnp.where(core == 0, their, ours)], axis=1
        ).reshape(4, tokens, 384)
    sent.append(send(bt_ref, btsib_ref, ssem.at[OTHER + 2], rsem.at[OTHER + 2], dp=sib))
    back = [exchange_stream(bsrc, bmid, backall_ref, s, ssem, rsem, EX + 14 + 7 * s, sent) for s in (0, 1)]
    back = run(back)

    def planes(h):
        hc = halves[h]
        quarters = (slice(256 * h, 256 * h + 128), slice(256 * h + 128, 256 * h + 256))

        def pass_on(source, to, slot, cut=hc):
            ref = p_ref.at[rows24(source), cut]
            sent.append(send(ref, ref, ssem.at[ZA + 8 * h + slot], rsem.at[ZA + 8 * h + slot], tensor=(to + 8) % 8))

        def arrived(source, slot, cut=hc):
            wait_recv(p_ref.at[rows24(source + 8), cut], rsem.at[ZA + 8 * h + slot], tensor=(z + 1) % 8)

        total = part[rows24(z), hc]
        for i in reversed(order):
            wait_recv(zbuf.at[i, :, hc], rsem.at[ZP + 7 * h + i], tensor=zs[i])
            total = total + zbuf[i, :, hc]
        p_ref[rows24(z), hc] = total
        pass_on(z, z + 2, 2)
        pass_on(z, z - 2, 3)
        pass_on(z, z + 1, 0)
        pass_on(z, z - 1, 1)
        yield
        arrived(z - 2, 2)
        pass_on(z + 6, z + 2, 6, quarters[0])
        pass_on(z + 6, z + 1, 4)
        arrived(z + 2, 3)
        pass_on(z + 2, z - 2, 7, quarters[1])
        pass_on(z + 2, z - 1, 5)
        yield
        arrived(z - 1, 0)
        arrived(z + 1, 1)
        arrived(z - 3, 4)
        arrived(z + 3, 5)
        arrived(z - 4, 6, quarters[0])
        arrived(z - 4, 7, quarters[1])
        yield

    gathers = [planes(0), planes(1)]
    gathers = run(gathers)
    back = run(back)
    gathers = run(gathers)
    gathers = run(gathers)
    gbuf[...] = lax.dot_general(
        p_ref[:, pl.ds(pl.multiple_of(128 * (z // 2), 128), 128)], p_ref[...],
        (((0,), (0,)), ((), ())), precision=HI, preferred_element_type=F32,
    )
    half = 64 * (z % 2)
    away = gbuf.at[pl.ds(pl.multiple_of(half + 32 * (1 - core), 32), 32)]
    sent.append(send(away, cbuf, ssem.at[ZP + 14], rsem.at[ZP + 14], dp=sib))
    wait_recv(cbuf, rsem.at[ZP + 14], dp=sib)
    cbuf[...] += gbuf[pl.ds(pl.multiple_of(half + 32 * core, 32), 32), :]
    for i in range(3):
        sent.append(send(
            cbuf.at[pl.ds(pl.multiple_of(8 * xs[i], 8), 8)], xbuf.at[i], ssem.at[ZP + 15 + i], rsem.at[ZP + 15 + i],
            dp=dp_of(xs[i], y, core),
        ))
    total = cbuf[pl.ds(pl.multiple_of(8 * x, 8), 8), :]
    for i in range(3):
        wait_recv(xbuf.at[i], rsem.at[ZP + 15 + i], dp=sib)
        total = total + xbuf[i]
    ybuf[y] = total
    for i in range(3):
        sent.append(send(
            ybuf.at[y], ybuf.at[y], ssem.at[ZP + 18 + i], rsem.at[ZP + 18 + i], dp=dp_of(x, ys[i], core)
        ))
    for i in range(3):
        wait_recv(ybuf.at[(y + 3 - i) % 4], rsem.at[ZP + 18 + i], dp=sib)
    gram_ref[z, core, x] = (ybuf[0] + ybuf[1]) + (ybuf[2] + ybuf[3])
    mine = gram_ref.at[z, core, x]
    for i in order:
        sent.append(send(mine, mine, ssem.at[ZP + 21 + i], rsem.at[ZP + 21 + i], tensor=zs[i]))
    back = run(back)
    for i in reversed(order):
        wait_recv(gram_ref.at[(z + 7 - i) % 8, core, x], rsem.at[ZP + 21 + i], tensor=zs[i])
    cuts = (slice(0, 2), slice(2, 8))

    def along(j, i):
        mine = gram_ref.at[cuts[j], core, x]
        slot = GP + 7 * j + i
        return copy_to(mine, mine, ssem.at[slot], rsem.at[slot], dp=dp_of(xs[i], y, core))

    def across(j, i):
        there = gram_ref.at[cuts[j], core, x if i == 3 else (x + 3 - i) % 4]
        slot = GP + 7 * j + 3 + i
        return copy_to(there, there, ssem.at[slot], rsem.at[slot], dp=sib)

    def pass_rows(j):
        for i in range(3):
            wait_recv(gram_ref.at[cuts[j], core, (x + 3 - i) % 4], rsem.at[GP + 7 * j + i], dp=sib)
            across(j, i).start()

    def end_rows(j):
        for i in range(4):
            there = gram_ref.at[cuts[j], 1 - core, x if i == 3 else (x + 3 - i) % 4]
            wait_recv(there, rsem.at[GP + 7 * j + 3 + i], dp=sib)
            across(j, i).wait_send()

    for j in (0, 1):
        for i in range(3):
            copy = along(j, i)
            copy.start()
            sent.append(copy)
        across(j, 3).start()
    return pass_rows, end_rows


def chol_steps(pass_rows, end_rows, g_ref, p_ref, o_ref, s_ref, w_ref):
    n_p = p_ref.shape[0]
    s_ref[:, 512:512 + n_p] = p_ref[...].T
    s_ref[:, 512 + n_p:] = jnp.zeros((512, s_ref.shape[1] - 512 - n_p), F32)
    pass_rows(0)
    end_rows(0)
    s_ref[0:128, 0:512] = g_ref[0:2].reshape(128, 512)
    lane = lax.broadcasted_iota(jnp.int32, (8, 128), 1)
    sub = lax.broadcasted_iota(jnp.int32, (8, 128), 0)

    def lane_splat(v, j):
        return jnp.broadcast_to(v[:, j:j + 1], (8, 128))

    def row_splat(v, i):
        return jnp.broadcast_to(v[i:i + 1, :], (8, 128))

    def block(kb, carry):
        base = pl.multiple_of(kb * 128, 128)
        rest = s_ref[pl.ds(base, 128), pl.ds(base, 128)]
        for k in range(16):
            if k == 12:
                pl.when(kb == 0)(lambda: pass_rows(1))
            x = rest[0:8]
            below = rest[8:]
            inside = (lane >= 8 * k) & (lane < 8 * k + 8)
            c = [lane_splat(x, 8 * k + q) for q in range(8)]
            x = jnp.where(inside, (lane - 8 * k == sub).astype(F32), x)
            inv, up, rows = [], [], []
            scale = jnp.ones((8, 128), F32)
            for p in range(8):
                pd = row_splat(c[p], p)
                ip = 1.0 / pd
                scale = jnp.where(sub == p, lax.rsqrt(pd), scale)
                m = jnp.where(sub > p, c[p] * ip, 0.0)
                u = {}
                for q in range(p + 1, 8):
                    u[q] = c[q][p:p + 1]
                    c[q] = c[q] - (c[p] * row_splat(c[q], p)) * ip
                r = x[p:p + 1]
                x = x - m * r
                inv.append(ip[0:1])
                up.append(u)
                rows.append(r)
            w_ref[8 * k:8 * k + 8, :] = jnp.where(lane <= sub + 8 * k, x * scale, 0.0)
            if k < 15:
                n = below.shape[0]
                e = [jnp.broadcast_to(below[:, 8 * k + q:8 * k + q + 1], (n, 128)) for q in range(8)]
                below = jnp.where(inside[0:1], 0.0, below)
                for p in range(8):
                    m = e[p] * inv[p]
                    for q in range(p + 1, 8):
                        e[q] = e[q] - m * up[p][q]
                    below = below - m * rows[p]
                rest = below
        @pl.when(kb == 0)
        def _():
            end_rows(1)
            s_ref[128:512, 0:512] = g_ref[2:8].reshape(384, 512)

        rows_k = pl.ds(base, 128)
        s_ref[rows_k, :] = jnp.dot(w_ref[...], s_ref[rows_k, :], precision=HI, preferred_element_type=F32)
        for rb in range(1, 4):
            @pl.when(rb > kb)
            def _():
                ub = s_ref[rows_k, 128 * rb:128 * rb + 128]
                s_ref[128 * rb:128 * rb + 128, 128 * rb:] -= lax.dot_general(
                    ub, s_ref[rows_k, 128 * rb:], (((0,), (0,)), ((), ())), precision=HI,
                    preferred_element_type=F32,
                )
        return carry

    lax.fori_loop(0, 4, block, 0)
    o_ref[...] = s_ref[:, 512:512 + n_p].T


SPLIT = ((0, 96), (96, 80), (0, 176))


def coeff_steps(sent, call_out, csem, bt_ref, btsib_ref, o_ref, back_ref, std_ref, gain_ref, inv_ref,
                call_ref, cown_ref, csq_ref, ig_ref, gg_ref,
                osib, rhs, c_ref, sbuf, rbuf, acc, s2, r2, fin, fsib, agb,
                xsq, ysq, zsq, sqs, ngbuf, stat, gx, gy, gc, ssem, rsem, gs, gr, ns, nr):
    x, y, core, z = place()
    sib = dp_of(x, y, 1 - core)
    xs = [(x + d) % 4 for d in (1, 2, 3)]
    ys = [(y + d) % 4 for d in (1, 2, 3)]
    zs = [(z + d) % 8 for d in range(1, 8)]
    first = ("x", "y")

    def half(who):
        return pl.ds(pl.multiple_of(256 * who, 128), 256)

    sent.append(send(o_ref.at[:, half(1 - core)], osib, ssem.at[0], rsem.at[0], dp=sib))

    def input_grad():
        total = back_ref[z // 2, pl.ds(2 * (z % 2), 2)]
        for i in range(7):
            wait_recv(ngbuf.at[i], nr.at[i], tensor=zs[i])
            total = total + ngbuf[i]
        std = std_ref[...]
        gain = gain_ref[:, pl.ds(pl.multiple_of(768 * z, 128), 768)]
        scaled = total * jnp.stack([gain[:, 0:384], gain[:, 384:768]])
        lane = lax.broadcasted_iota(jnp.int32, (32, 128), 1)

        def per_token(v):
            return jnp.sum(jnp.sum(v, axis=0), axis=1, keepdims=True)

        stat[z] = jnp.where(lane < 64, per_token(scaled), per_token(scaled * std))
        for i in range(7):
            sent.append(send(stat.at[z], stat.at[z], ns.at[7 + i], nr.at[7 + i], tensor=zs[i]))
        gx[x] = jnp.broadcast_to(jnp.sum(total * std, axis=1, keepdims=True), gx.shape[1:])
        for i in range(3):
            sent.append(send(gx.at[x], gx.at[x], ns.at[14 + i], nr.at[14 + i], dp=dp_of(xs[i], y, core)))
        yield
        for i in range(3):
            wait_recv(gx.at[(x + 3 - i) % 4], nr.at[14 + i], dp=sib)
        gy[y] = (gx[0] + gx[1]) + (gx[2] + gx[3])
        for i in range(3):
            sent.append(send(gy.at[y], gy.at[y], ns.at[17 + i], nr.at[17 + i], dp=dp_of(x, ys[i], core)))
        for i in range(7):
            wait_recv(stat.at[(z + 7 - i) % 8], nr.at[7 + i], tensor=zs[i])
        sums = stat[0]
        for i in range(1, 8):
            sums = sums + stat[i]
        sums = sums * (1.0 / (16 * 384))
        full = inv_ref[...] * (scaled - sums[:, 0:1] - std * sums[:, 64:65])
        ig_ref[:, 0:384] = full[0].astype(BF16)
        ig_ref[:, 384:768] = full[1].astype(BF16)
        yield
        for i in range(3):
            wait_recv(gy.at[(y + 3 - i) % 4], nr.at[17 + i], dp=sib)
        gc[core] = (gy[0] + gy[1]) + (gy[2] + gy[3])
        sent.append(send(gc.at[core], gc.at[core], ns.at[20], nr.at[20], dp=sib))
        yield
        wait_recv(gc.at[1 - core], nr.at[20], dp=sib)
        gg_ref[:, 0:384] = gc[0, 0] + gc[1, 0]
        gg_ref[:, 384:768] = gc[0, 1] + gc[1, 1]
        yield

    tokens_side = input_grad()
    next(tokens_side)

    def fill(v):
        top, low = split(v)
        n = v.shape[0]
        rhs[0:n, 0:256] = top
        rhs[n:2 * n, 0:256] = top
        rhs[0:n, 256:512] = low
        rhs[n:2 * n, 256:512] = low

    cols = bt_ref.shape[0]
    fill(o_ref[:, half(core)])
    for t in range(0, cols, 384):
        two = jnp.dot(bt_ref[t:t + 384, :], rhs[...], preferred_element_type=F32)
        c_ref[t:t + 384, :] = two[:, 0:256] + two[:, 256:512]
    wait_recv(osib, rsem.at[0], dp=sib)
    fill(osib[...])
    for t in range(0, cols, 384):
        two = jnp.dot(btsib_ref[t:t + 384, :], rhs[...], preferred_element_type=F32)
        c_ref[t:t + 384, :] += two[:, 0:256] + two[:, 256:512]

    def cols_of(who, s):
        return pl.ds(pl.multiple_of(256 * who + 128 * s, 128), 128)

    a0 = (x, y)
    b0 = (y, x)

    def own(s, off, b):
        a = (a0[s] + off) % 4
        bx, by = (a, b) if s == 0 else (b, a)
        return c_ref[pl.ds(pl.multiple_of(168 * (bx * 4 + by), 8), 168), 128 * s:128 * s + 128]

    def dev(s, a, b):
        a, b = a % 4, b % 4
        return dp_of(a, b, core) if s == 0 else dp_of(b, a, core)

    zero_pad = jnp.zeros((8, 128), F32)

    def padded(v):
        return jnp.concatenate([v, zero_pad], axis=0).astype(BF16)

    def reduce_direct(s):
        base = 8 + 6 * s
        a, b = a0[s], b0[s]
        offs = (2, 1, 3)
        for i in range(3):
            for j in range(4):
                sbuf[s, i, j] = padded(own(s, offs[i], j))
            sent.append(send(
                sbuf.at[s, i], rbuf.at[s, i], ssem.at[base + i], rsem.at[base + i], dp=dev(s, a + offs[i], b)
            ))
            yield
        for j in range(4):
            acc[s, j] = own(s, 0, j)
        for i in (1, 2, 0):
            wait_recv(rbuf.at[s, i], rsem.at[base + i], dp=sib)
        yield

        def summed(off):
            j = (b + off) % 4
            return (acc[s, j] + rbuf[s, 0, j, 0:168].astype(F32)) + (
                rbuf[s, 1, j, 0:168].astype(F32) + rbuf[s, 2, j, 0:168].astype(F32)
            )

        for i in range(3):
            s2[s, i] = padded(summed(offs[i]))
            sent.append(send(
                s2.at[s, i], r2.at[s, i], ssem.at[base + 3 + i], rsem.at[base + 3 + i], dp=dev(s, a, b + offs[i])
            ))
        yield
        total = summed(0)
        for i in (1, 2, 0):
            wait_recv(r2.at[s, i], rsem.at[base + 3 + i], dp=sib)
            total = total + r2[s, i, 0:168].astype(F32)
        fin[:, 128 * s:128 * s + 128] = total
        agb[x * 4 + y, :, cols_of(core, s)] = padded(total)
        yield

    round_robin([reduce_direct(0), reduce_direct(1), tokens_side])

    def norms():
        v = fin[...]
        xsq[x] = jnp.broadcast_to(jnp.sum(v * v, axis=0, keepdims=True), (8, 256))
        for i in range(3):
            sent.append(send(xsq.at[x], xsq.at[x], ssem.at[25 + i], rsem.at[25 + i], dp=dp_of(xs[i], y, core)))
        sent.append(send(fin, fsib, ssem.at[24], rsem.at[24], dp=sib))
        yield
        yield
        for i in range(3):
            wait_recv(xsq.at[(x + 3 - i) % 4], rsem.at[25 + i], dp=sib)
        ysq[y] = (xsq[0] + xsq[1]) + (xsq[2] + xsq[3])
        for i in range(3):
            sent.append(send(ysq.at[y], ysq.at[y], ssem.at[28 + i], rsem.at[28 + i], dp=dp_of(x, ys[i], core)))
        yield
        yield
        for i in range(3):
            wait_recv(ysq.at[(y + 3 - i) % 4], rsem.at[28 + i], dp=sib)
        zsq[z] = (ysq[0] + ysq[1]) + (ysq[2] + ysq[3])
        for i in range(7):
            sent.append(send(zsq.at[z], zsq.at[z], ssem.at[31 + i], rsem.at[31 + i], tensor=zs[i]))
        yield
        yield
        for i in range(7):
            wait_recv(zsq.at[(z + 7 - i) % 8], rsem.at[31 + i], tensor=zs[i])
        total = zsq[0]
        for i in range(1, 8):
            total = total + zsq[i]
        sqs[core] = total
        sent.append(send(sqs.at[core], sqs.at[core], ssem.at[38], rsem.at[38], dp=sib))
        yield
        wait_recv(fsib, rsem.at[24], dp=sib)
        left = jnp.where(core == 0, fin[0:84], fsib[84:168])
        right = jnp.where(core == 0, fsib[0:84], fin[84:168])
        cown_ref[:, 0:256] = left
        cown_ref[:, 256:512] = right
        yield
        wait_recv(sqs.at[1 - core], rsem.at[38], dp=sib)
        csq_ref[:, 0:256] = sqs[0]
        csq_ref[:, 256:512] = sqs[1]
        yield

    def loc(s):
        def at(who, bx, by, part):
            lo, rows = SPLIT[part]
            return agb.at[bx * 4 + by, pl.ds(lo, rows), cols_of(who, s)]
        return at

    round_robin([
        norms(),
        gather_stream(loc(0), first[0], gs, gr, 0, sent),
        gather_stream(loc(1), first[1], gs, gr, GATHER_SLOTS, sent),
    ])
    outs = []
    for j in range(8):
        two = jnp.concatenate([agb[2 * j, 0:168].astype(F32), agb[2 * j + 1, 0:168].astype(F32)], axis=0)
        call_ref[336 * j:336 * j + 336, :] = two.astype(BF16)
        out = pltpu.make_async_copy(
            call_ref.at[336 * j:336 * j + 336], call_out.at[336 * j:336 * j + 336], csem.at[j]
        )
        out.start()
        outs.append(out)
    for out in outs:
        out.wait()


def whole_kernel(*refs):
    ins, refs = list(refs[:6]), refs[6:]
    buf_out, ortho, call_out, cown, csq, ig, gg = refs[:7]
    buf, weight, moment, local, call, csem = refs[7:13]
    refs = refs[13:]
    fetch = [
        pltpu.make_async_copy(ins[3], weight, local.at[0]),
        pltpu.make_async_copy(ins[4], moment, local.at[1]),
    ]
    for copy in fetch:
        copy.start()
    ins[3], ins[4] = weight, moment
    store = pltpu.make_async_copy(buf, buf_out, local.at[2])
    front_scratch, refs = refs[:29], refs[29:]
    s_scr, w_scr, refs = refs[0], refs[1], refs[2:]
    p, gram, bt, btsib, backall, stdz, inv = front_scratch[:7]
    x, y, core, z = place()
    greet([{"tensor": (z + d) % 8} for d in range(1, 8)] + plane_peers(x, y, core))
    sent = []
    pass_rows, end_rows = front_steps(sent, fetch, store, *ins, p, gram, bt, btsib, buf, backall, stdz, inv, *front_scratch[7:])
    ngbuf, ns, nr = refs[15], refs[-2], refs[-1]
    for i in (3, 4, 2, 5, 1, 6, 0):
        to = (z + 1 + i) % 8
        sent.append(send(backall.at[to // 2, pl.ds(2 * (to % 2), 2)], ngbuf.at[i], ns.at[i], nr.at[i], tensor=to))
    chol_steps(pass_rows, end_rows, gram, p, ortho, s_scr, w_scr)
    wait_recv(btsib, front_scratch[-1].at[OTHER + 2], dp=dp_of(x, y, 1 - core))
    store.wait()
    coeff_steps(sent, call_out, csem, bt, btsib, ortho, backall, stdz, ins[1], inv, call, cown, csq, ig, gg, *refs)
    for copy in sent:
        copy.wait_send()


def whole(inputs, gain, out_grad, weight, moment, right_basis):
    vm = pl.BlockSpec(memory_space=pltpu.VMEM)
    rows, cols = moment.shape
    tokens = inputs.shape[0]
    anywhere = pl.BlockSpec(memory_space=pl.ANY)
    block = (2, tokens, 384)

    def f32(*shape):
        return pltpu.VMEM(shape, F32)

    def bf16(*shape):
        return pltpu.VMEM(shape, BF16)

    dma = pltpu.SemaphoreType.DMA
    front_scratch = [
        f32(rows, RANK),
        f32(8, 2, 4, 8, RANK),
        bf16(cols, 2 * rows),
        bf16(cols, 2 * rows),
        f32(4, 4, tokens, 384),
        f32(*block),
        f32(tokens, 384),
        f32(cols, RANK),
        bf16(2, 16 * tokens, cols),
        f32(right_basis.shape[0], 256),
        f32(8, 2, tokens, 384),
        bf16(4, 4, tokens, 384),
        bf16(2, 4, 4, 16, 384),
        bf16(4, 4, tokens, 384),
        bf16(4, 4, tokens, 384),
        bf16(2, rows, 16 * tokens),
        bf16(2 * rows, cols),
        f32(2, 16 * tokens, 256),
        f32(16 * tokens, 256),
        f32(4, 4, tokens, 384),
        f32(2, 4, 4, 16, 384),
        f32(rows, RANK),
        f32(7, 24, RANK),
        f32(128, RANK),
        f32(32, RANK),
        f32(3, 8, RANK),
        f32(4, 8, RANK),
        dma((GP + 14,)),
        dma((GP + 14,)),
    ]
    chol_scratch = [f32(RANK, 768), f32(128, 128)]
    coeff_scratch = [
        f32(192, 256),
        bf16(384, RANK),
        f32(2688, 256),
        bf16(2, 3, 4, 176, 128),
        bf16(2, 3, 4, 176, 128),
        f32(2, 4, 168, 128),
        bf16(2, 3, 176, 128),
        bf16(2, 3, 176, 128),
        f32(168, 256),
        f32(168, 256),
        bf16(16, 176, RANK),
        f32(4, 8, 256),
        f32(4, 8, 256),
        f32(8, 8, 256),
        f32(2, 8, 256),
        f32(7, *block),
        f32(8, 32, 128),
        f32(4, 2, 8, 384),
        f32(4, 2, 8, 384),
        f32(2, 2, 8, 384),
        dma((39,)),
        dma((39,)),
        dma((2 * GATHER_SLOTS,)),
        dma((2 * GATHER_SLOTS,)),
        dma((21,)),
        dma((21,)),
    ]
    return pl.pallas_call(
        whole_kernel,
        out_shape=(
            jax.ShapeDtypeStruct((rows, cols), F32),
            jax.ShapeDtypeStruct((rows, RANK), F32),
            jax.ShapeDtypeStruct((cols, RANK), BF16),
            jax.ShapeDtypeStruct((84, RANK), F32),
            jax.ShapeDtypeStruct((8, RANK), F32),
            jax.ShapeDtypeStruct((tokens, 768), BF16),
            jax.ShapeDtypeStruct((8, 768), F32),
        ),
        in_specs=[vm, vm, vm, anywhere, anywhere, vm],
        out_specs=(anywhere, vm, anywhere, vm, vm, vm, vm),
        scratch_shapes=[
            f32(rows, cols), bf16(rows, cols), f32(rows, cols), dma((3,)), bf16(cols, RANK), dma((8,)),
        ] + front_scratch + chol_scratch + coeff_scratch,
        compiler_params=pltpu.CompilerParams(
            collective_id=1, has_side_effects=True, vmem_limit_bytes=VMEM_LIMIT
        ),
    )(inputs, gain, out_grad, weight, moment, right_basis)


def final_kernel(group, qkv_scale, mlp_scale, o_ref, csq_ref, c_ref, buf_ref, cown_ref, ig_ref, gg_ref,
                 mom_ref, upd_ref, basis_ref, igo_ref, ggo_ref, lhs):
    rows = o_ref.shape[0]
    step = pl.program_id(0)

    @pl.when(step == 0)
    def _():
        inv = 1.0 / (jnp.sqrt(csq_ref[0:1]) + 1e-08)
        o = o_ref[...]
        lhs[0:rows, :] = o.astype(BF16)
        top, low = split(o * inv)
        lhs[rows:2 * rows, :] = top
        lhs[2 * rows:3 * rows, :] = low
        basis_ref[...] = cown_ref[...] * inv
        igo_ref[...] = ig_ref[...]
        ggo_ref[...] = gg_ref[0]

    out = lax.dot_general(lhs[...], c_ref[...], (((1,), (1,)), ((), ())), preferred_element_type=F32)
    tile = out.shape[1]
    position = lax.broadcasted_iota(jnp.int32, (1, tile), 1) + step * tile
    scale = jnp.where(position < group, qkv_scale, mlp_scale)
    mom_ref[...] = buf_ref[...] - (1.0 - MOMENTUM) * out[0:rows]
    upd_ref[...] = (out[rows:2 * rows] + out[2 * rows:3 * rows]) * scale


def final_products(o, squares, coeffs, buffer, coeff_own, input_grad, gain_grad, *scales):
    rows, cols = buffer.shape
    tile = 896

    def all_of(v):
        return pl.BlockSpec(v.shape, lambda i: (0,) * v.ndim)

    by_col = pl.BlockSpec((rows, tile), lambda i: (0, i))
    gain_out = jax.ShapeDtypeStruct((gain_grad.shape[1],), F32)
    return pl.pallas_call(
        lambda *refs: final_kernel(*scales, *refs),
        grid=(cols // tile,),
        out_shape=(
            jax.ShapeDtypeStruct(buffer.shape, F32),
            jax.ShapeDtypeStruct(buffer.shape, F32),
            jax.ShapeDtypeStruct(coeff_own.shape, F32),
            jax.ShapeDtypeStruct(input_grad.shape, BF16),
            gain_out,
        ),
        in_specs=[
            all_of(o),
            all_of(squares),
            pl.BlockSpec((tile, RANK), lambda i: (i, 0)),
            by_col,
            all_of(coeff_own),
            all_of(input_grad),
            all_of(gain_grad),
        ],
        out_specs=(by_col, by_col, all_of(coeff_own), all_of(input_grad), all_of(gain_out)),
        scratch_shapes=[pltpu.VMEM((3 * rows, RANK), BF16)],
        compiler_params=pltpu.CompilerParams(vmem_limit_bytes=VMEM_LIMIT),
    )(o, squares, coeffs, buffer, coeff_own, input_grad, gain_grad)


def per_device(inputs, norm_gain, out_grad, weight, moment, right_basis):
    tensor_count = lax.axis_size("tensor")
    gain = norm_gain[None, :]
    buffer, ortho, coeffs, coeff_own, squares, input_grad, gain_grad = whole(
        inputs, gain, out_grad, weight, moment, right_basis
    )
    qkv_group = 3 * HEADS * HEAD_DIM // tensor_count
    qkv_scale = 0.2 * math.sqrt(D * (3 * HEADS * HEAD_DIM) / RANK)
    mlp_scale = 0.2 * math.sqrt(D * FF / RANK)
    moment_new, update, basis_new, input_grad, gain_grad = final_products(
        ortho, squares, coeffs, buffer, coeff_own, input_grad, gain_grad, qkv_group, qkv_scale, mlp_scale
    )
    return (input_grad, gain_grad, moment_new, basis_new, update)


def solution(mesh):
    in_specs = (
        P("dp", None),
        P(),
        P("dp", "tensor"),
        P("dp", "tensor"),
        P("dp", "tensor"),
        P(("tensor", "dp"), None),
    )
    out_specs = (
        P("dp", "tensor"),
        P("tensor"),
        P("dp", "tensor"),
        P(("tensor", "dp"), None),
        P("dp", "tensor"),
    )
    return jax.shard_map(
        per_device, mesh=mesh, in_specs=in_specs, out_specs=out_specs, check_vma=False
    )
```

```python
import math

import jax
import jax.numpy as jnp
from jax import lax
from jax.experimental import pallas as pl
from jax.experimental.pallas import tpu as pltpu
from jax.sharding import PartitionSpec as P

D = 6144
HEADS = 24
HEAD_DIM = 128
FF = 12288
RANK = 512
MOMENTUM = 0.8
NORM_EPSILON = 1e-06

HI = lax.Precision.HIGHEST
MESH = pl.DeviceIdType.MESH
VMEM_LIMIT = 56 * 1024 * 1024
F32 = jnp.float32
BF16 = jnp.bfloat16


def dp_of(x, y, core):
    return (x * 4 + y) * 2 + core


def place():
    dp = lax.axis_index("dp")
    return dp // 8, (dp // 2) % 4, dp % 2, lax.axis_index("tensor")


def copy_to(src, dst, send_sem, recv_sem, **peer):
    return pltpu.make_async_remote_copy(
        src_ref=src, dst_ref=dst, send_sem=send_sem, recv_sem=recv_sem,
        device_id=peer, device_id_type=MESH,
    )


def send(src, dst, send_sem, recv_sem, **peer):
    copy = copy_to(src, dst, send_sem, recv_sem, **peer)
    copy.start()
    return copy


def wait_recv(dst, recv_sem, **peer):
    pltpu.make_async_remote_copy(
        src_ref=dst, dst_ref=dst, send_sem=recv_sem, recv_sem=recv_sem,
        device_id=peer, device_id_type=MESH,
    ).wait_recv()


def greet(peers):
    barrier = pltpu.get_barrier_semaphore()
    for peer in peers:
        pl.semaphore_signal(barrier, inc=1, device_id=peer, device_id_type=MESH)
    pl.semaphore_wait(barrier, len(peers))


def plane_peers(x, y, core):
    return (
        [{"dp": dp_of((x + d) % 4, y, core)} for d in (1, 2, 3)]
        + [{"dp": dp_of(x, (y + d) % 4, core)} for d in (1, 2, 3)]
        + [{"dp": dp_of(x, y, 1 - core)}]
    )


def round_robin(generators):
    live = list(generators)
    while live:
        still = []
        for g in live:
            try:
                next(g)
                still.append(g)
            except StopIteration:
                pass
        live = still


def gather_stream(loc, first, ssem, rsem, base, sent):
    x0, y0, core, _ = place()
    a0, b0 = (x0, y0) if first == "x" else (y0, x0)
    sib = dp_of(x0, y0, 1 - core)

    def xy(a, b):
        return (a % 4, b % 4) if first == "x" else (b % 4, a % 4)

    def at(a, b, part, who=None):
        return loc(core if who is None else who, *xy(a, b), part)

    def to(a, b, block, part, slot):
        ref = at(*block, part)
        sent.append(send(ref, ref, ssem.at[base + slot], rsem.at[base + slot], dp=dp_of(*xy(a, b), core)))

    def got(block, part, slot):
        wait_recv(at(*block, part), rsem.at[base + slot], dp=sib)

    def share(block, slot):
        ref = at(*block, 2)
        sent.append(send(ref, ref, ssem.at[base + slot], rsem.at[base + slot], dp=sib))

    def spread(k, block):
        to(a0, b0 + 1, block, 2, 4 + 4 * k)
        to(a0, b0 - 1, block, 2, 5 + 4 * k)

    offs = (0, -1, 1, 2)
    to(a0 + 1, b0, (a0, b0), 2, 0)
    to(a0 - 1, b0, (a0, b0), 2, 1)
    yield
    spread(0, (a0, b0))
    share((a0, b0), 20)
    yield
    got((a0 - 1, b0), 2, 0)
    to(a0 + 1, b0, (a0 - 1, b0), 0, 2)
    got((a0 + 1, b0), 2, 1)
    to(a0 - 1, b0, (a0 + 1, b0), 1, 3)
    spread(1, (a0 - 1, b0))
    spread(2, (a0 + 1, b0))
    yield
    share((a0 - 1, b0), 21)
    share((a0 + 1, b0), 22)
    got((a0 + 2, b0), 0, 2)
    got((a0 + 2, b0), 1, 3)
    spread(3, (a0 + 2, b0))
    share((a0 + 2, b0), 23)
    yield
    for k in range(4):
        a = a0 + offs[k]
        got((a, b0 - 1), 2, 4 + 4 * k)
        to(a0, b0 + 1, (a, b0 - 1), 0, 6 + 4 * k)
        got((a, b0 + 1), 2, 5 + 4 * k)
        to(a0, b0 - 1, (a, b0 + 1), 1, 7 + 4 * k)
        share((a, b0 - 1), 24 + 3 * k)
        share((a, b0 + 1), 25 + 3 * k)
        yield
    for k in range(4):
        a = a0 + offs[k]
        got((a, b0 + 2), 0, 6 + 4 * k)
        got((a, b0 + 2), 1, 7 + 4 * k)
        share((a, b0 + 2), 26 + 3 * k)
        yield
    for k in range(4):
        a = a0 + offs[k]
        wait_recv(at(a, b0, 2, 1 - core), rsem.at[base + 20 + k], dp=sib)
        for j, b in enumerate((b0 - 1, b0 + 1, b0 + 2)):
            wait_recv(at(a, b, 2, 1 - core), rsem.at[base + 24 + 3 * k + j], dp=sib)
    yield


GATHER_SLOTS = 36
EXCHANGE_SLOTS = 6


def exchange_stream(src, mid, out, s, ssem, rsem, base, sent):
    x, y, core, _ = place()
    sib = dp_of(x, y, 1 - core)
    half = slice(16 * s, 16 * s + 16)

    def part(ref, a):
        return ref.at[a, :, half] if s == 0 else ref.at[:, a, half]

    def swapped(ref, b):
        return ref.at[:, b, half] if s == 0 else ref.at[b, :, half]

    a0, b0 = (x, y) if s == 0 else (y, x)

    def dev(a, b):
        return dp_of(a, b, core) if s == 0 else dp_of(b, a, core)

    mine = pltpu.make_async_copy(part(src, a0), mid.at[s, a0], ssem.at[base + 6])
    mine.start()
    for i in range(3):
        to = (a0 + 1 + i) % 4
        sent.append(send(part(src, to), mid.at[s, a0], ssem.at[base + i], rsem.at[base + i], dp=dev(to, b0)))
    yield
    for i in range(3):
        wait_recv(mid.at[s, (a0 + 3 - i) % 4], rsem.at[base + i], dp=sib)
    mine.wait()
    own = pltpu.make_async_copy(mid.at[s, :, b0], swapped(out, b0), ssem.at[base + 6])
    own.start()
    for i in range(3):
        to = (b0 + 1 + i) % 4
        sent.append(send(
            mid.at[s, :, to], swapped(out, b0), ssem.at[base + 3 + i], rsem.at[base + 3 + i], dp=dev(a0, to)
        ))
    yield
    own.wait()
    for i in range(3):
        wait_recv(swapped(out, (b0 + 3 - i) % 4), rsem.at[base + 3 + i], dp=sib)
    yield


def split(v):
    top = v.astype(BF16)
    return top, (v - top.astype(F32)).astype(BF16)


EX = 4 * GATHER_SLOTS
ZP = EX + 28
OTHER = ZP + 35
ZA = OTHER + 4
GP = ZA + 16


def front_steps(sent, fetch, store, in_ref, gain_ref, g_ref, w_ref, m_ref, r_ref,
                p_ref, gram_ref, bt_ref, btsib_ref, buf_ref, backall_ref, std_ref, inv_ref,
                rall, gall, got, std, nrm, exmid, exout, exsib, xt, both, bk, bksib, bsrc, bmid,
                part, zbuf, gbuf, cbuf, xbuf, ybuf, ssem, rsem):
    x, y, core, z = place()
    chip = x * 4 + y
    sib = dp_of(x, y, 1 - core)
    xs = [(x + d) % 4 for d in (1, 2, 3)]
    ys = [(y + d) % 4 for d in (1, 2, 3)]
    zs = [(z + d) % 8 for d in range(1, 8)]
    rows, cols = m_ref.shape
    tokens, width = in_ref.shape
    cut = 1408

    other = pl.multiple_of(256 * (1 - core), 128)
    sent.append(send(r_ref.at[:, pl.ds(other, 256)], got, ssem.at[OTHER], rsem.at[OTHER], dp=sib))
    gall[core, pl.ds(pl.multiple_of(32 * chip, 32), 32)] = g_ref[...]

    def loc_g(s):
        def loc(who, bx, by, part):
            lo, n = ((0, cut), (cut, cols - cut), (0, cols))[part]
            return gall.at[who, pl.ds(pl.multiple_of(32 * (bx * 4 + by) + 16 * s, 16), 16), pl.ds(lo, n)]
        return loc

    def loc_r(s):
        def loc(who, bx, by, part):
            lo, n = ((0, 88), (88, 80), (0, 168))[part]
            row = pl.multiple_of((bx * 4 + by) * 168 + lo, 8)
            return rall.at[pl.ds(row, n), pl.ds(pl.multiple_of(256 * who + 128 * s, 128), 128)]
        return loc

    g_streams = [gather_stream(loc_g(s), "xy"[s], ssem, rsem, (2 + s) * GATHER_SLOTS, sent) for s in (0, 1)]
    for g in g_streams:
        next(g)
    for g in g_streams:
        next(g)

    wide = [in_ref[:, 384 * b:384 * b + 384].astype(F32) for b in range(16)]
    mean = sum(jnp.sum(v, axis=1, keepdims=True) for v in wide) * (1.0 / width)
    centered = [in_ref[:, 384 * b:384 * b + 384].astype(F32) - mean for b in range(16)]
    var = sum(jnp.sum(v * v, axis=1, keepdims=True) for v in centered) * (1.0 / width)
    inv = lax.rsqrt(var + NORM_EPSILON)
    inv_ref[...] = jnp.broadcast_to(inv, inv_ref.shape)
    for b in range(16):
        v = (in_ref[:, 384 * b:384 * b + 384].astype(F32) - mean) * inv
        std[b // 2, b % 2] = v
        nrm[b // 4, b % 4] = (v * gain_ref[:, 384 * b:384 * b + 384]).astype(BF16)
    std_ref[...] = std[z]
    ex = [exchange_stream(nrm, exmid, exout, s, ssem, rsem, EX + 7 * s, sent) for s in (0, 1)]
    for g in ex:
        next(g)

    wait_recv(got, rsem.at[OTHER], dp=sib)
    mine = r_ref[:, pl.ds(pl.multiple_of(256 * core, 128), 256)]
    theirs = got[...]
    rall[pl.ds(pl.multiple_of(chip * 168, 8), 168), pl.ds(pl.multiple_of(256 * core, 128), 256)] = jnp.concatenate(
        [jnp.where(core == 0, mine, theirs), jnp.where(core == 0, theirs, mine)], axis=0
    )
    r_streams = [gather_stream(loc_r(s), "xy"[s], ssem, rsem, s * GATHER_SLOTS, sent) for s in (0, 1)]

    def run(gens):
        live = []
        for g in gens:
            try:
                next(g)
                live.append(g)
            except StopIteration:
                pass
        return live

    def mine192(v):
        return jnp.where(core == 0, v[:, 0:192].astype(F32), v[:, 192:384].astype(F32))

    def after_exchange():
        sent.append(send(exout, exsib, ssem.at[OTHER + 1], rsem.at[OTHER + 1], dp=sib))
        for q in range(4):
            v = exout[q].reshape(4 * tokens, 384)
            xt[core, :, 128 * q:128 * q + 128] = mine192(v).T.astype(BF16)
        yield
        wait_recv(exsib, rsem.at[OTHER + 1], dp=sib)
        for q in range(4):
            v = exsib[q].reshape(4 * tokens, 384)
            xt[1 - core, :, 128 * q:128 * q + 128] = mine192(v).T.astype(BF16)
        yield

    def compute():
        for copy in fetch:
            copy.wait()
        for t in range(0, cols, 384):
            acc = m_ref[:, t:t + 384]
            for c in (0, 1):
                acc = acc + jnp.dot(xt[c], gall[c, :, t:t + 384], preferred_element_type=F32)
            buf_ref[:, t:t + 384] = acc
            top, low = split(acc)
            both[0:rows, t:t + 384] = top
            both[rows:2 * rows, t:t + 384] = low
            yield
        store.start()

    bk[:, :, 128:256] = jnp.zeros((2, 512, 128), F32)
    tail = after_exchange()
    work = compute()
    r_live, g_live, x_live = r_streams, g_streams, ex
    r_live = run(r_live)
    tail_live = [tail]
    while g_live or x_live or tail_live:
        g_live = run(g_live)
        if x_live:
            x_live = run(x_live)
        elif tail_live:
            tail_live = run(tail_live)
        r_live = run(r_live)
    work_live = [work]
    while r_live or work_live:
        r_live = run(r_live)
        work_live = run(work_live)

    order = (3, 4, 2, 5, 1, 6, 0)

    def rows24(q):
        return pl.ds(pl.multiple_of(24 * (q % 8), 8), 24)

    halves = [slice(0, 256), slice(256, 512)]
    for h, hc in enumerate(halves):
        acc = jnp.zeros((rows, 256), F32)
        for t in range(0, cols, 384):
            r_top, r_low = split(rall[t:t + 384, hc])
            one = jnp.dot(both[:, t:t + 384], r_top, preferred_element_type=F32)
            two = jnp.dot(both[0:rows, t:t + 384], r_low, preferred_element_type=F32)
            acc = acc + (one[0:rows] + (one[rows:] + two))
        part[:, hc] = acc
        for i in order:
            sent.append(send(
                part.at[rows24(zs[i]), hc], zbuf.at[i, :, hc], ssem.at[ZP + 7 * h + i], rsem.at[ZP + 7 * h + i],
                tensor=zs[i],
            ))
    for c in (0, 1):
        for q in (0, 256):
            bk[c, q:q + 256, 0:192] = lax.dot_general(
                gall[c, q:q + 256, :], w_ref[...], (((1,), (1,)), ((), ())), preferred_element_type=F32
            )
    sent.append(send(bk.at[1 - core], bksib, ssem.at[OTHER + 3], rsem.at[OTHER + 3], dp=sib))
    for t in range(0, cols, 384):
        bt_ref[t:t + 384, :] = both[:, t:t + 384].astype(F32).T.astype(BF16)
    wait_recv(bksib, rsem.at[OTHER + 3], dp=sib)
    for q in range(4):
        ours = bk[core, 128 * q:128 * q + 128, 0:192]
        their = bksib[128 * q:128 * q + 128, 0:192]
        bsrc[q] = jnp.concatenate(
            [jnp.where(core == 0, ours, their), jnp.where(core == 0, their, ours)], axis=1
        ).reshape(4, tokens, 384)
    sent.append(send(bt_ref, btsib_ref, ssem.at[OTHER + 2], rsem.at[OTHER + 2], dp=sib))
    back = [exchange_stream(bsrc, bmid, backall_ref, s, ssem, rsem, EX + 14 + 7 * s, sent) for s in (0, 1)]
    back = run(back)

    def planes(h):
        hc = halves[h]
        quarters = (slice(256 * h, 256 * h + 128), slice(256 * h + 128, 256 * h + 256))

        def pass_on(source, to, slot, cut=hc):
            ref = p_ref.at[rows24(source), cut]
            sent.append(send(ref, ref, ssem.at[ZA + 8 * h + slot], rsem.at[ZA + 8 * h + slot], tensor=(to + 8) % 8))

        def arrived(source, slot, cut=hc):
            wait_recv(p_ref.at[rows24(source + 8), cut], rsem.at[ZA + 8 * h + slot], tensor=(z + 1) % 8)

        total = part[rows24(z), hc]
        for i in reversed(order):
            wait_recv(zbuf.at[i, :, hc], rsem.at[ZP + 7 * h + i], tensor=zs[i])
            total = total + zbuf[i, :, hc]
        p_ref[rows24(z), hc] = total
        pass_on(z, z + 2, 2)
        pass_on(z, z - 2, 3)
        pass_on(z, z + 1, 0)
        pass_on(z, z - 1, 1)
        yield
        arrived(z - 2, 2)
        pass_on(z + 6, z + 2, 6, quarters[0])
        pass_on(z + 6, z + 1, 4)
        arrived(z + 2, 3)
        pass_on(z + 2, z - 2, 7, quarters[1])
        pass_on(z + 2, z - 1, 5)
        yield
        arrived(z - 1, 0)
        arrived(z + 1, 1)
        arrived(z - 3, 4)
        arrived(z + 3, 5)
        arrived(z - 4, 6, quarters[0])
        arrived(z - 4, 7, quarters[1])
        yield

    gathers = [planes(0), planes(1)]
    gathers = run(gathers)
    back = run(back)
    gathers = run(gathers)
    gathers = run(gathers)
    gbuf[...] = lax.dot_general(
        p_ref[:, pl.ds(pl.multiple_of(128 * (z // 2), 128), 128)], p_ref[...],
        (((0,), (0,)), ((), ())), precision=HI, preferred_element_type=F32,
    )
    half = 64 * (z % 2)
    away = gbuf.at[pl.ds(pl.multiple_of(half + 32 * (1 - core), 32), 32)]
    sent.append(send(away, cbuf, ssem.at[ZP + 14], rsem.at[ZP + 14], dp=sib))
    wait_recv(cbuf, rsem.at[ZP + 14], dp=sib)
    cbuf[...] += gbuf[pl.ds(pl.multiple_of(half + 32 * core, 32), 32), :]
    for i in range(3):
        sent.append(send(
            cbuf.at[pl.ds(pl.multiple_of(8 * xs[i], 8), 8)], xbuf.at[i], ssem.at[ZP + 15 + i], rsem.at[ZP + 15 + i],
            dp=dp_of(xs[i], y, core),
        ))
    total = cbuf[pl.ds(pl.multiple_of(8 * x, 8), 8), :]
    for i in range(3):
        wait_recv(xbuf.at[i], rsem.at[ZP + 15 + i], dp=sib)
        total = total + xbuf[i]
    ybuf[y] = total
    for i in range(3):
        sent.append(send(
            ybuf.at[y], ybuf.at[y], ssem.at[ZP + 18 + i], rsem.at[ZP + 18 + i], dp=dp_of(x, ys[i], core)
        ))
    for i in range(3):
        wait_recv(ybuf.at[(y + 3 - i) % 4], rsem.at[ZP + 18 + i], dp=sib)
    gram_ref[z, core, x] = (ybuf[0] + ybuf[1]) + (ybuf[2] + ybuf[3])
    mine = gram_ref.at[z, core, x]
    for i in order:
        sent.append(send(mine, mine, ssem.at[ZP + 21 + i], rsem.at[ZP + 21 + i], tensor=zs[i]))
    back = run(back)
    for i in reversed(order):
        wait_recv(gram_ref.at[(z + 7 - i) % 8, core, x], rsem.at[ZP + 21 + i], tensor=zs[i])
    cuts = (slice(0, 2), slice(2, 8))

    def along(j, i):
        mine = gram_ref.at[cuts[j], core, x]
        slot = GP + 7 * j + i
        return copy_to(mine, mine, ssem.at[slot], rsem.at[slot], dp=dp_of(xs[i], y, core))

    def across(j, i):
        there = gram_ref.at[cuts[j], core, x if i == 3 else (x + 3 - i) % 4]
        slot = GP + 7 * j + 3 + i
        return copy_to(there, there, ssem.at[slot], rsem.at[slot], dp=sib)

    def pass_rows(j):
        for i in range(3):
            wait_recv(gram_ref.at[cuts[j], core, (x + 3 - i) % 4], rsem.at[GP + 7 * j + i], dp=sib)
            across(j, i).start()

    def end_rows(j):
        for i in range(4):
            there = gram_ref.at[cuts[j], 1 - core, x if i == 3 else (x + 3 - i) % 4]
            wait_recv(there, rsem.at[GP + 7 * j + 3 + i], dp=sib)
            across(j, i).wait_send()

    for j in (0, 1):
        for i in range(3):
            copy = along(j, i)
            copy.start()
            sent.append(copy)
        across(j, 3).start()
    return pass_rows, end_rows


def chol_steps(pass_rows, end_rows, g_ref, p_ref, o_ref, s_ref, w_ref):
    n_p = p_ref.shape[0]
    s_ref[:, 512:512 + n_p] = p_ref[...].T
    s_ref[:, 512 + n_p:] = jnp.zeros((512, s_ref.shape[1] - 512 - n_p), F32)
    pass_rows(0)
    end_rows(0)
    s_ref[0:128, 0:512] = g_ref[0:2].reshape(128, 512)
    lane = lax.broadcasted_iota(jnp.int32, (8, 128), 1)
    sub = lax.broadcasted_iota(jnp.int32, (8, 128), 0)

    def lane_splat(v, j):
        return jnp.broadcast_to(v[:, j:j + 1], (8, 128))

    def row_splat(v, i):
        return jnp.broadcast_to(v[i:i + 1, :], (8, 128))

    for kb in range(4):
        base = 128 * kb
        rest = s_ref[base:base + 128, base:base + 128]
        for k in range(16):
            if kb == 0 and k == 12:
                pass_rows(1)
            x = rest[0:8]
            below = rest[8:]
            inside = (lane >= 8 * k) & (lane < 8 * k + 8)
            c = [lane_splat(x, 8 * k + q) for q in range(8)]
            x = jnp.where(inside, (lane - 8 * k == sub).astype(F32), x)
            inv, up, rows = [], [], []
            scale = jnp.ones((8, 128), F32)
            for p in range(8):
                pd = row_splat(c[p], p)
                ip = 1.0 / pd
                scale = jnp.where(sub == p, lax.rsqrt(pd), scale)
                m = jnp.where(sub > p, c[p] * ip, 0.0)
                u = {}
                for q in range(p + 1, 8):
                    u[q] = c[q][p:p + 1]
                    c[q] = c[q] - (c[p] * row_splat(c[q], p)) * ip
                r = x[p:p + 1]
                x = x - m * r
                inv.append(ip[0:1])
                up.append(u)
                rows.append(r)
            w_ref[8 * k:8 * k + 8, :] = jnp.where(lane <= sub + 8 * k, x * scale, 0.0)
            if k < 15:
                n = below.shape[0]
                e = [jnp.broadcast_to(below[:, 8 * k + q:8 * k + q + 1], (n, 128)) for q in range(8)]
                below = jnp.where(inside[0:1], 0.0, below)
                for p in range(8):
                    m = e[p] * inv[p]
                    for q in range(p + 1, 8):
                        e[q] = e[q] - m * up[p][q]
                    below = below - m * rows[p]
                rest = below
        if kb == 0:
            end_rows(1)
            s_ref[128:512, 0:512] = g_ref[2:8].reshape(384, 512)
        s_ref[base:base + 128, base + 128:] = jnp.dot(
            w_ref[...], s_ref[base:base + 128, base + 128:], precision=HI, preferred_element_type=F32
        )
        if kb < 3:
            s_ref[base + 128:, base + 128:] -= lax.dot_general(
                s_ref[base:base + 128, base + 128:512], s_ref[base:base + 128, base + 128:],
                (((0,), (0,)), ((), ())), precision=HI, preferred_element_type=F32,
            )
    o_ref[...] = s_ref[:, 512:512 + n_p].T


SPLIT = ((0, 96), (96, 80), (0, 176))


def coeff_steps(sent, call_out, csem, bt_ref, btsib_ref, o_ref, back_ref, std_ref, gain_ref, inv_ref,
                call_ref, cown_ref, csq_ref, ig_ref, gg_ref,
                osib, rhs, c_ref, sbuf, rbuf, acc, s2, r2, fin, fsib, agb,
                xsq, ysq, zsq, sqs, ngbuf, stat, gx, gy, gc, ssem, rsem, gs, gr, ns, nr):
    x, y, core, z = place()
    sib = dp_of(x, y, 1 - core)
    xs = [(x + d) % 4 for d in (1, 2, 3)]
    ys = [(y + d) % 4 for d in (1, 2, 3)]
    zs = [(z + d) % 8 for d in range(1, 8)]
    first = ("x", "y")

    def half(who):
        return pl.ds(pl.multiple_of(256 * who, 128), 256)

    sent.append(send(o_ref.at[:, half(1 - core)], osib, ssem.at[0], rsem.at[0], dp=sib))

    def input_grad():
        total = back_ref[z // 2, pl.ds(2 * (z % 2), 2)]
        for i in range(7):
            wait_recv(ngbuf.at[i], nr.at[i], tensor=zs[i])
            total = total + ngbuf[i]
        std = std_ref[...]
        gain = gain_ref[:, pl.ds(pl.multiple_of(768 * z, 128), 768)]
        scaled = total * jnp.stack([gain[:, 0:384], gain[:, 384:768]])
        lane = lax.broadcasted_iota(jnp.int32, (32, 128), 1)

        def per_token(v):
            return jnp.sum(jnp.sum(v, axis=0), axis=1, keepdims=True)

        stat[z] = jnp.where(lane < 64, per_token(scaled), per_token(scaled * std))
        for i in range(7):
            sent.append(send(stat.at[z], stat.at[z], ns.at[7 + i], nr.at[7 + i], tensor=zs[i]))
        gx[x] = jnp.broadcast_to(jnp.sum(total * std, axis=1, keepdims=True), gx.shape[1:])
        for i in range(3):
            sent.append(send(gx.at[x], gx.at[x], ns.at[14 + i], nr.at[14 + i], dp=dp_of(xs[i], y, core)))
        yield
        for i in range(3):
            wait_recv(gx.at[(x + 3 - i) % 4], nr.at[14 + i], dp=sib)
        gy[y] = (gx[0] + gx[1]) + (gx[2] + gx[3])
        for i in range(3):
            sent.append(send(gy.at[y], gy.at[y], ns.at[17 + i], nr.at[17 + i], dp=dp_of(x, ys[i], core)))
        for i in range(7):
            wait_recv(stat.at[(z + 7 - i) % 8], nr.at[7 + i], tensor=zs[i])
        sums = stat[0]
        for i in range(1, 8):
            sums = sums + stat[i]
        sums = sums * (1.0 / (16 * 384))
        full = inv_ref[...] * (scaled - sums[:, 0:1] - std * sums[:, 64:65])
        ig_ref[:, 0:384] = full[0].astype(BF16)
        ig_ref[:, 384:768] = full[1].astype(BF16)
        yield
        for i in range(3):
            wait_recv(gy.at[(y + 3 - i) % 4], nr.at[17 + i], dp=sib)
        gc[core] = (gy[0] + gy[1]) + (gy[2] + gy[3])
        sent.append(send(gc.at[core], gc.at[core], ns.at[20], nr.at[20], dp=sib))
        yield
        wait_recv(gc.at[1 - core], nr.at[20], dp=sib)
        gg_ref[:, 0:384] = gc[0, 0] + gc[1, 0]
        gg_ref[:, 384:768] = gc[0, 1] + gc[1, 1]
        yield

    tokens_side = input_grad()

    def begin_tokens():
        for _ in range(2):
            yield
        next(tokens_side)
        yield

    def fill(v):
        top, low = split(v)
        n = v.shape[0]
        rhs[0:n, 0:256] = top
        rhs[n:2 * n, 0:256] = top
        rhs[0:n, 256:512] = low
        rhs[n:2 * n, 256:512] = low

    cols = bt_ref.shape[0]
    fill(o_ref[:, half(core)])
    for t in range(0, cols, 384):
        two = jnp.dot(bt_ref[t:t + 384, :], rhs[...], preferred_element_type=F32)
        c_ref[t:t + 384, :] = two[:, 0:256] + two[:, 256:512]
    wait_recv(osib, rsem.at[0], dp=sib)
    fill(osib[...])
    for t in range(0, cols, 384):
        two = jnp.dot(btsib_ref[t:t + 384, :], rhs[...], preferred_element_type=F32)
        c_ref[t:t + 384, :] += two[:, 0:256] + two[:, 256:512]

    def cols_of(who, s):
        return pl.ds(pl.multiple_of(256 * who + 128 * s, 128), 128)

    a0 = (x, y)
    b0 = (y, x)

    def own(s, off, b):
        a = (a0[s] + off) % 4
        bx, by = (a, b) if s == 0 else (b, a)
        return c_ref[pl.ds(pl.multiple_of(168 * (bx * 4 + by), 8), 168), 128 * s:128 * s + 128]

    def dev(s, a, b):
        a, b = a % 4, b % 4
        return dp_of(a, b, core) if s == 0 else dp_of(b, a, core)

    zero_pad = jnp.zeros((8, 128), F32)

    def padded(v):
        return jnp.concatenate([v, zero_pad], axis=0).astype(BF16)

    def reduce_direct(s):
        base = 8 + 6 * s
        a, b = a0[s], b0[s]
        offs = (2, 1, 3)
        for i in range(3):
            for j in range(4):
                sbuf[s, i, j] = padded(own(s, offs[i], j))
            sent.append(send(
                sbuf.at[s, i], rbuf.at[s, i], ssem.at[base + i], rsem.at[base + i], dp=dev(s, a + offs[i], b)
            ))
            yield
        for j in range(4):
            acc[s, j] = own(s, 0, j)
        for i in (1, 2, 0):
            wait_recv(rbuf.at[s, i], rsem.at[base + i], dp=sib)
        yield

        def summed(off):
            j = (b + off) % 4
            return (acc[s, j] + rbuf[s, 0, j, 0:168].astype(F32)) + (
                rbuf[s, 1, j, 0:168].astype(F32) + rbuf[s, 2, j, 0:168].astype(F32)
            )

        for i in range(3):
            s2[s, i] = padded(summed(offs[i]))
            sent.append(send(
                s2.at[s, i], r2.at[s, i], ssem.at[base + 3 + i], rsem.at[base + 3 + i], dp=dev(s, a, b + offs[i])
            ))
        yield
        total = summed(0)
        for i in (1, 2, 0):
            wait_recv(r2.at[s, i], rsem.at[base + 3 + i], dp=sib)
            total = total + r2[s, i, 0:168].astype(F32)
        fin[:, 128 * s:128 * s + 128] = total
        agb[x * 4 + y, :, cols_of(core, s)] = padded(total)
        yield

    round_robin([reduce_direct(0), reduce_direct(1), begin_tokens()])

    def norms():
        v = fin[...]
        xsq[x] = jnp.broadcast_to(jnp.sum(v * v, axis=0, keepdims=True), (8, 256))
        for i in range(3):
            sent.append(send(xsq.at[x], xsq.at[x], ssem.at[25 + i], rsem.at[25 + i], dp=dp_of(xs[i], y, core)))
        sent.append(send(fin, fsib, ssem.at[24], rsem.at[24], dp=sib))
        yield
        yield
        for i in range(3):
            wait_recv(xsq.at[(x + 3 - i) % 4], rsem.at[25 + i], dp=sib)
        ysq[y] = (xsq[0] + xsq[1]) + (xsq[2] + xsq[3])
        for i in range(3):
            sent.append(send(ysq.at[y], ysq.at[y], ssem.at[28 + i], rsem.at[28 + i], dp=dp_of(x, ys[i], core)))
        yield
        yield
        for i in range(3):
            wait_recv(ysq.at[(y + 3 - i) % 4], rsem.at[28 + i], dp=sib)
        zsq[z] = (ysq[0] + ysq[1]) + (ysq[2] + ysq[3])
        for i in range(7):
            sent.append(send(zsq.at[z], zsq.at[z], ssem.at[31 + i], rsem.at[31 + i], tensor=zs[i]))
        yield
        yield
        for i in range(7):
            wait_recv(zsq.at[(z + 7 - i) % 8], rsem.at[31 + i], tensor=zs[i])
        total = zsq[0]
        for i in range(1, 8):
            total = total + zsq[i]
        sqs[core] = total
        sent.append(send(sqs.at[core], sqs.at[core], ssem.at[38], rsem.at[38], dp=sib))
        yield
        wait_recv(fsib, rsem.at[24], dp=sib)
        left = jnp.where(core == 0, fin[0:84], fsib[84:168])
        right = jnp.where(core == 0, fsib[0:84], fin[84:168])
        cown_ref[:, 0:256] = left
        cown_ref[:, 256:512] = right
        yield
        wait_recv(sqs.at[1 - core], rsem.at[38], dp=sib)
        csq_ref[:, 0:256] = sqs[0]
        csq_ref[:, 256:512] = sqs[1]
        yield

    def loc(s):
        def at(who, bx, by, part):
            lo, rows = SPLIT[part]
            return agb.at[bx * 4 + by, pl.ds(lo, rows), cols_of(who, s)]
        return at

    round_robin([
        gather_stream(loc(0), first[0], gs, gr, 0, sent),
        gather_stream(loc(1), first[1], gs, gr, GATHER_SLOTS, sent),
        norms(),
        tokens_side,
    ])
    outs = []
    for j in range(8):
        two = jnp.concatenate([agb[2 * j, 0:168].astype(F32), agb[2 * j + 1, 0:168].astype(F32)], axis=0)
        call_ref[336 * j:336 * j + 336, :] = two.astype(BF16)
        out = pltpu.make_async_copy(
            call_ref.at[336 * j:336 * j + 336], call_out.at[336 * j:336 * j + 336], csem.at[j]
        )
        out.start()
        outs.append(out)
    for out in outs:
        out.wait()


def whole_kernel(*refs):
    ins, refs = list(refs[:6]), refs[6:]
    buf_out, ortho, call_out, cown, csq, ig, gg = refs[:7]
    buf, weight, moment, local, call, csem = refs[7:13]
    refs = refs[13:]
    fetch = [
        pltpu.make_async_copy(ins[3], weight, local.at[0]),
        pltpu.make_async_copy(ins[4], moment, local.at[1]),
    ]
    for copy in fetch:
        copy.start()
    ins[3], ins[4] = weight, moment
    store = pltpu.make_async_copy(buf, buf_out, local.at[2])
    front_scratch, refs = refs[:29], refs[29:]
    s_scr, w_scr, refs = refs[0], refs[1], refs[2:]
    p, gram, bt, btsib, backall, stdz, inv = front_scratch[:7]
    x, y, core, z = place()
    greet([{"tensor": (z + d) % 8} for d in range(1, 8)] + plane_peers(x, y, core))
    sent = []
    pass_rows, end_rows = front_steps(sent, fetch, store, *ins, p, gram, bt, btsib, buf, backall, stdz, inv, *front_scratch[7:])
    ngbuf, ns, nr = refs[15], refs[-2], refs[-1]
    for i in (3, 4, 2, 5, 1, 6, 0):
        to = (z + 1 + i) % 8
        sent.append(send(backall.at[to // 2, pl.ds(2 * (to % 2), 2)], ngbuf.at[i], ns.at[i], nr.at[i], tensor=to))
    chol_steps(pass_rows, end_rows, gram, p, ortho, s_scr, w_scr)
    wait_recv(btsib, front_scratch[-1].at[OTHER + 2], dp=dp_of(x, y, 1 - core))
    store.wait()
    coeff_steps(sent, call_out, csem, bt, btsib, ortho, backall, stdz, ins[1], inv, call, cown, csq, ig, gg, *refs)
    for copy in sent:
        copy.wait_send()


def whole(inputs, gain, out_grad, weight, moment, right_basis):
    vm = pl.BlockSpec(memory_space=pltpu.VMEM)
    rows, cols = moment.shape
    tokens = inputs.shape[0]
    anywhere = pl.BlockSpec(memory_space=pl.ANY)
    block = (2, tokens, 384)

    def f32(*shape):
        return pltpu.VMEM(shape, F32)

    def bf16(*shape):
        return pltpu.VMEM(shape, BF16)

    dma = pltpu.SemaphoreType.DMA
    front_scratch = [
        f32(rows, RANK),
        f32(8, 2, 4, 8, RANK),
        bf16(cols, 2 * rows),
        bf16(cols, 2 * rows),
        f32(4, 4, tokens, 384),
        f32(*block),
        f32(tokens, 384),
        f32(cols, RANK),
        bf16(2, 16 * tokens, cols),
        f32(right_basis.shape[0], 256),
        f32(8, 2, tokens, 384),
        bf16(4, 4, tokens, 384),
        bf16(2, 4, 4, 16, 384),
        bf16(4, 4, tokens, 384),
        bf16(4, 4, tokens, 384),
        bf16(2, rows, 16 * tokens),
        bf16(2 * rows, cols),
        f32(2, 16 * tokens, 256),
        f32(16 * tokens, 256),
        f32(4, 4, tokens, 384),
        f32(2, 4, 4, 16, 384),
        f32(rows, RANK),
        f32(7, 24, RANK),
        f32(128, RANK),
        f32(32, RANK),
        f32(3, 8, RANK),
        f32(4, 8, RANK),
        dma((GP + 14,)),
        dma((GP + 14,)),
    ]
    chol_scratch = [f32(RANK, 768), f32(128, 128)]
    coeff_scratch = [
        f32(192, 256),
        bf16(384, RANK),
        f32(2688, 256),
        bf16(2, 3, 4, 176, 128),
        bf16(2, 3, 4, 176, 128),
        f32(2, 4, 168, 128),
        bf16(2, 3, 176, 128),
        bf16(2, 3, 176, 128),
        f32(168, 256),
        f32(168, 256),
        bf16(16, 176, RANK),
        f32(4, 8, 256),
        f32(4, 8, 256),
        f32(8, 8, 256),
        f32(2, 8, 256),
        f32(7, *block),
        f32(8, 32, 128),
        f32(4, 2, 8, 384),
        f32(4, 2, 8, 384),
        f32(2, 2, 8, 384),
        dma((39,)),
        dma((39,)),
        dma((2 * GATHER_SLOTS,)),
        dma((2 * GATHER_SLOTS,)),
        dma((21,)),
        dma((21,)),
    ]
    return pl.pallas_call(
        whole_kernel,
        out_shape=(
            jax.ShapeDtypeStruct((rows, cols), F32),
            jax.ShapeDtypeStruct((rows, RANK), F32),
            jax.ShapeDtypeStruct((cols, RANK), BF16),
            jax.ShapeDtypeStruct((84, RANK), F32),
            jax.ShapeDtypeStruct((8, RANK), F32),
            jax.ShapeDtypeStruct((tokens, 768), BF16),
            jax.ShapeDtypeStruct((8, 768), F32),
        ),
        in_specs=[vm, vm, vm, anywhere, anywhere, vm],
        out_specs=(anywhere, vm, anywhere, vm, vm, vm, vm),
        scratch_shapes=[
            f32(rows, cols), bf16(rows, cols), f32(rows, cols), dma((3,)), bf16(cols, RANK), dma((8,)),
        ] + front_scratch + chol_scratch + coeff_scratch,
        compiler_params=pltpu.CompilerParams(
            collective_id=1, has_side_effects=True, vmem_limit_bytes=VMEM_LIMIT
        ),
    )(inputs, gain, out_grad, weight, moment, right_basis)


def final_kernel(group, qkv_scale, mlp_scale, o_ref, csq_ref, c_ref, buf_ref, cown_ref, ig_ref, gg_ref,
                 mom_ref, upd_ref, basis_ref, igo_ref, ggo_ref, lhs):
    rows = o_ref.shape[0]
    step = pl.program_id(0)

    @pl.when(step == 0)
    def _():
        inv = 1.0 / (jnp.sqrt(csq_ref[0:1]) + 1e-08)
        o = o_ref[...]
        lhs[0:rows, :] = o.astype(BF16)
        top, low = split(o * inv)
        lhs[rows:2 * rows, :] = top
        lhs[2 * rows:3 * rows, :] = low
        basis_ref[...] = cown_ref[...] * inv
        igo_ref[...] = ig_ref[...]
        ggo_ref[...] = gg_ref[0]

    out = lax.dot_general(lhs[...], c_ref[...], (((1,), (1,)), ((), ())), preferred_element_type=F32)
    tile = out.shape[1]
    position = lax.broadcasted_iota(jnp.int32, (1, tile), 1) + step * tile
    scale = jnp.where(position < group, qkv_scale, mlp_scale)
    mom_ref[...] = buf_ref[...] - (1.0 - MOMENTUM) * out[0:rows]
    upd_ref[...] = (out[rows:2 * rows] + out[2 * rows:3 * rows]) * scale


def final_products(o, squares, coeffs, buffer, coeff_own, input_grad, gain_grad, *scales):
    rows, cols = buffer.shape
    tile = 896

    def all_of(v):
        return pl.BlockSpec(v.shape, lambda i: (0,) * v.ndim)

    by_col = pl.BlockSpec((rows, tile), lambda i: (0, i))
    gain_out = jax.ShapeDtypeStruct((gain_grad.shape[1],), F32)
    return pl.pallas_call(
        lambda *refs: final_kernel(*scales, *refs),
        grid=(cols // tile,),
        out_shape=(
            jax.ShapeDtypeStruct(buffer.shape, F32),
            jax.ShapeDtypeStruct(buffer.shape, F32),
            jax.ShapeDtypeStruct(coeff_own.shape, F32),
            jax.ShapeDtypeStruct(input_grad.shape, BF16),
            gain_out,
        ),
        in_specs=[
            all_of(o),
            all_of(squares),
            pl.BlockSpec((tile, RANK), lambda i: (i, 0)),
            by_col,
            all_of(coeff_own),
            all_of(input_grad),
            all_of(gain_grad),
        ],
        out_specs=(by_col, by_col, all_of(coeff_own), all_of(input_grad), all_of(gain_out)),
        scratch_shapes=[pltpu.VMEM((3 * rows, RANK), BF16)],
        compiler_params=pltpu.CompilerParams(vmem_limit_bytes=VMEM_LIMIT),
    )(o, squares, coeffs, buffer, coeff_own, input_grad, gain_grad)


def per_device(inputs, norm_gain, out_grad, weight, moment, right_basis):
    tensor_count = lax.axis_size("tensor")
    gain = norm_gain[None, :]
    buffer, ortho, coeffs, coeff_own, squares, input_grad, gain_grad = whole(
        inputs, gain, out_grad, weight, moment, right_basis
    )
    qkv_group = 3 * HEADS * HEAD_DIM // tensor_count
    qkv_scale = 0.2 * math.sqrt(D * (3 * HEADS * HEAD_DIM) / RANK)
    mlp_scale = 0.2 * math.sqrt(D * FF / RANK)
    moment_new, update, basis_new, input_grad, gain_grad = final_products(
        ortho, squares, coeffs, buffer, coeff_own, input_grad, gain_grad, qkv_group, qkv_scale, mlp_scale
    )
    return (input_grad, gain_grad, moment_new, basis_new, update)


def solution(mesh):
    in_specs = (
        P("dp", None),
        P(),
        P("dp", "tensor"),
        P("dp", "tensor"),
        P("dp", "tensor"),
        P(("tensor", "dp"), None),
    )
    out_specs = (
        P("dp", "tensor"),
        P("tensor"),
        P("dp", "tensor"),
        P(("tensor", "dp"), None),
        P("dp", "tensor"),
    )
    return jax.shard_map(
        per_device, mesh=mesh, in_specs=in_specs, out_specs=out_specs, check_vma=False
    )
```

```python
import math

import jax
import jax.numpy as jnp
from jax import lax
from jax.experimental import pallas as pl
from jax.experimental.pallas import tpu as pltpu
from jax.sharding import PartitionSpec as P

D = 6144
HEADS = 24
HEAD_DIM = 128
FF = 12288
RANK = 512
MOMENTUM = 0.8
NORM_EPSILON = 1e-06

HI = lax.Precision.HIGHEST
MESH = pl.DeviceIdType.MESH
VMEM_LIMIT = 56 * 1024 * 1024
F32 = jnp.float32
BF16 = jnp.bfloat16


def dp_of(x, y, core):
    return (x * 4 + y) * 2 + core


def place():
    dp = lax.axis_index("dp")
    return dp // 8, (dp // 2) % 4, dp % 2, lax.axis_index("tensor")


def copy_to(src, dst, send_sem, recv_sem, **peer):
    return pltpu.make_async_remote_copy(
        src_ref=src, dst_ref=dst, send_sem=send_sem, recv_sem=recv_sem,
        device_id=peer, device_id_type=MESH,
    )


def send(src, dst, send_sem, recv_sem, **peer):
    copy = copy_to(src, dst, send_sem, recv_sem, **peer)
    copy.start()
    return copy


def wait_recv(dst, recv_sem, **peer):
    pltpu.make_async_remote_copy(
        src_ref=dst, dst_ref=dst, send_sem=recv_sem, recv_sem=recv_sem,
        device_id=peer, device_id_type=MESH,
    ).wait_recv()


def greet(peers):
    barrier = pltpu.get_barrier_semaphore()
    for peer in peers:
        pl.semaphore_signal(barrier, inc=1, device_id=peer, device_id_type=MESH)
    pl.semaphore_wait(barrier, len(peers))


def plane_peers(x, y, core):
    return (
        [{"dp": dp_of((x + d) % 4, y, core)} for d in (1, 2, 3)]
        + [{"dp": dp_of(x, (y + d) % 4, core)} for d in (1, 2, 3)]
        + [{"dp": dp_of(x, y, 1 - core)}]
    )


def round_robin(generators):
    live = list(generators)
    while live:
        still = []
        for g in live:
            try:
                next(g)
                still.append(g)
            except StopIteration:
                pass
        live = still


def gather_stream(loc, first, ssem, rsem, base, sent):
    x0, y0, core, _ = place()
    a0, b0 = (x0, y0) if first == "x" else (y0, x0)
    sib = dp_of(x0, y0, 1 - core)

    def xy(a, b):
        return (a % 4, b % 4) if first == "x" else (b % 4, a % 4)

    def at(a, b, part, who=None):
        return loc(core if who is None else who, *xy(a, b), part)

    def to(a, b, block, part, slot):
        ref = at(*block, part)
        sent.append(send(ref, ref, ssem.at[base + slot], rsem.at[base + slot], dp=dp_of(*xy(a, b), core)))

    def got(block, part, slot):
        wait_recv(at(*block, part), rsem.at[base + slot], dp=sib)

    def share(block, slot):
        ref = at(*block, 2)
        sent.append(send(ref, ref, ssem.at[base + slot], rsem.at[base + slot], dp=sib))

    def spread(k, block):
        to(a0, b0 + 1, block, 2, 4 + 4 * k)
        to(a0, b0 - 1, block, 2, 5 + 4 * k)

    offs = (0, -1, 1, 2)
    to(a0 + 1, b0, (a0, b0), 2, 0)
    to(a0 - 1, b0, (a0, b0), 2, 1)
    yield
    spread(0, (a0, b0))
    share((a0, b0), 20)
    yield
    got((a0 - 1, b0), 2, 0)
    to(a0 + 1, b0, (a0 - 1, b0), 0, 2)
    got((a0 + 1, b0), 2, 1)
    to(a0 - 1, b0, (a0 + 1, b0), 1, 3)
    spread(1, (a0 - 1, b0))
    spread(2, (a0 + 1, b0))
    yield
    share((a0 - 1, b0), 21)
    share((a0 + 1, b0), 22)
    got((a0 + 2, b0), 0, 2)
    got((a0 + 2, b0), 1, 3)
    spread(3, (a0 + 2, b0))
    share((a0 + 2, b0), 23)
    yield
    for k in range(4):
        a = a0 + offs[k]
        got((a, b0 - 1), 2, 4 + 4 * k)
        to(a0, b0 + 1, (a, b0 - 1), 0, 6 + 4 * k)
        got((a, b0 + 1), 2, 5 + 4 * k)
        to(a0, b0 - 1, (a, b0 + 1), 1, 7 + 4 * k)
        share((a, b0 - 1), 24 + 3 * k)
        share((a, b0 + 1), 25 + 3 * k)
        yield
    for k in range(4):
        a = a0 + offs[k]
        got((a, b0 + 2), 0, 6 + 4 * k)
        got((a, b0 + 2), 1, 7 + 4 * k)
        share((a, b0 + 2), 26 + 3 * k)
        yield
    for k in range(4):
        a = a0 + offs[k]
        wait_recv(at(a, b0, 2, 1 - core), rsem.at[base + 20 + k], dp=sib)
        for j, b in enumerate((b0 - 1, b0 + 1, b0 + 2)):
            wait_recv(at(a, b, 2, 1 - core), rsem.at[base + 24 + 3 * k + j], dp=sib)
    yield


GATHER_SLOTS = 36
EXCHANGE_SLOTS = 6


def exchange_stream(src, mid, out, s, ssem, rsem, base, sent):
    x, y, core, _ = place()
    sib = dp_of(x, y, 1 - core)
    half = slice(16 * s, 16 * s + 16)

    def part(ref, a):
        return ref.at[a, :, half] if s == 0 else ref.at[:, a, half]

    def swapped(ref, b):
        return ref.at[:, b, half] if s == 0 else ref.at[b, :, half]

    a0, b0 = (x, y) if s == 0 else (y, x)

    def dev(a, b):
        return dp_of(a, b, core) if s == 0 else dp_of(b, a, core)

    mine = pltpu.make_async_copy(part(src, a0), mid.at[s, a0], ssem.at[base + 6])
    mine.start()
    for i in range(3):
        to = (a0 + 1 + i) % 4
        sent.append(send(part(src, to), mid.at[s, a0], ssem.at[base + i], rsem.at[base + i], dp=dev(to, b0)))
    yield
    for i in range(3):
        wait_recv(mid.at[s, (a0 + 3 - i) % 4], rsem.at[base + i], dp=sib)
    mine.wait()
    own = pltpu.make_async_copy(mid.at[s, :, b0], swapped(out, b0), ssem.at[base + 6])
    own.start()
    for i in range(3):
        to = (b0 + 1 + i) % 4
        sent.append(send(
            mid.at[s, :, to], swapped(out, b0), ssem.at[base + 3 + i], rsem.at[base + 3 + i], dp=dev(a0, to)
        ))
    yield
    own.wait()
    for i in range(3):
        wait_recv(swapped(out, (b0 + 3 - i) % 4), rsem.at[base + 3 + i], dp=sib)
    yield


def split(v):
    top = v.astype(BF16)
    return top, (v - top.astype(F32)).astype(BF16)


EX = 4 * GATHER_SLOTS
ZP = EX + 28
OTHER = ZP + 35
ZA = OTHER + 4
GP = ZA + 16


def front_steps(sent, fetch, store, in_ref, gain_ref, g_ref, w_ref, m_ref, r_ref,
                p_ref, gram_ref, bt_ref, btsib_ref, buf_ref, backall_ref, std_ref, inv_ref,
                rall, gall, got, std, nrm, exmid, exout, exsib, xt, both, bk, bksib, bsrc, bmid,
                part, zbuf, gbuf, cbuf, xbuf, ybuf, ssem, rsem):
    x, y, core, z = place()
    chip = x * 4 + y
    sib = dp_of(x, y, 1 - core)
    xs = [(x + d) % 4 for d in (1, 2, 3)]
    ys = [(y + d) % 4 for d in (1, 2, 3)]
    zs = [(z + d) % 8 for d in range(1, 8)]
    rows, cols = m_ref.shape
    tokens, width = in_ref.shape
    cut = 1408

    other = pl.multiple_of(256 * (1 - core), 128)
    sent.append(send(r_ref.at[:, pl.ds(other, 256)], got, ssem.at[OTHER], rsem.at[OTHER], dp=sib))
    gall[core, pl.ds(pl.multiple_of(32 * chip, 32), 32)] = g_ref[...]

    def loc_g(s):
        def loc(who, bx, by, part):
            lo, n = ((0, cut), (cut, cols - cut), (0, cols))[part]
            return gall.at[who, pl.ds(pl.multiple_of(32 * (bx * 4 + by) + 16 * s, 16), 16), pl.ds(lo, n)]
        return loc

    def loc_r(s):
        def loc(who, bx, by, part):
            lo, n = ((0, 88), (88, 80), (0, 168))[part]
            row = pl.multiple_of((bx * 4 + by) * 168 + lo, 8)
            return rall.at[pl.ds(row, n), pl.ds(pl.multiple_of(256 * who + 128 * s, 128), 128)]
        return loc

    g_streams = [gather_stream(loc_g(s), "xy"[s], ssem, rsem, (2 + s) * GATHER_SLOTS, sent) for s in (0, 1)]
    for g in g_streams:
        next(g)
    for g in g_streams:
        next(g)

    wide = [in_ref[:, 384 * b:384 * b + 384].astype(F32) for b in range(16)]
    mean = sum(jnp.sum(v, axis=1, keepdims=True) for v in wide) * (1.0 / width)
    centered = [in_ref[:, 384 * b:384 * b + 384].astype(F32) - mean for b in range(16)]
    var = sum(jnp.sum(v * v, axis=1, keepdims=True) for v in centered) * (1.0 / width)
    inv = lax.rsqrt(var + NORM_EPSILON)
    inv_ref[...] = jnp.broadcast_to(inv, inv_ref.shape)
    for b in range(16):
        v = (in_ref[:, 384 * b:384 * b + 384].astype(F32) - mean) * inv
        std[b // 2, b % 2] = v
        nrm[b // 4, b % 4] = (v * gain_ref[:, 384 * b:384 * b + 384]).astype(BF16)
    std_ref[...] = std[z]
    ex = [exchange_stream(nrm, exmid, exout, s, ssem, rsem, EX + 7 * s, sent) for s in (0, 1)]
    for g in ex:
        next(g)

    wait_recv(got, rsem.at[OTHER], dp=sib)
    mine = r_ref[:, pl.ds(pl.multiple_of(256 * core, 128), 256)]
    theirs = got[...]
    rall[pl.ds(pl.multiple_of(chip * 168, 8), 168), pl.ds(pl.multiple_of(256 * core, 128), 256)] = jnp.concatenate(
        [jnp.where(core == 0, mine, theirs), jnp.where(core == 0, theirs, mine)], axis=0
    )
    r_streams = [gather_stream(loc_r(s), "xy"[s], ssem, rsem, s * GATHER_SLOTS, sent) for s in (0, 1)]

    def run(gens):
        live = []
        for g in gens:
            try:
                next(g)
                live.append(g)
            except StopIteration:
                pass
        return live

    def mine192(v):
        return jnp.where(core == 0, v[:, 0:192].astype(F32), v[:, 192:384].astype(F32))

    def after_exchange():
        sent.append(send(exout, exsib, ssem.at[OTHER + 1], rsem.at[OTHER + 1], dp=sib))
        for q in range(4):
            v = exout[q].reshape(4 * tokens, 384)
            xt[core, :, 128 * q:128 * q + 128] = mine192(v).T.astype(BF16)
        yield
        wait_recv(exsib, rsem.at[OTHER + 1], dp=sib)
        for q in range(4):
            v = exsib[q].reshape(4 * tokens, 384)
            xt[1 - core, :, 128 * q:128 * q + 128] = mine192(v).T.astype(BF16)
        yield

    def compute():
        for copy in fetch:
            copy.wait()
        for t in range(0, cols, 384):
            acc = m_ref[:, t:t + 384]
            for c in (0, 1):
                acc = acc + jnp.dot(xt[c], gall[c, :, t:t + 384], preferred_element_type=F32)
            buf_ref[:, t:t + 384] = acc
            top, low = split(acc)
            both[0:rows, t:t + 384] = top
            both[rows:2 * rows, t:t + 384] = low
            yield
        store.start()

    bk[:, :, 128:256] = jnp.zeros((2, 512, 128), F32)
    tail = after_exchange()
    work = compute()
    r_live, g_live, x_live = r_streams, g_streams, ex
    r_live = run(r_live)
    tail_live = [tail]
    r_turns = 7
    while g_live or x_live or tail_live:
        g_live = run(g_live)
        if x_live:
            x_live = run(x_live)
        elif tail_live:
            tail_live = run(tail_live)
        if r_turns:
            r_turns -= 1
            r_live = run(r_live)
    work_live = [work]
    while r_live or work_live:
        r_live = run(r_live)
        work_live = run(work_live)

    order = (3, 4, 2, 5, 1, 6, 0)

    def rows24(q):
        return pl.ds(pl.multiple_of(24 * (q % 8), 8), 24)

    halves = [slice(0, 256), slice(256, 512)]
    for h, hc in enumerate(halves):
        acc = jnp.zeros((rows, 256), F32)
        for t in range(0, cols, 384):
            r_top, r_low = split(rall[t:t + 384, hc])
            one = jnp.dot(both[:, t:t + 384], r_top, preferred_element_type=F32)
            two = jnp.dot(both[0:rows, t:t + 384], r_low, preferred_element_type=F32)
            acc = acc + (one[0:rows] + (one[rows:] + two))
        part[:, hc] = acc
        for i in order:
            sent.append(send(
                part.at[rows24(zs[i]), hc], zbuf.at[i, :, hc], ssem.at[ZP + 7 * h + i], rsem.at[ZP + 7 * h + i],
                tensor=zs[i],
            ))
    for c in (0, 1):
        for q in (0, 256):
            bk[c, q:q + 256, 0:192] = lax.dot_general(
                gall[c, q:q + 256, :], w_ref[...], (((1,), (1,)), ((), ())), preferred_element_type=F32
            )
    sent.append(send(bk.at[1 - core], bksib, ssem.at[OTHER + 3], rsem.at[OTHER + 3], dp=sib))
    for t in range(0, cols, 384):
        bt_ref[t:t + 384, :] = both[:, t:t + 384].astype(F32).T.astype(BF16)
    wait_recv(bksib, rsem.at[OTHER + 3], dp=sib)
    for q in range(4):
        ours = bk[core, 128 * q:128 * q + 128, 0:192]
        their = bksib[128 * q:128 * q + 128, 0:192]
        bsrc[q] = jnp.concatenate(
            [jnp.where(core == 0, ours, their), jnp.where(core == 0, their, ours)], axis=1
        ).reshape(4, tokens, 384)
    sent.append(send(bt_ref, btsib_ref, ssem.at[OTHER + 2], rsem.at[OTHER + 2], dp=sib))
    back = [exchange_stream(bsrc, bmid, backall_ref, s, ssem, rsem, EX + 14 + 7 * s, sent) for s in (0, 1)]
    back = run(back)

    def planes(h):
        hc = halves[h]
        quarters = (slice(256 * h, 256 * h + 128), slice(256 * h + 128, 256 * h + 256))

        def pass_on(source, to, slot, cut=hc):
            ref = p_ref.at[rows24(source), cut]
            sent.append(send(ref, ref, ssem.at[ZA + 8 * h + slot], rsem.at[ZA + 8 * h + slot], tensor=(to + 8) % 8))

        def arrived(source, slot, cut=hc):
            wait_recv(p_ref.at[rows24(source + 8), cut], rsem.at[ZA + 8 * h + slot], tensor=(z + 1) % 8)

        total = part[rows24(z), hc]
        for i in reversed(order):
            wait_recv(zbuf.at[i, :, hc], rsem.at[ZP + 7 * h + i], tensor=zs[i])
            total = total + zbuf[i, :, hc]
        p_ref[rows24(z), hc] = total
        pass_on(z, z + 2, 2)
        pass_on(z, z - 2, 3)
        pass_on(z, z + 1, 0)
        pass_on(z, z - 1, 1)
        yield
        arrived(z - 2, 2)
        pass_on(z + 6, z + 2, 6, quarters[0])
        pass_on(z + 6, z + 1, 4)
        arrived(z + 2, 3)
        pass_on(z + 2, z - 2, 7, quarters[1])
        pass_on(z + 2, z - 1, 5)
        yield
        arrived(z - 1, 0)
        arrived(z + 1, 1)
        arrived(z - 3, 4)
        arrived(z + 3, 5)
        arrived(z - 4, 6, quarters[0])
        arrived(z - 4, 7, quarters[1])
        yield

    gathers = [planes(0), planes(1)]
    gathers = run(gathers)
    gathers = run(gathers)
    back = run(back)
    gathers = run(gathers)
    gbuf[...] = lax.dot_general(
        p_ref[:, pl.ds(pl.multiple_of(128 * (z // 2), 128), 128)], p_ref[...],
        (((0,), (0,)), ((), ())), precision=HI, preferred_element_type=F32,
    )
    half = 64 * (z % 2)
    away = gbuf.at[pl.ds(pl.multiple_of(half + 32 * (1 - core), 32), 32)]
    sent.append(send(away, cbuf, ssem.at[ZP + 14], rsem.at[ZP + 14], dp=sib))
    wait_recv(cbuf, rsem.at[ZP + 14], dp=sib)
    cbuf[...] += gbuf[pl.ds(pl.multiple_of(half + 32 * core, 32), 32), :]
    for i in range(3):
        sent.append(send(
            cbuf.at[pl.ds(pl.multiple_of(8 * xs[i], 8), 8)], xbuf.at[i], ssem.at[ZP + 15 + i], rsem.at[ZP + 15 + i],
            dp=dp_of(xs[i], y, core),
        ))
    total = cbuf[pl.ds(pl.multiple_of(8 * x, 8), 8), :]
    for i in range(3):
        wait_recv(xbuf.at[i], rsem.at[ZP + 15 + i], dp=sib)
        total = total + xbuf[i]
    ybuf[y] = total
    for i in range(3):
        sent.append(send(
            ybuf.at[y], ybuf.at[y], ssem.at[ZP + 18 + i], rsem.at[ZP + 18 + i], dp=dp_of(x, ys[i], core)
        ))
    for i in range(3):
        wait_recv(ybuf.at[(y + 3 - i) % 4], rsem.at[ZP + 18 + i], dp=sib)
    gram_ref[z, core, x] = (ybuf[0] + ybuf[1]) + (ybuf[2] + ybuf[3])
    mine = gram_ref.at[z, core, x]
    for i in order:
        sent.append(send(mine, mine, ssem.at[ZP + 21 + i], rsem.at[ZP + 21 + i], tensor=zs[i]))
    back = run(back)
    for i in reversed(order):
        wait_recv(gram_ref.at[(z + 7 - i) % 8, core, x], rsem.at[ZP + 21 + i], tensor=zs[i])
    cuts = (slice(0, 2), slice(2, 8))

    def along(j, i):
        mine = gram_ref.at[cuts[j], core, x]
        slot = GP + 7 * j + i
        return copy_to(mine, mine, ssem.at[slot], rsem.at[slot], dp=dp_of(xs[i], y, core))

    def across(j, i):
        there = gram_ref.at[cuts[j], core, x if i == 3 else (x + 3 - i) % 4]
        slot = GP + 7 * j + 3 + i
        return copy_to(there, there, ssem.at[slot], rsem.at[slot], dp=sib)

    def pass_rows(j):
        for i in range(3):
            wait_recv(gram_ref.at[cuts[j], core, (x + 3 - i) % 4], rsem.at[GP + 7 * j + i], dp=sib)
            across(j, i).start()

    def end_rows(j):
        for i in range(4):
            there = gram_ref.at[cuts[j], 1 - core, x if i == 3 else (x + 3 - i) % 4]
            wait_recv(there, rsem.at[GP + 7 * j + 3 + i], dp=sib)
            across(j, i).wait_send()

    for j in (0, 1):
        for i in range(3):
            copy = along(j, i)
            copy.start()
            sent.append(copy)
        across(j, 3).start()
    return pass_rows, end_rows


def chol_steps(pass_rows, end_rows, g_ref, p_ref, o_ref, s_ref, w_ref):
    n_p = p_ref.shape[0]
    s_ref[:, 512:512 + n_p] = p_ref[...].T
    s_ref[:, 512 + n_p:] = jnp.zeros((512, s_ref.shape[1] - 512 - n_p), F32)
    pass_rows(0)
    end_rows(0)
    s_ref[0:128, 0:512] = g_ref[0:2].reshape(128, 512)
    lane = lax.broadcasted_iota(jnp.int32, (8, 128), 1)
    sub = lax.broadcasted_iota(jnp.int32, (8, 128), 0)

    def lane_splat(v, j):
        return jnp.broadcast_to(v[:, j:j + 1], (8, 128))

    def row_splat(v, i):
        return jnp.broadcast_to(v[i:i + 1, :], (8, 128))

    for kb in range(4):
        base = 128 * kb
        rest = s_ref[base:base + 128, base:base + 128]
        for k in range(16):
            if kb == 0 and k == 12:
                pass_rows(1)
            x = rest[0:8]
            below = rest[8:]
            inside = (lane >= 8 * k) & (lane < 8 * k + 8)
            c = [lane_splat(x, 8 * k + q) for q in range(8)]
            x = jnp.where(inside, (lane - 8 * k == sub).astype(F32), x)
            inv, up, rows = [], [], []
            scale = jnp.ones((8, 128), F32)
            for p in range(8):
                pd = row_splat(c[p], p)
                ip = 1.0 / pd
                scale = jnp.where(sub == p, lax.rsqrt(pd), scale)
                m = jnp.where(sub > p, c[p] * ip, 0.0)
                u = {}
                for q in range(p + 1, 8):
                    u[q] = c[q][p:p + 1]
                    c[q] = c[q] - (c[p] * row_splat(c[q], p)) * ip
                r = x[p:p + 1]
                x = x - m * r
                inv.append(ip[0:1])
                up.append(u)
                rows.append(r)
            w_ref[8 * k:8 * k + 8, :] = jnp.where(lane <= sub + 8 * k, x * scale, 0.0)
            if k < 15:
                n = below.shape[0]
                e = [jnp.broadcast_to(below[:, 8 * k + q:8 * k + q + 1], (n, 128)) for q in range(8)]
                below = jnp.where(inside[0:1], 0.0, below)
                for p in range(8):
                    m = e[p] * inv[p]
                    for q in range(p + 1, 8):
                        e[q] = e[q] - m * up[p][q]
                    below = below - m * rows[p]
                rest = below
        if kb == 0:
            end_rows(1)
            s_ref[128:512, 0:512] = g_ref[2:8].reshape(384, 512)
        s_ref[base:base + 128, base + 128:] = jnp.dot(
            w_ref[...], s_ref[base:base + 128, base + 128:], precision=HI, preferred_element_type=F32
        )
        if kb < 3:
            s_ref[base + 128:, base + 128:] -= lax.dot_general(
                s_ref[base:base + 128, base + 128:512], s_ref[base:base + 128, base + 128:],
                (((0,), (0,)), ((), ())), precision=HI, preferred_element_type=F32,
            )
    o_ref[...] = s_ref[:, 512:512 + n_p].T


SPLIT = ((0, 96), (96, 80), (0, 176))


def coeff_steps(sent, call_out, csem, bt_ref, btsib_ref, o_ref, back_ref, std_ref, gain_ref, inv_ref,
                call_ref, cown_ref, csq_ref, ig_ref, gg_ref,
                osib, rhs, c_ref, sbuf, rbuf, acc, s2, r2, fin, fsib, agb,
                xsq, ysq, zsq, sqs, ngbuf, stat, gx, gy, gc, ssem, rsem, gs, gr, ns, nr):
    x, y, core, z = place()
    sib = dp_of(x, y, 1 - core)
    xs = [(x + d) % 4 for d in (1, 2, 3)]
    ys = [(y + d) % 4 for d in (1, 2, 3)]
    zs = [(z + d) % 8 for d in range(1, 8)]
    first = ("x", "y")

    def half(who):
        return pl.ds(pl.multiple_of(256 * who, 128), 256)

    sent.append(send(o_ref.at[:, half(1 - core)], osib, ssem.at[0], rsem.at[0], dp=sib))

    def input_grad():
        total = back_ref[z // 2, pl.ds(2 * (z % 2), 2)]
        for i in range(7):
            wait_recv(ngbuf.at[i], nr.at[i], tensor=zs[i])
            total = total + ngbuf[i]
        std = std_ref[...]
        gain = gain_ref[:, pl.ds(pl.multiple_of(768 * z, 128), 768)]
        scaled = total * jnp.stack([gain[:, 0:384], gain[:, 384:768]])
        lane = lax.broadcasted_iota(jnp.int32, (32, 128), 1)

        def per_token(v):
            return jnp.sum(jnp.sum(v, axis=0), axis=1, keepdims=True)

        stat[z] = jnp.where(lane < 64, per_token(scaled), per_token(scaled * std))
        for i in range(7):
            sent.append(send(stat.at[z], stat.at[z], ns.at[7 + i], nr.at[7 + i], tensor=zs[i]))
        gx[x] = jnp.broadcast_to(jnp.sum(total * std, axis=1, keepdims=True), gx.shape[1:])
        for i in range(3):
            sent.append(send(gx.at[x], gx.at[x], ns.at[14 + i], nr.at[14 + i], dp=dp_of(xs[i], y, core)))
        yield
        for i in range(3):
            wait_recv(gx.at[(x + 3 - i) % 4], nr.at[14 + i], dp=sib)
        gy[y] = (gx[0] + gx[1]) + (gx[2] + gx[3])
        for i in range(3):
            sent.append(send(gy.at[y], gy.at[y], ns.at[17 + i], nr.at[17 + i], dp=dp_of(x, ys[i], core)))
        for i in range(7):
            wait_recv(stat.at[(z + 7 - i) % 8], nr.at[7 + i], tensor=zs[i])
        sums = stat[0]
        for i in range(1, 8):
            sums = sums + stat[i]
        sums = sums * (1.0 / (16 * 384))
        full = inv_ref[...] * (scaled - sums[:, 0:1] - std * sums[:, 64:65])
        ig_ref[:, 0:384] = full[0].astype(BF16)
        ig_ref[:, 384:768] = full[1].astype(BF16)
        yield
        for i in range(3):
            wait_recv(gy.at[(y + 3 - i) % 4], nr.at[17 + i], dp=sib)
        gc[core] = (gy[0] + gy[1]) + (gy[2] + gy[3])
        sent.append(send(gc.at[core], gc.at[core], ns.at[20], nr.at[20], dp=sib))
        yield
        wait_recv(gc.at[1 - core], nr.at[20], dp=sib)
        gg_ref[:, 0:384] = gc[0, 0] + gc[1, 0]
        gg_ref[:, 384:768] = gc[0, 1] + gc[1, 1]
        yield

    tokens_side = input_grad()

    def begin_tokens():
        for _ in range(2):
            yield
        next(tokens_side)
        yield

    def fill(v):
        top, low = split(v)
        n = v.shape[0]
        rhs[0:n, 0:256] = top
        rhs[n:2 * n, 0:256] = top
        rhs[0:n, 256:512] = low
        rhs[n:2 * n, 256:512] = low

    cols = bt_ref.shape[0]
    fill(o_ref[:, half(core)])
    for t in range(0, cols, 384):
        two = jnp.dot(bt_ref[t:t + 384, :], rhs[...], preferred_element_type=F32)
        c_ref[t:t + 384, :] = two[:, 0:256] + two[:, 256:512]
    wait_recv(osib, rsem.at[0], dp=sib)
    fill(osib[...])
    for t in range(0, cols, 384):
        two = jnp.dot(btsib_ref[t:t + 384, :], rhs[...], preferred_element_type=F32)
        c_ref[t:t + 384, :] += two[:, 0:256] + two[:, 256:512]

    def cols_of(who, s):
        return pl.ds(pl.multiple_of(256 * who + 128 * s, 128), 128)

    a0 = (x, y)
    b0 = (y, x)

    def own(s, off, b):
        a = (a0[s] + off) % 4
        bx, by = (a, b) if s == 0 else (b, a)
        return c_ref[pl.ds(pl.multiple_of(168 * (bx * 4 + by), 8), 168), 128 * s:128 * s + 128]

    def dev(s, a, b):
        a, b = a % 4, b % 4
        return dp_of(a, b, core) if s == 0 else dp_of(b, a, core)

    zero_pad = jnp.zeros((8, 128), F32)

    def padded(v):
        return jnp.concatenate([v, zero_pad], axis=0).astype(BF16)

    def reduce_direct(s):
        base = 8 + 6 * s
        a, b = a0[s], b0[s]
        offs = (2, 1, 3)
        for i in range(3):
            for j in range(4):
                sbuf[s, i, j] = padded(own(s, offs[i], j))
            sent.append(send(
                sbuf.at[s, i], rbuf.at[s, i], ssem.at[base + i], rsem.at[base + i], dp=dev(s, a + offs[i], b)
            ))
            yield
        for j in range(4):
            acc[s, j] = own(s, 0, j)
        for i in (1, 2, 0):
            wait_recv(rbuf.at[s, i], rsem.at[base + i], dp=sib)
        yield

        def summed(off):
            j = (b + off) % 4
            return (acc[s, j] + rbuf[s, 0, j, 0:168].astype(F32)) + (
                rbuf[s, 1, j, 0:168].astype(F32) + rbuf[s, 2, j, 0:168].astype(F32)
            )

        for i in range(3):
            s2[s, i] = padded(summed(offs[i]))
            sent.append(send(
                s2.at[s, i], r2.at[s, i], ssem.at[base + 3 + i], rsem.at[base + 3 + i], dp=dev(s, a, b + offs[i])
            ))
        yield
        total = summed(0)
        for i in (1, 2, 0):
            wait_recv(r2.at[s, i], rsem.at[base + 3 + i], dp=sib)
            total = total + r2[s, i, 0:168].astype(F32)
        fin[:, 128 * s:128 * s + 128] = total
        agb[x * 4 + y, :, cols_of(core, s)] = padded(total)
        yield

    round_robin([reduce_direct(0), reduce_direct(1), begin_tokens()])

    def norms():
        v = fin[...]
        xsq[x] = jnp.broadcast_to(jnp.sum(v * v, axis=0, keepdims=True), (8, 256))
        for i in range(3):
            sent.append(send(xsq.at[x], xsq.at[x], ssem.at[25 + i], rsem.at[25 + i], dp=dp_of(xs[i], y, core)))
        sent.append(send(fin, fsib, ssem.at[24], rsem.at[24], dp=sib))
        yield
        yield
        for i in range(3):
            wait_recv(xsq.at[(x + 3 - i) % 4], rsem.at[25 + i], dp=sib)
        ysq[y] = (xsq[0] + xsq[1]) + (xsq[2] + xsq[3])
        for i in range(3):
            sent.append(send(ysq.at[y], ysq.at[y], ssem.at[28 + i], rsem.at[28 + i], dp=dp_of(x, ys[i], core)))
        yield
        yield
        for i in range(3):
            wait_recv(ysq.at[(y + 3 - i) % 4], rsem.at[28 + i], dp=sib)
        zsq[z] = (ysq[0] + ysq[1]) + (ysq[2] + ysq[3])
        for i in range(7):
            sent.append(send(zsq.at[z], zsq.at[z], ssem.at[31 + i], rsem.at[31 + i], tensor=zs[i]))
        yield
        yield
        for i in range(7):
            wait_recv(zsq.at[(z + 7 - i) % 8], rsem.at[31 + i], tensor=zs[i])
        total = zsq[0]
        for i in range(1, 8):
            total = total + zsq[i]
        sqs[core] = total
        sent.append(send(sqs.at[core], sqs.at[core], ssem.at[38], rsem.at[38], dp=sib))
        yield
        wait_recv(fsib, rsem.at[24], dp=sib)
        left = jnp.where(core == 0, fin[0:84], fsib[84:168])
        right = jnp.where(core == 0, fsib[0:84], fin[84:168])
        cown_ref[:, 0:256] = left
        cown_ref[:, 256:512] = right
        yield
        wait_recv(sqs.at[1 - core], rsem.at[38], dp=sib)
        csq_ref[:, 0:256] = sqs[0]
        csq_ref[:, 256:512] = sqs[1]
        yield

    def loc(s):
        def at(who, bx, by, part):
            lo, rows = SPLIT[part]
            return agb.at[bx * 4 + by, pl.ds(lo, rows), cols_of(who, s)]
        return at

    round_robin([
        gather_stream(loc(0), first[0], gs, gr, 0, sent),
        gather_stream(loc(1), first[1], gs, gr, GATHER_SLOTS, sent),
        norms(),
        tokens_side,
    ])
    outs = []
    for j in range(8):
        two = jnp.concatenate([agb[2 * j, 0:168].astype(F32), agb[2 * j + 1, 0:168].astype(F32)], axis=0)
        call_ref[336 * j:336 * j + 336, :] = two.astype(BF16)
        out = pltpu.make_async_copy(
            call_ref.at[336 * j:336 * j + 336], call_out.at[336 * j:336 * j + 336], csem.at[j]
        )
        out.start()
        outs.append(out)
    for out in outs:
        out.wait()


def whole_kernel(*refs):
    ins, refs = list(refs[:6]), refs[6:]
    buf_out, ortho, call_out, cown, csq, ig, gg = refs[:7]
    buf, weight, moment, local, call, csem = refs[7:13]
    refs = refs[13:]
    fetch = [
        pltpu.make_async_copy(ins[3], weight, local.at[0]),
        pltpu.make_async_copy(ins[4], moment, local.at[1]),
    ]
    for copy in fetch:
        copy.start()
    ins[3], ins[4] = weight, moment
    store = pltpu.make_async_copy(buf, buf_out, local.at[2])
    front_scratch, refs = refs[:29], refs[29:]
    s_scr, w_scr, refs = refs[0], refs[1], refs[2:]
    p, gram, bt, btsib, backall, stdz, inv = front_scratch[:7]
    x, y, core, z = place()
    greet([{"tensor": (z + d) % 8} for d in range(1, 8)] + plane_peers(x, y, core))
    sent = []
    pass_rows, end_rows = front_steps(sent, fetch, store, *ins, p, gram, bt, btsib, buf, backall, stdz, inv, *front_scratch[7:])
    ngbuf, ns, nr = refs[15], refs[-2], refs[-1]
    for i in (3, 4, 2, 5, 1, 6, 0):
        to = (z + 1 + i) % 8
        sent.append(send(backall.at[to // 2, pl.ds(2 * (to % 2), 2)], ngbuf.at[i], ns.at[i], nr.at[i], tensor=to))
    chol_steps(pass_rows, end_rows, gram, p, ortho, s_scr, w_scr)
    wait_recv(btsib, front_scratch[-1].at[OTHER + 2], dp=dp_of(x, y, 1 - core))
    store.wait()
    coeff_steps(sent, call_out, csem, bt, btsib, ortho, backall, stdz, ins[1], inv, call, cown, csq, ig, gg, *refs)
    for copy in sent:
        copy.wait_send()


def whole(inputs, gain, out_grad, weight, moment, right_basis):
    vm = pl.BlockSpec(memory_space=pltpu.VMEM)
    rows, cols = moment.shape
    tokens = inputs.shape[0]
    anywhere = pl.BlockSpec(memory_space=pl.ANY)
    block = (2, tokens, 384)

    def f32(*shape):
        return pltpu.VMEM(shape, F32)

    def bf16(*shape):
        return pltpu.VMEM(shape, BF16)

    dma = pltpu.SemaphoreType.DMA
    front_scratch = [
        f32(rows, RANK),
        f32(8, 2, 4, 8, RANK),
        bf16(cols, 2 * rows),
        bf16(cols, 2 * rows),
        f32(4, 4, tokens, 384),
        f32(*block),
        f32(tokens, 384),
        f32(cols, RANK),
        bf16(2, 16 * tokens, cols),
        f32(right_basis.shape[0], 256),
        f32(8, 2, tokens, 384),
        bf16(4, 4, tokens, 384),
        bf16(2, 4, 4, 16, 384),
        bf16(4, 4, tokens, 384),
        bf16(4, 4, tokens, 384),
        bf16(2, rows, 16 * tokens),
        bf16(2 * rows, cols),
        f32(2, 16 * tokens, 256),
        f32(16 * tokens, 256),
        f32(4, 4, tokens, 384),
        f32(2, 4, 4, 16, 384),
        f32(rows, RANK),
        f32(7, 24, RANK),
        f32(128, RANK),
        f32(32, RANK),
        f32(3, 8, RANK),
        f32(4, 8, RANK),
        dma((GP + 14,)),
        dma((GP + 14,)),
    ]
    chol_scratch = [f32(RANK, 768), f32(128, 128)]
    coeff_scratch = [
        f32(192, 256),
        bf16(384, RANK),
        f32(2688, 256),
        bf16(2, 3, 4, 176, 128),
        bf16(2, 3, 4, 176, 128),
        f32(2, 4, 168, 128),
        bf16(2, 3, 176, 128),
        bf16(2, 3, 176, 128),
        f32(168, 256),
        f32(168, 256),
        bf16(16, 176, RANK),
        f32(4, 8, 256),
        f32(4, 8, 256),
        f32(8, 8, 256),
        f32(2, 8, 256),
        f32(7, *block),
        f32(8, 32, 128),
        f32(4, 2, 8, 384),
        f32(4, 2, 8, 384),
        f32(2, 2, 8, 384),
        dma((39,)),
        dma((39,)),
        dma((2 * GATHER_SLOTS,)),
        dma((2 * GATHER_SLOTS,)),
        dma((21,)),
        dma((21,)),
    ]
    return pl.pallas_call(
        whole_kernel,
        out_shape=(
            jax.ShapeDtypeStruct((rows, cols), F32),
            jax.ShapeDtypeStruct((rows, RANK), F32),
            jax.ShapeDtypeStruct((cols, RANK), BF16),
            jax.ShapeDtypeStruct((84, RANK), F32),
            jax.ShapeDtypeStruct((8, RANK), F32),
            jax.ShapeDtypeStruct((tokens, 768), BF16),
            jax.ShapeDtypeStruct((8, 768), F32),
        ),
        in_specs=[vm, vm, vm, anywhere, anywhere, vm],
        out_specs=(anywhere, vm, anywhere, vm, vm, vm, vm),
        scratch_shapes=[
            f32(rows, cols), bf16(rows, cols), f32(rows, cols), dma((3,)), bf16(cols, RANK), dma((8,)),
        ] + front_scratch + chol_scratch + coeff_scratch,
        compiler_params=pltpu.CompilerParams(
            collective_id=1, has_side_effects=True, vmem_limit_bytes=VMEM_LIMIT
        ),
    )(inputs, gain, out_grad, weight, moment, right_basis)


def final_kernel(group, qkv_scale, mlp_scale, o_ref, csq_ref, c_ref, buf_ref, cown_ref, ig_ref, gg_ref,
                 mom_ref, upd_ref, basis_ref, igo_ref, ggo_ref, lhs):
    rows = o_ref.shape[0]
    step = pl.program_id(0)

    @pl.when(step == 0)
    def _():
        inv = 1.0 / (jnp.sqrt(csq_ref[0:1]) + 1e-08)
        o = o_ref[...]
        lhs[0:rows, :] = o.astype(BF16)
        top, low = split(o * inv)
        lhs[rows:2 * rows, :] = top
        lhs[2 * rows:3 * rows, :] = low
        basis_ref[...] = cown_ref[...] * inv
        igo_ref[...] = ig_ref[...]
        ggo_ref[...] = gg_ref[0]

    out = lax.dot_general(lhs[...], c_ref[...], (((1,), (1,)), ((), ())), preferred_element_type=F32)
    tile = out.shape[1]
    position = lax.broadcasted_iota(jnp.int32, (1, tile), 1) + step * tile
    scale = jnp.where(position < group, qkv_scale, mlp_scale)
    mom_ref[...] = buf_ref[...] - (1.0 - MOMENTUM) * out[0:rows]
    upd_ref[...] = (out[rows:2 * rows] + out[2 * rows:3 * rows]) * scale


def final_products(o, squares, coeffs, buffer, coeff_own, input_grad, gain_grad, *scales):
    rows, cols = buffer.shape
    tile = 896

    def all_of(v):
        return pl.BlockSpec(v.shape, lambda i: (0,) * v.ndim)

    by_col = pl.BlockSpec((rows, tile), lambda i: (0, i))
    gain_out = jax.ShapeDtypeStruct((gain_grad.shape[1],), F32)
    return pl.pallas_call(
        lambda *refs: final_kernel(*scales, *refs),
        grid=(cols // tile,),
        out_shape=(
            jax.ShapeDtypeStruct(buffer.shape, F32),
            jax.ShapeDtypeStruct(buffer.shape, F32),
            jax.ShapeDtypeStruct(coeff_own.shape, F32),
            jax.ShapeDtypeStruct(input_grad.shape, BF16),
            gain_out,
        ),
        in_specs=[
            all_of(o),
            all_of(squares),
            pl.BlockSpec((tile, RANK), lambda i: (i, 0)),
            by_col,
            all_of(coeff_own),
            all_of(input_grad),
            all_of(gain_grad),
        ],
        out_specs=(by_col, by_col, all_of(coeff_own), all_of(input_grad), all_of(gain_out)),
        scratch_shapes=[pltpu.VMEM((3 * rows, RANK), BF16)],
        compiler_params=pltpu.CompilerParams(vmem_limit_bytes=VMEM_LIMIT),
    )(o, squares, coeffs, buffer, coeff_own, input_grad, gain_grad)


def per_device(inputs, norm_gain, out_grad, weight, moment, right_basis):
    tensor_count = lax.axis_size("tensor")
    gain = norm_gain[None, :]
    buffer, ortho, coeffs, coeff_own, squares, input_grad, gain_grad = whole(
        inputs, gain, out_grad, weight, moment, right_basis
    )
    qkv_group = 3 * HEADS * HEAD_DIM // tensor_count
    qkv_scale = 0.2 * math.sqrt(D * (3 * HEADS * HEAD_DIM) / RANK)
    mlp_scale = 0.2 * math.sqrt(D * FF / RANK)
    moment_new, update, basis_new, input_grad, gain_grad = final_products(
        ortho, squares, coeffs, buffer, coeff_own, input_grad, gain_grad, qkv_group, qkv_scale, mlp_scale
    )
    return (input_grad, gain_grad, moment_new, basis_new, update)


def solution(mesh):
    in_specs = (
        P("dp", None),
        P(),
        P("dp", "tensor"),
        P("dp", "tensor"),
        P("dp", "tensor"),
        P(("tensor", "dp"), None),
    )
    out_specs = (
        P("dp", "tensor"),
        P("tensor"),
        P("dp", "tensor"),
        P(("tensor", "dp"), None),
        P("dp", "tensor"),
    )
    return jax.shard_map(
        per_device, mesh=mesh, in_specs=in_specs, out_specs=out_specs, check_vma=False
    )
```
